32 devices in a mesh: dp: 8 (over z, x), mod: 4 (over y, core).
Axes of the slice: x: 2, y: 2, z: 4, core: 2. Of those that a mesh axis runs over, the one named last changes fastest.
Arguments:
- tokens: bfloat16 [64, 256, 1152], P(('dp', 'mod')), may hold values from -6 to 6
- condition: float32 [48, 1152], P('dp'), may hold values from -9 to 9
- counts: int32 [8, 4], P('dp'), may hold values from 1 to 2, as said below
- sample_order: int32 [8, 6], P('dp'), may hold values from 0 to 5, each once within a row
- weight_qkv: bfloat16 [1152, 3456], replicated, may hold values from -0.1875 to 0.1875
- bias_query: float32 [1152], replicated, may hold values from -3 to 3
- bias_value: float32 [1152], replicated, may hold values from -3 to 3
- weight_out: bfloat16 [1152, 1152], replicated, may hold values from -0.75 to 0.75
- bias_out: float32 [1152], replicated, may hold values from -3 to 3
- weight_up: bfloat16 [1152, 4608], replicated, may hold values from -0.1875 to 0.1875
- bias_up: float32 [4608], replicated, may hold values from -3 to 3
- weight_down: bfloat16 [4608, 1152], replicated, may hold values from -0.09375 to 0.09375
- bias_down: float32 [1152], replicated, may hold values from -3 to 3
- weight_ada: bfloat16 [1152, 6912], P(None, 'mod'), may hold values from -0.1875 to 0.1875
- bias_ada: bfloat16 [6912], P('mod'), may hold values from -3 to 3
- cotangent: bfloat16 [64, 256, 1152], P(('dp', 'mod')), may hold values from -6 to 6
Outputs:
- mixed_out: bfloat16 [64, 256, 1152], P(('dp', 'mod'))
- grad_tokens: bfloat16 [64, 256, 1152], P(('dp', 'mod'))
- grad_condition: float32 [48, 1152], P('dp')
- grad_weight_qkv: float32 [1152, 3456], P('dp', 'mod')
- grad_bias_query: float32 [1152], P('dp')
- grad_bias_value: float32 [1152], P('dp')
- grad_weight_out: float32 [1152, 1152], P('dp', 'mod')
- grad_bias_out: float32 [1152], P('dp')
- grad_weight_up: float32 [1152, 4608], P('dp', 'mod')
- grad_bias_up: float32 [4608], P('dp')
- grad_weight_down: float32 [4608, 1152], P('dp', 'mod')
- grad_bias_down: float32 [1152], P('dp')
- grad_weight_ada: float32 [1152, 6912], P('dp', 'mod')
- grad_bias_ada: float32 [6912], P('mod')
The draws below stay inside these ranges and needn't reach their ends.
Inputs may be any that keep to these rules, and one draw needn't show every extreme that they name: Each row of counts sums to 6, and in every row some device holds exactly 2 samples.
All inputs are finite; a program needn't handle non-finite values.
Results may differ from the reference program's by a relative error of at most 0.024.
The reference program's roundings to bfloat16 on the way count: a program that leaves them out, or rounds other values in their place, can miss the bound.
Values may be sent and summed in bfloat16 or wider, within the bound.
No kernel may reach another device: no remote copies, remote signals or barrier semaphores. Data moves between devices by JAX's collectives and lax.ppermute only.
A program may use at most 192 MiB of HBM per device.

```python
import jax
import jax.numpy as jnp
from jax import lax

D = 1152
HEADS = 16
HEAD = 72
FF = 4608
SEQ = 256
SLOTS = 2
ROW_SAMPLES = 6
SAMPLES = 48
ALL_SLOTS = 64
N_DP = 8
N_MOD = 4


def draw_counts(key, part):
    key = jax.random.fold_in(key, 11)
    removed = SLOTS * N_MOD - ROW_SAMPLES

    def one_row(row_key):
        full_key, spread_key = jax.random.split(row_key)
        full_device = jax.random.randint(full_key, (), 0, N_MOD)
        others = (full_device + 1 + jnp.arange(N_MOD - 1, dtype=jnp.int32)) % N_MOD
        tickets = jnp.repeat(others, SLOTS - 1, total_repeat_length=(N_MOD - 1) * (SLOTS - 1))
        shuffled = jax.random.permutation(spread_key, tickets)
        taken = shuffled[:removed]
        minus = jnp.sum((taken[:, None] == jnp.arange(N_MOD, dtype=jnp.int32)[None, :]).astype(jnp.int32), axis=0)
        return (SLOTS - minus).astype(jnp.int32)
    return jax.vmap(one_row)(jax.random.split(key, N_DP))


def shard_levels(stream_key, extent, shards, least, largest):
    gain, own = 1.0, jax.random.fold_in(stream_key, 6)
    for axis_at, shards_of in shards:
        heights = jnp.exp(jax.random.uniform(jax.random.fold_in(own, axis_at), (shards_of,), jnp.float32, least / len(shards), largest / len(shards)))
        gain = gain * jnp.repeat(heights, extent[axis_at] // shards_of).reshape([-1 if axis == axis_at else 1 for axis in range(len(extent))])
    return gain


def scatter_about(own_key, extent, width, bound, cuts=(), kind=jnp.bfloat16):
    loudness = shard_levels(own_key, extent, cuts, -0.22, 0.18) if cuts else 1.0
    values = jax.random.normal(own_key, extent, jnp.float32) * width * loudness
    return jnp.minimum(jnp.maximum(values, -bound), bound).astype(kind)


def setup_inputs(seed: int = 0) -> dict:
    seeds = jax.random.split(jax.random.key(seed), 17)
    tokens = scatter_about(seeds[0], (ALL_SLOTS, SEQ, D), 1.0, 6.0, ((0, 32),))
    condition = scatter_about(seeds[1], (SAMPLES, D), 1.5, 9.0, ((0, 8),), jnp.float32)
    counts = draw_counts(jax.random.fold_in(seeds[16], 71), 0)
    sample_order = jax.vmap(lambda own: jax.random.permutation(own, ROW_SAMPLES))(jax.random.split(seeds[3], N_DP)).reshape((N_DP, ROW_SAMPLES)).astype(jnp.int32)
    weight_qkv = scatter_about(seeds[4], (D, 3 * D), D ** -0.5, 0.1875)
    bias_query = scatter_about(seeds[5], (D,), 0.5, 3.0, (), jnp.float32)
    bias_value = scatter_about(seeds[6], (D,), 0.5, 3.0, (), jnp.float32)
    weight_out = scatter_about(seeds[7], (D, D), (D // 16) ** -0.5, 0.75)
    bias_out = scatter_about(seeds[8], (D,), 0.5, 3.0, (), jnp.float32)
    weight_up = scatter_about(seeds[9], (D, FF), D ** -0.5, 0.1875)
    bias_up = scatter_about(seeds[10], (FF,), 0.5, 3.0, (), jnp.float32)
    weight_down = scatter_about(seeds[11], (FF, D), FF ** -0.5, 0.09375)
    bias_down = scatter_about(seeds[12], (D,), 0.5, 3.0, (), jnp.float32)
    weight_ada = scatter_about(seeds[13], (D, 6 * D), D ** -0.5, 0.1875, ((1, 4),))
    bias_ada = scatter_about(seeds[14], (6 * D,), 0.5, 3.0, ((0, 4),))
    cotangent = scatter_about(seeds[15], (ALL_SLOTS, SEQ, D), 1.0, 6.0, ((0, 32),))
    return dict(tokens=tokens, condition=condition, counts=counts, sample_order=sample_order, weight_qkv=weight_qkv, bias_query=bias_query, bias_value=bias_value, weight_out=weight_out, bias_out=bias_out, weight_up=weight_up, bias_up=bias_up, weight_down=weight_down, bias_down=bias_down, weight_ada=weight_ada, bias_ada=bias_ada, cotangent=cotangent)


@jax.custom_vjp
def low(v):
    return lax.optimization_barrier(v.astype(jnp.bfloat16)).astype(jnp.float32)

@jax.custom_vjp
def low_back(v):
    return v

def low_keep(v):
    return (low(v), None)

def low_pass(kept, grad):
    return (grad,)

def back_keep(v):
    return (v, None)

def back_low(kept, grad):
    return (low(grad),)
low.defvjp(low_keep, low_pass)
low_back.defvjp(back_keep, back_low)
norm_eps = 1e-06
highest = lax.Precision.HIGHEST

def layer_norm(values_in):
    average = lax.optimization_barrier(jnp.mean(values_in, axis=-1, keepdims=True))
    centred = values_in - average
    variance = lax.optimization_barrier(jnp.mean(centred * centred, axis=-1, keepdims=True))
    return centred * lax.rsqrt(variance + norm_eps)

def slot_samples(counts, sample_order):
    counts_int = counts.astype(jnp.int32)
    starts = (jnp.cumsum(counts_int, axis=1) - counts_int).astype(jnp.int32)
    within = jnp.arange(SLOTS, dtype=jnp.int32)
    position = starts[:, :, None] + within[None, None, :]
    live_slots = within[None, None, :] < counts_int[:, :, None]
    position = jnp.minimum(position, ROW_SAMPLES - 1).astype(jnp.int32)
    local_rows = jnp.take_along_axis(sample_order.astype(jnp.int32), position.reshape(N_DP, N_MOD * SLOTS), axis=1)
    offsets = (jnp.arange(N_DP, dtype=jnp.int32) * ROW_SAMPLES)[:, None]
    return ((local_rows + offsets).reshape(-1).astype(jnp.int32), live_slots.reshape(-1))

def block_forward(inputs_f, modulation, alive_mask, trunk):
    weight_qkv, bias_query, bias_value, weight_out, bias_out, weight_up, bias_up, weight_down, bias_down = trunk
    pieces = [modulation[:, None, column * D:(column + 1) * D] for column in range(6)]
    shift_a, scale_a, gate_a, shift_b, scale_b, gate_b = pieces
    group_size = inputs_f.shape[0]
    entry_a = low(layer_norm(inputs_f) * (1.0 + scale_a) + shift_a)
    bias_qkv = jnp.concatenate([bias_query, jnp.zeros_like(bias_query), bias_value])
    packed = low(low_back(jnp.einsum('bsd,de->bse', entry_a, weight_qkv, precision=highest) + bias_qkv))
    queries = packed[:, :, :D].reshape(group_size, SEQ, HEADS, HEAD)
    keys_all = packed[:, :, D:2 * D].reshape(group_size, SEQ, HEADS, HEAD)
    values_all = packed[:, :, 2 * D:].reshape(group_size, SEQ, HEADS, HEAD)
    scores = low_back(jnp.einsum('bqhd,bkhd->bhqk', queries, keys_all, precision=highest) * HEAD ** (-0.5))
    softmax_w = low(jax.nn.softmax(scores, axis=-1))
    attended = jnp.einsum('bhqk,bkhd->bqhd', softmax_w, values_all, precision=highest)
    attended = low(low_back(attended.reshape(group_size, SEQ, D)))
    projected = low_back(jnp.einsum('bsd,de->bse', attended, weight_out, precision=highest) + bias_out)
    residual = inputs_f + gate_a * projected
    entry_b = low(layer_norm(residual) * (1.0 + scale_b) + shift_b)
    upward = low_back(jnp.einsum('bsd,df->bsf', entry_b, weight_up, precision=highest) + bias_up)
    active = low(jax.nn.gelu(upward, approximate=True))
    downward = low_back(jnp.einsum('bsf,fd->bsd', active, weight_down, precision=highest) + bias_down)
    return alive_mask[:, None, None] * (residual + gate_b * downward)

def reference(tokens, condition, counts, sample_order, weight_qkv, bias_query, bias_value, weight_out, bias_out, weight_up, bias_up, weight_down, bias_down, weight_ada, bias_ada, cotangent):
    sample_of_slot, live_slots = slot_samples(counts, sample_order)
    alive_all = live_slots.astype(jnp.float32)
    float_args = (tokens.astype(jnp.float32), condition.astype(jnp.float32), weight_qkv.astype(jnp.float32), bias_query.astype(jnp.float32), bias_value.astype(jnp.float32), weight_out.astype(jnp.float32), bias_out.astype(jnp.float32), weight_up.astype(jnp.float32), bias_up.astype(jnp.float32), weight_down.astype(jnp.float32), bias_down.astype(jnp.float32), weight_ada.astype(jnp.float32), bias_ada.astype(jnp.float32))

    def forward(inputs_all, condition_f, weight_qkv_f, bias_query_f, bias_value_f, weight_out_f, bias_out_f, weight_up_f, bias_up_f, weight_down_f, bias_down_f, weight_ada_f, bias_ada_f):
        trunk = (weight_qkv_f, bias_query_f, bias_value_f, weight_out_f, bias_out_f, weight_up_f, bias_up_f, weight_down_f, bias_down_f)
        lifted = low(jax.nn.silu(condition_f))
        modulation_all = low_back(jnp.dot(lifted, weight_ada_f, precision=highest, preferred_element_type=jnp.float32) + bias_ada_f)
        per_slot = modulation_all[sample_of_slot]
        group_size = SLOTS * N_MOD
        shaped = inputs_all.reshape(N_DP, group_size, SEQ, D)
        mod_groups = per_slot.reshape(N_DP, group_size, 6 * D)
        alive_groups = alive_all.reshape(N_DP, group_size)

        def scan_step(carry, group):
            return (carry, jax.checkpoint(block_forward)(group[0], group[1], group[2], trunk))
        _, outputs = lax.scan(scan_step, None, (shaped, mod_groups, alive_groups))
        return outputs.reshape(N_DP * group_size, SEQ, D)
    output, pullback = jax.vjp(forward, *float_args)
    grads = pullback(cotangent.astype(jnp.float32))
    return (output.astype(jnp.bfloat16), grads[0].astype(jnp.bfloat16), grads[1], grads[2], grads[3], grads[4], grads[5], grads[6], grads[7], grads[8], grads[9], grads[10], grads[11], grads[12])
```

```python
import functools

import jax
import jax.numpy as jnp
from jax import lax
from jax.experimental import pallas as pl
from jax.experimental.pallas import tpu as pltpu
from jax.sharding import PartitionSpec as P

HEADS = 16
HEAD = 72
LANES = 128
SCALE = HEAD ** (-0.5)
GELU = (2.0 / 3.141592653589793) ** 0.5
COST = 1.0e6


norm_eps = 1e-06
highest = lax.Precision.HIGHEST


def layer_norm(values_in):
    average = jnp.mean(values_in, axis=-1, keepdims=True)
    centred = values_in - average
    variance = jnp.mean(centred * centred, axis=-1, keepdims=True)
    factor = lax.rsqrt(variance + norm_eps)
    return (centred * factor, factor)


def norm_back(grad_normed, normed, factor):
    first_mean = jnp.mean(grad_normed, axis=-1, keepdims=True)
    second_mean = jnp.mean(grad_normed * normed, axis=-1, keepdims=True)
    return factor * (grad_normed - first_mean - normed * second_mean)


def swap(value, axis, bit):
    pairs = [(index, index ^ bit) for index in range(lax.axis_size(axis))]
    return lax.ppermute(value, axis, pairs)


def own_bit(axis, bit):
    return lax.axis_index(axis) // bit % 2


def pick(value, dim, which):
    return lax.dynamic_index_in_dim(value, which, dim, keepdims=False)


def halve(value, dim, axis, bit):
    mine = own_bit(axis, bit)
    got = swap(pick(value, dim, 1 - mine), axis, bit)
    kept = pick(value, dim, mine)
    return (kept.astype(jnp.float32) + got.astype(jnp.float32)).astype(value.dtype)


def bits_below(count):
    return [1 << power for power in range(count.bit_length() - 1)]


class Scatter:
    def __init__(self, value, names, block):
        self.names = list(names)
        self.value = value.reshape((2,) * len(self.names) + tuple(block))

    def step(self, axis, bit):
        at = self.names.index((axis, bit))
        self.value = halve(self.value, at, axis, bit)
        self.names.pop(at)

    def steps(self, todo):
        for axis, bit in todo:
            self.step(axis, bit)
        return self.value


def weight_grad_kernel(left_own, left_got, right_own, right_got, out_ref):
    total = jnp.dot(left_own[...], right_own[...], preferred_element_type=jnp.float32)
    total += jnp.dot(left_got[...], right_got[...], preferred_element_type=jnp.float32)
    out_ref[...] = total.astype(out_ref.dtype).reshape(out_ref.shape)


def weight_grad(left_own, left_got, right_own, right_got, tile, out_shape, out_block, out_index):
    rows, depth = left_own.shape
    steps = right_own.shape[1] // tile
    left_spec = pl.BlockSpec((rows, depth), lambda step: (0, 0))
    right_spec = pl.BlockSpec((depth, tile), lambda step: (0, step))
    return pl.pallas_call(
        weight_grad_kernel,
        grid=(steps,),
        in_specs=[left_spec, left_spec, right_spec, right_spec],
        out_specs=pl.BlockSpec(out_block, out_index),
        out_shape=jax.ShapeDtypeStruct(out_shape, jnp.bfloat16),
        compiler_params=pltpu.CompilerParams(vmem_limit_bytes=48 * 1024 * 1024),
        cost_estimate=pl.CostEstimate(
            flops=4 * rows * depth * tile * steps,
            bytes_accessed=4 * rows * depth + 4 * depth * tile * steps + 2 * rows * tile * steps,
            transcendentals=0,
        ),
    )(left_own, left_got, right_own, right_got)


def shards(
    tokens,
    condition,
    counts,
    sample_order,
    weight_qkv,
    bias_query,
    bias_value,
    weight_out,
    bias_out,
    weight_up,
    bias_up,
    weight_down,
    bias_down,
    weight_ada,
    bias_ada,
    cotangent,
):
    slot_count, seq_len, model_width = tokens.shape
    mod_count = lax.axis_size("mod")
    mod_index = lax.axis_index("mod")
    dp_count = lax.axis_size("dp")
    half_mod = mod_count // 2
    core = own_bit("mod", 1)
    row_counts = counts[0]
    row_total = sample_order.shape[1]
    starts = jnp.cumsum(row_counts) - row_counts
    device_ids = jnp.arange(mod_count, dtype=jnp.int32)
    own_count = jnp.sum(jnp.where(device_ids == mod_index, row_counts, 0))
    first_slot = jnp.sum(jnp.where(device_ids == mod_index, starts, 0))
    within = jnp.arange(slot_count, dtype=jnp.int32)
    alive_mask = (within < own_count).astype(jnp.float32)
    position = jnp.minimum(first_slot + within, row_total - 1)
    local_rows = jnp.take(sample_order[0], position)
    picker = (local_rows[:, None] == jnp.arange(row_total, dtype=jnp.int32)[None, :]).astype(
        jnp.float32
    )
    lifted = jax.nn.silu(condition).astype(jnp.bfloat16)
    lifted_all = lax.all_gather(lifted, "dp", axis=0, tiled=True)
    part_mods = jnp.dot(lifted, weight_ada, preferred_element_type=jnp.float32) + bias_ada.astype(
        jnp.float32
    )
    modulation = jnp.dot(
        picker, lax.all_gather(part_mods, "mod", axis=1, tiled=True), precision=highest
    )
    pieces = [
        modulation[:, None, column * model_width : (column + 1) * model_width]
        for column in range(6)
    ]
    shift_a, scale_a, gate_a, shift_b, scale_b, gate_b = pieces
    inputs_f = tokens.astype(jnp.float32)
    normed_a, factor_a = layer_norm(inputs_f)
    entry_a = (normed_a * (1.0 + scale_a) + shift_a).astype(jnp.bfloat16)
    bias_qkv = jnp.concatenate([bias_query, jnp.zeros_like(bias_query), bias_value])
    packed = (
        jnp.einsum("bsd,de->bse", entry_a, weight_qkv, preferred_element_type=jnp.float32)
        + bias_qkv
    ).astype(jnp.bfloat16)
    queries = packed[:, :, :model_width].reshape(slot_count, seq_len, HEADS, HEAD)
    keys_all = packed[:, :, model_width : 2 * model_width].reshape(slot_count, seq_len, HEADS, HEAD)
    values_all = packed[:, :, 2 * model_width :].reshape(slot_count, seq_len, HEADS, HEAD)
    score_scale = HEAD ** (-0.5)
    scores = (
        jnp.einsum("bqhd,bkhd->bhqk", queries, keys_all, preferred_element_type=jnp.float32)
        * score_scale
    )
    log_total = jax.nn.logsumexp(scores, axis=-1, keepdims=True)
    softmax_w = jnp.exp(scores - log_total).astype(jnp.bfloat16)
    attended = jnp.einsum(
        "bhqk,bkhd->bqhd", softmax_w, values_all, preferred_element_type=jnp.float32
    )
    attended = attended.reshape(slot_count, seq_len, model_width).astype(jnp.bfloat16)
    projected = (
        jnp.einsum("bsd,de->bse", attended, weight_out, preferred_element_type=jnp.float32)
        + bias_out
    )
    residual = inputs_f + gate_a * projected
    normed_b, factor_b = layer_norm(residual)
    entry_b = (normed_b * (1.0 + scale_b) + shift_b).astype(jnp.bfloat16)
    upward = (
        jnp.einsum("bsd,df->bsf", entry_b, weight_up, preferred_element_type=jnp.float32) + bias_up
    )
    active_low = jax.nn.gelu(upward, approximate=True).astype(jnp.bfloat16)
    downward = (
        jnp.einsum("bsf,fd->bsd", active_low, weight_down, preferred_element_type=jnp.float32)
        + bias_down
    )
    mixed_out = (alive_mask[:, None, None] * (residual + gate_b * downward)).astype(jnp.bfloat16)
    grad_out = cotangent.astype(jnp.float32) * alive_mask[:, None, None]
    grad_gate_b = jnp.sum(grad_out * downward, axis=1)
    grad_down = (grad_out * gate_b).astype(jnp.bfloat16)
    grad_bias_down = jnp.sum(grad_down.astype(jnp.float32), axis=(0, 1))
    grad_active = jnp.einsum(
        "bsd,fd->bsf", grad_down, weight_down, preferred_element_type=jnp.float32
    )
    _, gelu_back = jax.vjp(lambda inside: jax.nn.gelu(inside, approximate=True), upward)
    grad_upward = gelu_back(grad_active)[0].astype(jnp.bfloat16)
    grad_bias_up = jnp.sum(grad_upward.astype(jnp.float32), axis=(0, 1))
    grad_entry_b = jnp.einsum(
        "bsf,df->bsd", grad_upward, weight_up, preferred_element_type=jnp.float32
    )
    grad_shift_b = jnp.sum(grad_entry_b, axis=1)
    grad_scale_b = jnp.sum(grad_entry_b * normed_b, axis=1)
    grad_resid = grad_out + norm_back(grad_entry_b * (1.0 + scale_b), normed_b, factor_b)
    grad_gate_a = jnp.sum(grad_resid * projected, axis=1)
    grad_proj = (grad_resid * gate_a).astype(jnp.bfloat16)
    grad_bias_out = jnp.sum(grad_proj.astype(jnp.float32), axis=(0, 1))
    grad_attended = jnp.einsum(
        "bse,de->bsd", grad_proj, weight_out, preferred_element_type=jnp.float32
    )
    grad_attended = grad_attended.astype(jnp.bfloat16).reshape(slot_count, seq_len, HEADS, HEAD)
    again_scores = (
        jnp.einsum("bqhd,bkhd->bhqk", queries, keys_all, preferred_element_type=jnp.float32)
        * score_scale
    )
    again_probs = jnp.exp(again_scores - log_total)
    again_low = again_probs.astype(jnp.bfloat16)
    grad_values = jnp.einsum(
        "bhqk,bqhd->bkhd", again_low, grad_attended, preferred_element_type=jnp.float32
    )
    grad_probs = jnp.einsum(
        "bqhd,bkhd->bhqk", grad_attended, values_all, preferred_element_type=jnp.float32
    )
    row_dots = jnp.sum(grad_probs * again_probs, axis=-1, keepdims=True)
    grad_scores = (again_probs * (grad_probs - row_dots)).astype(jnp.bfloat16)
    grad_queries = (
        jnp.einsum("bhqk,bkhd->bqhd", grad_scores, keys_all, preferred_element_type=jnp.float32)
        * score_scale
    )
    grad_keys = (
        jnp.einsum("bhqk,bqhd->bkhd", grad_scores, queries, preferred_element_type=jnp.float32)
        * score_scale
    )
    grad_packed = jnp.concatenate(
        [
            grad_queries.reshape(slot_count, seq_len, model_width),
            grad_keys.reshape(slot_count, seq_len, model_width),
            grad_values.reshape(slot_count, seq_len, model_width),
        ],
        axis=-1,
    ).astype(jnp.bfloat16)
    grad_bias_all = jnp.sum(grad_packed.astype(jnp.float32), axis=(0, 1))
    grad_bias_query = grad_bias_all[:model_width]
    grad_bias_value = grad_bias_all[2 * model_width :]
    grad_entry_a = jnp.einsum(
        "bse,de->bsd", grad_packed, weight_qkv, preferred_element_type=jnp.float32
    )
    grad_shift_a = jnp.sum(grad_entry_a, axis=1)
    grad_scale_a = jnp.sum(grad_entry_a * normed_a, axis=1)
    grad_tokens = (
        grad_resid + norm_back(grad_entry_a * (1.0 + scale_a), normed_a, factor_a)
    ).astype(jnp.bfloat16)
    grad_modulation = jnp.concatenate(
        [grad_shift_a, grad_scale_a, grad_gate_a, grad_shift_b, grad_scale_b, grad_gate_b], axis=1
    )
    tokens_here = slot_count * seq_len
    ff_width = weight_up.shape[1]
    dp_bits = bits_below(dp_count)
    cut = max(dp_count // 4, 2)
    x_steps = [("dp", bit) for bit in dp_bits if bit < cut]
    z_steps = [("dp", bit) for bit in dp_bits if bit >= cut]
    y_steps = [("mod", bit) for bit in bits_below(mod_count) if bit > 1]
    dp_names = [("dp", bit) for bit in reversed(dp_bits)]
    y_names = list(reversed(y_steps))
    row_width = model_width // dp_count

    def columns_of(value, block, pad_to):
        parts = value.reshape(tokens_here, half_mod, 2, block)
        halves = []
        for which in (core, 1 - core):
            part = pick(parts, 2, which)
            part = jnp.pad(part, ((0, 0), (0, 0), (0, pad_to - block)))
            halves.append(part.reshape(tokens_here, half_mod * pad_to))
        return halves

    def weight_by_columns(left, right):
        block = right.shape[-1] // mod_count
        pad_to = -(-block // 128) * 128
        left_t = left.reshape(tokens_here, model_width).T
        mine, others = columns_of(right, block, pad_to)
        result = weight_grad(
            left_t,
            swap(left_t, "mod", 1),
            mine,
            swap(others, "mod", 1),
            pad_to,
            (half_mod, model_width, pad_to),
            (1, model_width, pad_to),
            lambda step: (step, 0, 0),
        )
        return Scatter(result, y_names + dp_names, (row_width, pad_to)), block

    down_t = grad_down.reshape(tokens_here, model_width).T.reshape(
        half_mod, 2, model_width // mod_count, tokens_here
    )
    down_mine = pick(down_t, 1, core).reshape(model_width // 2, tokens_here)
    down_others = pick(down_t, 1, 1 - core).reshape(model_width // 2, tokens_here)
    active_flat = active_low.reshape(tokens_here, ff_width)
    down_block = ff_width // dp_count
    piece = cut * down_block
    pieces_count = dp_count // cut
    down_result = weight_grad(
        down_mine,
        swap(down_others, "mod", 1),
        active_flat,
        swap(active_flat, "mod", 1),
        piece,
        (pieces_count, model_width // 2, piece),
        (1, model_width // 2, piece),
        lambda step: (step, 0, 0),
    )
    down_rows = model_width // mod_count
    z_names = list(reversed(z_steps))
    x_names = list(reversed(x_steps))
    down_done = Scatter(down_result, z_names + y_names, (down_rows, piece)).steps(y_steps + z_steps)
    down_done = down_done.reshape(down_rows, cut, down_block).transpose(1, 0, 2)
    down_done = Scatter(down_done, x_names, (down_rows, down_block)).steps(x_steps)
    grad_weight_down = down_done.astype(jnp.float32).T

    up_scatter, up_block = weight_by_columns(entry_b, grad_upward)
    grad_weight_up = up_scatter.steps(x_steps + z_steps + y_steps)[:, :up_block]
    grad_weight_up = grad_weight_up.astype(jnp.float32)
    out_scatter, out_block = weight_by_columns(attended, grad_proj)
    grad_weight_out = out_scatter.steps(x_steps + y_steps + z_steps)[:, :out_block]
    grad_weight_out = grad_weight_out.astype(jnp.float32)
    qkv_scatter, qkv_block = weight_by_columns(entry_a, grad_packed)
    grad_weight_qkv = qkv_scatter.steps(y_steps + x_steps + z_steps)[:, :qkv_block]
    grad_weight_qkv = grad_weight_qkv.astype(jnp.float32)

    bias_parts = [grad_bias_query, grad_bias_value, grad_bias_out, grad_bias_up, grad_bias_down]
    bias_rows = jnp.concatenate([part.reshape(dp_count, -1) for part in bias_parts], axis=1)
    bias_sum = Scatter(bias_rows, dp_names, bias_rows.shape[1:]).steps(x_steps + z_steps)
    for axis, bit in y_steps + [("mod", 1)]:
        bias_sum = bias_sum + swap(bias_sum, axis, bit)
    bias_done = []
    for part in bias_parts:
        width = part.shape[0] // dp_count
        bias_done.append(bias_sum[:width])
        bias_sum = bias_sum[width:]
    row_grads = jnp.dot(picker.T, grad_modulation, precision=highest)
    row_blocks = row_grads.astype(jnp.bfloat16).reshape(row_total, mod_count, -1).transpose(1, 0, 2)
    part_grads = Scatter(
        row_blocks, y_names + [("mod", 1)], row_blocks.shape[1:]
    ).steps([("mod", 1)] + y_steps)
    rows_all = lax.all_gather(part_grads, "dp", axis=0, tiled=True)
    lifted_own = lax.dynamic_slice_in_dim(
        lifted_all, lax.axis_index("dp") * row_width, row_width, axis=1
    )
    grad_weight_ada = jnp.einsum(
        "rd,rc->dc", lifted_own, rows_all, preferred_element_type=jnp.float32
    )
    grad_bias_ada = jnp.sum(rows_all.astype(jnp.float32), axis=0)
    cond_part = jnp.einsum("rc,dc->rd", part_grads, weight_ada, preferred_element_type=jnp.float32)
    cond_sum = cond_part
    for axis, bit in [("mod", 1)] + y_steps:
        cond_sum = cond_sum + swap(cond_sum, axis, bit)
    _, silu_back = jax.vjp(jax.nn.silu, condition)
    grad_condition = silu_back(cond_sum)[0]
    return (
        mixed_out,
        grad_tokens,
        grad_condition,
        grad_weight_qkv,
        bias_done[0],
        bias_done[1],
        grad_weight_out,
        bias_done[2],
        grad_weight_up,
        bias_done[3],
        grad_weight_down,
        bias_done[4],
        grad_weight_ada,
        grad_bias_ada,
    )


def head_window(head):
    low = HEAD * head
    start = low // LANES * LANES
    stop = -(-(low + HEAD) // LANES) * LANES
    lanes = lax.broadcasted_iota(jnp.int32, (1, stop - start), 1) + start
    return start, stop, (lanes >= low) & (lanes < low + HEAD)


def dot(left, right, left_dim=1, right_dim=0):
    return lax.dot_general(
        left, right, (((left_dim,), (right_dim,)), ((), ())), preferred_element_type=jnp.float32
    )


def whole(shape):
    return pl.BlockSpec(shape, lambda *_: (0,) * len(shape))


def cost(time):
    return pl.CostEstimate(flops=int(time * COST), bytes_accessed=1, transcendentals=0)


def resident(shape):
    return pl.BlockSpec(memory_space=pltpu.VMEM)


def run(body, info, grid, ins, outs, scratch=(), after=(), time=5.0, vmem=63):
    count_in, count_after = len(ins), len(after)

    def kernel(info_ref, *refs):
        body(info_ref, *refs[:count_in], *refs[count_in + count_after :])

    return pl.pallas_call(
        kernel,
        grid_spec=pltpu.PrefetchScalarGridSpec(
            num_scalar_prefetch=1,
            grid=grid,
            in_specs=[spec for _, spec in ins] + [pl.BlockSpec(memory_space=pl.ANY)] * count_after,
            out_specs=[spec for _, _, spec in outs],
            scratch_shapes=list(scratch),
        ),
        out_shape=[jax.ShapeDtypeStruct(shape, dtype) for shape, dtype, _ in outs],
        compiler_params=pltpu.CompilerParams(vmem_limit_bytes=vmem * 1024 * 1024),
        cost_estimate=cost(time),
    )(info, *[value for value, _ in ins], *after)


GROUP = 4
POWER = SCALE * 1.4426950408889634
CORE, ROW_Y, ROW_X, ROW_Z0, ROW_Z1, LIVE, SAMPLE = 0, 1, 2, 3, 4, 5, 7


def start_body(counts, order, condition, weight_t, bias_ada, info, part, lifted):
    mod_index, dp_index = lax.axis_index("mod"), lax.axis_index("dp")
    own_count, first_slot = 0, 0
    for at in range(counts.shape[1]):
        own_count += jnp.where(mod_index == at, counts[0, at], 0)
        first_slot += jnp.where(at < mod_index, counts[0, at], 0)
    info[CORE], info[ROW_Y] = mod_index % 2, mod_index // 2
    info[ROW_X], info[ROW_Z0], info[ROW_Z1] = dp_index % 2, dp_index // 2 % 2, dp_index // 4
    for slot in range(2):
        info[LIVE + slot] = jnp.where(slot < own_count, 1, 0)
        info[SAMPLE + slot] = order[0, jnp.minimum(first_slot + slot, order.shape[1] - 1)]
    rows = condition.shape[0]
    values = condition[...]
    values = (values / (1.0 + jnp.exp(-values))).astype(jnp.bfloat16)
    lifted[...] = jnp.zeros_like(lifted)
    lifted[:rows] = values.astype(jnp.float32)
    part[...] = jnp.zeros_like(part)
    part[:rows] = dot(values, weight_t[...], 1, 1) + bias_ada[...]


def stats_body(info, tokens, query, value, out, up, down, stats, bias_qkv, bias_out, bias_up, bias_down):
    for slot in range(tokens.shape[0]):
        values = tokens[slot].astype(jnp.float32)
        average = jnp.mean(values, axis=-1, keepdims=True)
        centred = values - average
        factor = lax.rsqrt(jnp.mean(centred * centred, axis=-1, keepdims=True) + norm_eps)
        lane = lax.broadcasted_iota(jnp.int32, (1, LANES), 1)
        stats[slot] = jnp.where(lane == 0, average, factor)
    width = query.shape[0]
    bias_qkv[...] = jnp.zeros_like(bias_qkv)
    bias_qkv[0, :width] = query[...]
    bias_qkv[0, 2 * width :] = value[...]
    bias_out[0] = out[...]
    for at in range(4):
        bias_up[at] = up[at * width : (at + 1) * width]
    bias_down[0] = down[...]


def feed(entry, down, up, bias, weight_down):
    inner = dot(entry, up) + bias
    back = dot(down, weight_down, 1, 1)
    square = inner * inner
    bend = jnp.tanh(GELU * (inner + 0.044715 * (square * inner)))
    half = 0.5 * (1.0 + bend)
    slope = half + 0.5 * inner * (1.0 - bend * bend) * (GELU + 3.0 * 0.044715 * GELU * square)
    grad = (back * slope).astype(jnp.bfloat16)
    active = (inner * half).astype(jnp.bfloat16)
    return active, grad, jnp.sum(grad.astype(jnp.float32), axis=0, keepdims=True)


class Copies:
    def __init__(self, semaphores):
        self.semaphores, self.count, self.going = semaphores, 0, []

    def start(self, source, target):
        copy = pltpu.make_async_copy(source, target, self.semaphores.at[self.count])
        self.count += 1
        copy.start()
        return copy

    def leave(self, source, target):
        self.going.append(self.start(source, target))

    def end(self):
        for copy in self.going:
            copy.wait()


def columns_at(ref, block, width):
    return ref.at[:, pl.ds(pl.multiple_of(block * width, LANES), width)]


def rows_at(ref, block, width):
    return ref.at[pl.ds(pl.multiple_of(block * width, LANES), width)]


def hold(*shape):
    return pltpu.VMEM(shape, jnp.bfloat16)


def forward_body(info, *refs):
    tokens, cot, weight_qkv, weight_out, weight_up, weight_down = refs[:6]
    parts, stats, bias_qkv, bias_out, bias_up = refs[6:10], refs[10], *refs[11:14]
    lefts, packed, proj, entry_b, down, mine, others = refs[14:21]
    mods, logs, bias_down, bias_grad = refs[21:25]
    x, g, wq, wo, wu, wd, packed_v, lefts_v, proj_v, entry_v, down_v, mine_v, others_v = refs[25:38]
    value_t, out_t, semaphores = refs[38:]
    slots, seq, width = x.shape
    block = wu.shape[-1]
    copies = Copies(semaphores)
    got_x = [copies.start(tokens.at[slot], x.at[slot]) for slot in range(slots)]
    thirds = [slice(at * width, (at + 1) * width) for at in range(3)]
    got_q = [copies.start(weight_qkv.at[:, third], wq.at[at]) for at, third in enumerate(thirds)]
    got_g = copies.start(cot, g)
    got_o = copies.start(weight_out, wo)
    ahead = []
    for at in range(2):
        spot = 2 * at + 1 - info[CORE]
        ahead.append(copies.start(columns_at(weight_up, spot, block), wu.at[at]))
        ahead.append(copies.start(rows_at(weight_down, spot, block), wd.at[at]))

    own = 2 * info[ROW_Y] + info[CORE]
    columns = parts[0].shape[1]
    for slot in range(slots):
        for far, part in enumerate(parts):
            row = part[pl.ds(info[SAMPLE + slot], 1)]
            for spot in range(4):

                @pl.when(own ^ far == spot)
                def _():
                    low, high = spot * columns, (spot + 1) * columns
                    for piece in range(low // width, -(-high // width)):
                        start, stop = max(low, piece * width), min(high, (piece + 1) * width)
                        mods[slot, piece : piece + 1, start - piece * width : stop - piece * width] = (
                            row[:, start - low : stop - low]
                        )

    for slot in range(slots):
        rows = slice(slot * seq, (slot + 1) * seq)
        got_x[slot].wait()
        normed = (x[slot].astype(jnp.float32) - stats[slot, :, :1]) * stats[slot, :, 1:2]
        value = (normed * (1.0 + mods[slot, 1:2]) + mods[slot, 0:1]).astype(jnp.bfloat16)
        entry_v[rows] = value
        lefts_v[:width, rows] = value.T
    for at, third in enumerate(thirds):
        got_q[at].wait()
        part = dot(entry_v[...], wq[at]) + bias_qkv[:, third]
        packed_v[:, third] = part.astype(jnp.bfloat16)
    copies.leave(packed_v, packed)

    got_g.wait()
    sums = jnp.zeros((1, width), jnp.float32)
    for slot in range(slots):
        rows = slice(slot * seq, (slot + 1) * seq)
        live = info[LIVE + slot].astype(jnp.float32)
        grad = (g[slot].astype(jnp.float32) * live * mods[slot, 5:6]).astype(jnp.bfloat16)
        down_v[rows] = grad
        sums += jnp.sum(grad.astype(jnp.float32), axis=0, keepdims=True)
        turned = grad.T
        part = width // 4
        for at in range(4):
            piece = turned[at * part : (at + 1) * part]
            place = at // 2 * part

            @pl.when(info[CORE] == at % 2)
            def _():
                mine_v[place : place + part, rows] = piece

            @pl.when(info[CORE] != at % 2)
            def _():
                lefts_v[3 * width + place : 3 * width + place + part, rows] = piece

    bias_down[...] = sums
    copies.leave(down_v, down)
    copies.leave(mine_v, mine)

    for slot in range(slots):
        rows = slice(slot * seq, (slot + 1) * seq)
        value_t[...] = packed_v[rows, 2 * width :].T.astype(jnp.float32)
        for first in range(0, HEADS, GROUP):
            heads = range(first, first + GROUP)
            scores = []
            for head in heads:
                start, stop, inside = head_window(head)
                query = jnp.where(inside, packed_v[rows, start:stop], 0)
                scores.append(dot(packed_v[rows, width + start : width + stop], query, 1, 1) * POWER)
            tops = [jnp.max(score, axis=0, keepdims=True) for score in scores]
            powers = [jnp.exp2(score - top) for score, top in zip(scores, tops)]
            totals = [jnp.sum(power, axis=0, keepdims=True) for power in powers]
            for head, top, power, total in zip(heads, tops, powers, totals):
                logs[slot, head : head + 1] = top + jnp.log2(total)
                mine_rows = slice(head * HEAD, (head + 1) * HEAD)
                result = dot(value_t[mine_rows].astype(jnp.bfloat16), power.astype(jnp.bfloat16))
                out_t[mine_rows] = result * (1.0 / total)
        lefts_v[width : 2 * width, rows] = out_t[...].astype(jnp.bfloat16)

    got_o.wait()
    proj_v[...] = dot(lefts_v[width : 2 * width], wo[...], 0, 0) + bias_out[...]
    copies.leave(proj_v, proj)
    for slot in range(slots):
        rows = slice(slot * seq, (slot + 1) * seq)
        residual = x[slot].astype(jnp.float32) + mods[slot, 2:3] * proj_v[rows]
        normed, _ = layer_norm(residual)
        value = (normed * (1.0 + mods[slot, 4:5]) + mods[slot, 3:4]).astype(jnp.bfloat16)
        entry_v[rows] = value
        lefts_v[2 * width : 3 * width, rows] = value.T
    copies.leave(lefts_v, lefts)
    copies.leave(entry_v, entry_b)

    for at in range(2):
        ahead[2 * at].wait()
        ahead[2 * at + 1].wait()
        bias = bias_up[pl.ds(2 * at + 1 - info[CORE], 1)]
        others_v[0, at], others_v[1, at], bias_grad[at] = feed(
            entry_v[...], down_v[...], wu[at], bias, wd[at]
        )
        for kind in range(2):
            copies.leave(others_v.at[kind, at], others.at[kind, at])
    copies.end()


def feed_mine_body(info, *refs):
    entry_b, down, weight_up, weight_down, bias_up, active, grad, bias_grad = refs[:8]
    entry_v, down_v, wu, wd, active_v, grad_v, semaphores = refs[8:]
    block = wu.shape[-1]
    copies = Copies(semaphores)
    ahead = [copies.start(entry_b, entry_v)]
    for at in range(2):
        spot = 2 * at + info[CORE]
        ahead.append(copies.start(columns_at(weight_up, spot, block), wu.at[at]))
        if at == 0:
            ahead.append(copies.start(down, down_v))
        ahead.append(copies.start(rows_at(weight_down, spot, block), wd.at[at]))
    for at in range(2):
        for copy in ahead[:4] if at == 0 else ahead[4:]:
            copy.wait()
        bias = bias_up[pl.ds(2 * at + info[CORE], 1)]
        active_v[at], grad_v[at], bias_grad[at] = feed(
            entry_v[...], down_v[...], wu[at], bias, wd[at]
        )
        copies.leave(active_v.at[at], active.at[at])
        copies.leave(grad_v.at[at], grad.at[at])
    copies.end()


def down_grad_body(info, *refs):
    mine, lefts_got, others, active_mine, others_got, mine_got = refs[:6]
    keep_a, send_a, keep_b, send_b = refs[6:10]
    left, right, keep_a_v, send_a_v, keep_b_v, send_b_v, semaphores = refs[10:]
    depth = mine.shape[1]
    rows = mine.shape[0] // 2
    half = rows // 2
    wide = right.shape[-1] // 2
    base = lefts_got.shape[0] - 2 * rows
    copies = Copies(semaphores)
    ahead = []
    for part in range(2):
        for bit in range(2):
            place = slice((2 * part + bit) * half, (2 * part + bit + 1) * half)
            spot = (info[ROW_Y] ^ bit) * rows + part * half
            for source, start, tokens in ((mine, 0, slice(0, depth)), (lefts_got, base, slice(depth, 2 * depth))):
                own = source.at[pl.ds(pl.multiple_of(start + spot, 16), half)]
                ahead.append(copies.start(own, left.at[place, tokens]))
    blocks = [[], []]
    for chunk in range(2):
        same = (info[ROW_Z0] ^ (1 - chunk)) == info[CORE]
        for bit in range(2):
            at = info[ROW_Z1] ^ bit
            columns = slice(bit * wide, (bit + 1) * wide)
            for kind, (one, two) in enumerate(((active_mine, others), (others_got, mine_got))):
                target = right.at[chunk, kind * depth : (kind + 1) * depth, columns]
                one = one.at[at] if kind == 0 else one.at[0, at]
                two = two.at[0, at] if kind == 0 else two.at[at]
                copy = pltpu.make_async_copy(one, target, semaphores.at[copies.count])
                also = pltpu.make_async_copy(two, target, semaphores.at[copies.count])
                copies.count += 1
                pl.when(same)(copy.start)
                pl.when(jnp.logical_not(same))(also.start)
                blocks[chunk].append(copy)
    for copy in ahead:
        copy.wait()
    for chunk in range(2):
        for copy in blocks[chunk]:
            copy.wait()
        total = dot(left[...], right[chunk]).astype(jnp.bfloat16)
        for bit in range(2):
            columns = slice(bit * wide, (bit + 1) * wide)
            place = 2 * (1 - chunk) + bit
            keep_a_v[place] = total[:half, columns]
            send_a_v[place] = total[half : 2 * half, columns]
            for low in range(2):
                own = slice((2 + low) * half, (3 + low) * half)
                (keep_b_v if chunk else send_b_v)[2 * low + bit] = total[own, columns]
        for source, target in ((keep_a_v, keep_a), (send_a_v, send_a)):
            place = pl.ds(2 * (1 - chunk), 2)
            copies.leave(source.at[place], target.at[place])
        copies.leave(*((keep_b_v, keep_b) if chunk else (send_b_v, send_b)))
    copies.end()


def down_grad(info, mine, lefts_got, actives, after):
    depth, wide = actives[0].shape[-2:]
    half = mine.shape[0] // 4
    shape = (4, half, wide)
    ins = (mine, lefts_got, *actives)
    anywhere = pl.BlockSpec(memory_space=pl.ANY)
    return run(
        down_grad_body,
        info,
        (1,),
        [(value, anywhere) for value in ins],
        [(shape, jnp.bfloat16, anywhere)] * 4,
        [hold(4 * half, 2 * depth), hold(2, 2 * depth, 2 * wide)]
        + [hold(*shape)] * 4
        + [pltpu.SemaphoreType.DMA((24,))],
        after,
    )


def column_grad(info, own, got, rights, parts, groups, after):
    depth = own.shape[-1]
    rows = own.shape[0] // 28
    width = 8 * rows
    count = len(parts)

    def body(info, own, got, *rest):
        rights, rest = rest[: len(rights_in)], rest[len(rights_in) :]
        outs, rest = rest[: 2 * count], rest[2 * count :]
        holds, rest = rest[: 2 * count], rest[2 * count :]
        lefts, wides, semaphores = rest[: len(groups)], rest[len(groups) : -1], rest[-1]
        copies = Copies(semaphores)
        ahead = []
        for at, (spot, start, columns, _) in enumerate(groups):
            copies_of = []
            for block in range(8):
                bit_x, bit_0, bit_1 = 1 - block // 4, block // 2 % 2, block % 2
                owner = (
                    4 * (info[ROW_Z1] ^ bit_1) + 2 * (info[ROW_Z0] ^ bit_0) + (info[ROW_X] ^ bit_x)
                )
                place = pl.ds(pl.multiple_of(spot * width + owner * rows, 16), rows)
                there = slice(block * rows, (block + 1) * rows)
                for kind, source in enumerate((own, got)):
                    target = lefts[at].at[there, kind * depth : (kind + 1) * depth]
                    copies_of.append(copies.start(source.at[place], target))
            for bit in range(2):
                row = 0
                for ref in rights:
                    source = ref.at[ref.shape[0] - 1, info[ROW_Y] ^ bit, :, start : start + columns]
                    tokens = ref.shape[2]
                    target = wides[at].at[row : row + tokens, bit * columns : (bit + 1) * columns]
                    copies_of.append(copies.start(source, target))
                    row += tokens
            ahead.append(copies_of)
        for chunk in range(2):
            totals = []
            for at in range(len(groups)):
                if chunk == 0:
                    for copy in ahead[at]:
                        copy.wait()
                totals.append(dot(lefts[at][chunk * 4 * rows : (chunk + 1) * 4 * rows], wides[at][...]))
            for at, (order, start, columns) in enumerate(parts):
                keep, send = holds[2 * at], holds[2 * at + 1]
                for block in range(4):
                    for bit_y in range(2):
                        piece = gather(totals, block, bit_y, start, columns)
                        bit = {"x": 1 - chunk, "0": block // 2, "1": block % 2, "y": bit_y}
                        spot = tuple(bit[name] for name in order[1:])
                        target = send if bit[order[0]] else keep
                        target[4 * spot[0] + 2 * spot[1] + spot[2]] = piece.astype(jnp.bfloat16)
                if order[0] == "x":
                    copies.leave(*((keep, outs[2 * at]) if chunk else (send, outs[2 * at + 1])))
                elif chunk:
                    copies.leave(keep, outs[2 * at])
                    copies.leave(send, outs[2 * at + 1])
        copies.end()

    def gather(totals, block, bit_y, start, columns):
        own = slice(block * rows, (block + 1) * rows)
        pieces = []
        for at, (_, first, wide, middle) in enumerate(groups):
            after_this = groups[at + 1] if at + 1 < len(groups) else None
            low = max(start, middle // LANES * LANES if at else 0)
            high = min(start + columns, after_this[3] // LANES * LANES if after_this else first + wide)
            base = bit_y * wide - first
            if at and middle % LANES and low == middle // LANES * LANES and low < high:
                before = groups[at - 1]
                lane = lax.broadcasted_iota(jnp.int32, (1, LANES), 1) + low
                old = totals[at - 1][own, bit_y * before[2] - before[1] + low :][:, :LANES]
                new = totals[at][own, base + low : base + low + LANES]
                pieces.append(jnp.where(lane < middle, old, new))
                low += LANES
            if low < high:
                pieces.append(totals[at][own, base + low : base + high])
        return pieces[0] if len(pieces) == 1 else jnp.concatenate(pieces, axis=1)

    rights_in = rights
    anywhere = pl.BlockSpec(memory_space=pl.ANY)
    shapes = [(8, rows, columns) for _, _, columns in parts for _ in range(2)]
    return run(
        body,
        info,
        (1,),
        [(value, anywhere) for value in (own, got, *rights)],
        [(shape, jnp.bfloat16, anywhere) for shape in shapes],
        [hold(*shape) for shape in shapes]
        + [hold(width, 2 * depth)] * len(groups)
        + [hold(2 * depth, 2 * columns) for _, _, columns, _ in groups]
        + [pltpu.SemaphoreType.DMA((64,))],
        after,
        time=8.0,
    )


def fold_body(info, kept_0, kept_1, got_0, got_1, keep, send):
    for kept, got, out in ((kept_0, got_0, keep), (kept_1, got_1, send)):
        out[...] = (kept[...].astype(jnp.float32) + got[...].astype(jnp.float32)).astype(out.dtype)


def fold(info, kept, got, after):
    count, rows, columns = kept.shape
    half = count // 2
    low = pl.BlockSpec((half // 2, rows, columns), lambda step, bits: (step, 0, 0))
    high = pl.BlockSpec((half // 2, rows, columns), lambda step, bits: (step + 2, 0, 0))
    return run(
        fold_body,
        info,
        (2,),
        [(kept, low), (kept, high), (got, low), (got, high)],
        [((half, rows, columns), kept.dtype, low)] * 2,
        (),
        after,
        time=3.0,
    )


def fold_wide_body(info, *refs):
    count = len(refs) // 6
    for at in range(count):
        fold_body(info, *refs[4 * at : 4 * at + 4], *refs[4 * count + 2 * at : 4 * count + 2 * at + 2])


def fold_wide(info, pairs, after):
    ins, outs = [], []
    for kept, got in pairs:
        count, rows, columns = kept.shape
        half = count // 2
        low = pl.BlockSpec((half // 2, rows, columns), lambda step, bits: (step, 0, 0))
        high = pl.BlockSpec((half // 2, rows, columns), lambda step, bits: (step + 2, 0, 0))
        ins += [(value, spec) for value in (kept, got) for spec in (low, high)]
        outs += [((half, rows, columns), kept.dtype, low)] * 2
    results = run(fold_wide_body, info, (2,), ins, outs, (), after)
    return list(zip(results[::2], results[1::2]))


def fold_all_body(info, *refs, join):
    ins = len(refs) - 2 if join is not None else len(refs) // 2
    outs = refs[ins:]
    place = 0
    for at in range(ins // 2):
        kept, got = refs[2 * at], refs[2 * at + 1]
        keep, send = outs if join is not None else outs[2 * at : 2 * at + 2]
        own = [slice(None)] * 3
        if join is not None:
            own[join] = slice(place, place + kept.shape[join])
            place += kept.shape[join]
        half = kept.shape[0] // 2
        if half:
            for out, rows in ((keep, slice(0, half)), (send, slice(half, 2 * half))):
                total = kept[rows].astype(jnp.float32) + got[rows].astype(jnp.float32)
                out[tuple(own)] = total.astype(out.dtype)
            continue
        total = (kept[0].astype(jnp.float32) + got[0].astype(jnp.float32)).astype(keep.dtype)
        half = total.shape[-1] // 2
        for side in range(2):

            @pl.when(info[ROW_X] == side)
            def _():
                keep[0] = total[:, side * half : (side + 1) * half]
                send[0] = total[:, (1 - side) * half : (2 - side) * half]


def fold_all(info, pairs, after, join=None, place=resident, time=5.0):
    shapes = []
    for kept, _ in pairs:
        count, rows, columns = kept.shape
        shapes.append((count // 2, rows, columns) if count > 1 else (1, rows, columns // 2))
    if join is not None:
        shape = list(shapes[0])
        shape[join] = sum(one[join] for one in shapes)
        shapes = [tuple(shape)]
    outs = [(shape, pairs[0][0].dtype, place(shape)) for shape in shapes for _ in range(2)]
    ins = [(value, place(value.shape)) for pair in pairs for value in pair]
    body = functools.partial(fold_all_body, join=join)
    vmem = 24 if place is resident else 63
    results = run(body, info, (1,), ins, outs, (), after, time=time, vmem=vmem)
    return list(zip(results[::2], results[1::2]))


def last_body(info, *refs):
    up, qkv, out = refs[-3:]

    def total(kept, got):
        return kept[0].astype(jnp.float32) + got[0].astype(jnp.float32)

    up[...] = total(*refs[:2])
    both = total(*refs[2:4])
    edge = qkv.shape[1]
    qkv[...] = both[:, :edge]
    out[...] = both[:, edge:]


def down_last_body(info, kept, got, out):
    out[...] = kept[0].astype(jnp.float32) + got[0].astype(jnp.float32)


def back_body(info, *refs):
    others, grad_mine, weight_up, tokens, cot, proj, weight_out, packed, mods, logs = refs[:10]
    resid, grad_packed, shared_0, shared_1, send_0, send_1 = refs[10:16]
    sums, bias_out, bias_qkv = refs[16:19]
    grads, wu, x, g, proj_v, wo, packed_v, acc, resid_v, grad_v, att_v = refs[19:30]
    key_t, query_t, rest_v, result_v, mine_v, send_v, semaphores = refs[30:]
    slots, seq, width = x.shape
    block = wu.shape[-1]
    copies = Copies(semaphores)
    ahead = []
    for at in range(2):
        for kind, source in enumerate((others.at[1, at], grad_mine.at[at])):
            spot = 2 * at + (info[CORE] if kind else 1 - info[CORE])
            place = 2 * at + kind
            ahead.append(copies.start(source, grads.at[place]))
            ahead.append(copies.start(columns_at(weight_up, spot, block), wu.at[place]))
    late = [copies.start(tokens, x), copies.start(cot, g), copies.start(proj, proj_v)]
    got_o = copies.start(weight_out, wo)
    got_p = copies.start(packed, packed_v)
    for place in range(4):
        ahead[2 * place].wait()
        ahead[2 * place + 1].wait()
        part = dot(grads[place], wu[place], 1, 1)
        if place == 0:
            acc[...] = part
        else:
            acc[...] += part
    for copy in late:
        copy.wait()
    bias = jnp.zeros((1, width), jnp.float32)
    for slot in range(slots):
        rows = slice(slot * seq, (slot + 1) * seq)
        grad = acc[rows]
        projected = proj_v[rows]
        normed, factor = layer_norm(x[slot].astype(jnp.float32) + mods[slot, 2:3] * projected)
        live = info[LIVE + slot].astype(jnp.float32)
        sums[slot, 0:1] = jnp.sum(grad, axis=0, keepdims=True)
        sums[slot, 1:2] = jnp.sum(grad * normed, axis=0, keepdims=True)
        back = g[slot].astype(jnp.float32) * live + norm_back(
            grad * (1.0 + mods[slot, 4:5]), normed, factor
        )
        resid_v[rows] = back
        sums[slot, 2:3] = jnp.sum(back * projected, axis=0, keepdims=True)
        result = (back * mods[slot, 2:3]).astype(jnp.bfloat16)
        grad_v[rows] = result
        bias += jnp.sum(result.astype(jnp.float32), axis=0, keepdims=True)
    bias_out[...] = bias
    copies.leave(resid_v, resid)

    got_o.wait()
    att_v[...] = dot(grad_v[...], wo[...], 1, 1).astype(jnp.bfloat16)
    got_p.wait()
    total = jnp.zeros((1, 3 * width), jnp.float32)
    for slot in range(slots):
        rows = slice(slot * seq, (slot + 1) * seq)
        key_t[...] = packed_v[rows, width : 2 * width].T.astype(jnp.float32)
        rest_v[...] = jnp.zeros_like(rest_v)
        for first in range(0, HEADS, GROUP):
            heads = range(first, first + GROUP)
            queries, grads_att, probs, grad_probs = [], [], [], []
            for head in heads:
                start, stop, inside = head_window(head)
                queries.append(jnp.where(inside, packed_v[rows, start:stop], 0))
                grads_att.append(jnp.where(inside, att_v[rows, start:stop], 0))
                key = packed_v[rows, width + start : width + stop]
                value = packed_v[rows, 2 * width + start : 2 * width + stop]
                probs.append(dot(key, queries[-1], 1, 1))
                grad_probs.append(dot(value, grads_att[-1], 1, 1))
            probs = [
                jnp.exp2(score * POWER - logs[slot, head : head + 1])
                for head, score in zip(heads, probs)
            ]
            inner = [
                jnp.sum(prob * grad, axis=0, keepdims=True) for prob, grad in zip(probs, grad_probs)
            ]
            grad_scores = [
                (prob * (grad - mean)).astype(jnp.bfloat16)
                for prob, grad, mean in zip(probs, grad_probs, inner)
            ]
            for at, head in enumerate(heads):
                start, stop, _ = head_window(head)
                own = slice(head * HEAD, (head + 1) * HEAD)
                query_t[own] = dot(key_t[own].astype(jnp.bfloat16), grad_scores[at]) * SCALE
                rest_v[:, start:stop] += dot(grad_scores[at], queries[at]) * SCALE
                rest_v[:, width + start : width + stop] += dot(
                    probs[at].astype(jnp.bfloat16), grads_att[at]
                )
        parts = [query_t[...].T, rest_v[...]]
        result = jnp.concatenate(parts, axis=1)
        low = result.astype(jnp.bfloat16)
        result_v[rows] = low
        total += jnp.sum(low.astype(jnp.float32), axis=0, keepdims=True)
        block, out_block = 3 * width // 4, width // 4
        rounded = grad_v[rows].astype(jnp.float32)
        for at in range(4):
            piece = jnp.concatenate(
                [
                    result[:, at * block : (at + 1) * block],
                    rounded[:, at * out_block : (at + 1) * out_block],
                ],
                axis=1,
            ).astype(jnp.bfloat16)

            @pl.when(info[CORE] == at % 2)
            def _():
                mine_v[slot, at // 2] = piece

            @pl.when(info[CORE] != at % 2)
            def _():
                send_v[slot, at // 2] = piece

        copies.leave(send_v.at[slot], (send_0, send_1)[slot].at[0])
        copies.leave(mine_v.at[slot], (shared_0, shared_1)[slot].at[0])
        copies.leave(result_v.at[rows], grad_packed.at[rows])
    bias_qkv[...] = total
    copies.end()


def token_grad_body(info, *refs):
    grad_packed, weight_qkv, resid, tokens, mods, grad_tokens, sums = refs[:7]
    grads, wq, resid_v, x, acc, tokens_v, semaphores = refs[7:]
    slots, seq, width = x.shape
    copies = Copies(semaphores)
    ahead = []
    for at in range(3):
        third = slice(at * width, (at + 1) * width)
        ahead.append(copies.start(grad_packed.at[:, third], grads.at[at]))
        ahead.append(copies.start(weight_qkv.at[:, third], wq.at[at]))
    late = [copies.start(tokens, x), copies.start(resid, resid_v)]
    for at in range(3):
        ahead[2 * at].wait()
        ahead[2 * at + 1].wait()
        part = dot(grads[at], wq[at], 1, 1)
        if at == 0:
            acc[...] = part
        else:
            acc[...] += part
    for copy in late:
        copy.wait()
    for slot in range(slots):
        rows = slice(slot * seq, (slot + 1) * seq)
        back = acc[rows]
        normed, factor = layer_norm(x[slot].astype(jnp.float32))
        sums[slot, 0:1] = jnp.sum(back, axis=0, keepdims=True)
        sums[slot, 1:2] = jnp.sum(back * normed, axis=0, keepdims=True)
        result = resid_v[rows] + norm_back(back * (1.0 + mods[slot, 1:2]), normed, factor)
        tokens_v[slot] = result.astype(jnp.bfloat16)
        copies.leave(tokens_v.at[slot], grad_tokens.at[slot])
    copies.end()


def output_body(info, *refs):
    others, active_mine, weight_down, tokens, cot, proj, mods, bias, mixed, sums = refs[:10]
    active, wd, x, g, proj_v, acc, mixed_v, semaphores = refs[10:]
    slots, seq, width = x.shape
    block = wd.shape[1]
    copies = Copies(semaphores)
    ahead = []
    for at in range(2):
        for kind, source in enumerate((others.at[0, at], active_mine.at[at])):
            spot = 2 * at + (info[CORE] if kind else 1 - info[CORE])
            place = 2 * at + kind
            ahead.append(copies.start(source, active.at[place]))
            ahead.append(copies.start(rows_at(weight_down, spot, block), wd.at[place]))
    late = [copies.start(tokens, x), copies.start(cot, g), copies.start(proj, proj_v)]
    for place in range(4):
        ahead[2 * place].wait()
        ahead[2 * place + 1].wait()
        part = dot(active[place], wd[place])
        if place == 0:
            acc[...] = part
        else:
            acc[...] += part
    for copy in late:
        copy.wait()
    for slot in range(slots):
        rows = slice(slot * seq, (slot + 1) * seq)
        downward = acc[rows] + bias[...]
        live = info[LIVE + slot].astype(jnp.float32)
        residual = x[slot].astype(jnp.float32) + mods[slot, 2:3] * proj_v[rows]
        mixed_v[slot] = (live * (residual + mods[slot, 5:6] * downward)).astype(jnp.bfloat16)
        copies.leave(mixed_v.at[slot], mixed.at[slot])
        sums[slot] = jnp.sum(g[slot].astype(jnp.float32) * live * downward, axis=0, keepdims=True)
    copies.end()


def small_body(info, sums_a, sums_b, sums_gate, in_qkv, in_out, in_up_0, in_up_1, in_down, *rest):
    keep, send = rest
    width = in_out.shape[-1]
    part = width // 8
    grads = jnp.concatenate(
        [
            jnp.concatenate(
                [
                    sums_a[slot, 0:1],
                    sums_a[slot, 1:2],
                    sums_b[slot, 2:3],
                    sums_b[slot, 0:1],
                    sums_b[slot, 1:2],
                    sums_gate[slot],
                ],
                axis=1,
            )
            for slot in range(sums_a.shape[0])
        ],
        axis=0,
    )
    query, value = in_qkv[:, :width], in_qkv[:, 2 * width :]
    even = info[CORE] == 0
    ups = []
    for at in range(2):
        ups.append(jnp.where(even, in_up_0[at], in_up_1[at]))
        ups.append(jnp.where(even, in_up_1[at], in_up_0[at]))
    up = jnp.concatenate(ups, axis=1)
    wide = up.shape[1] // 8
    columns = grads.shape[1] // 4
    row = lax.broadcasted_iota(jnp.int32, (8, 1), 0)
    biases = []
    for at in range(8):
        own = slice(at * part, (at + 1) * part)
        biases.append(
            jnp.concatenate(
                [
                    query[:, own],
                    value[:, own],
                    in_out[:, own],
                    up[:, at * wide : (at + 1) * wide],
                    in_down[:, own],
                    jnp.zeros((1, columns - 4 * part - wide), jnp.float32),
                ],
                axis=1,
            )
        )
    biases = jnp.concatenate(biases, axis=0)
    for at in range(4):
        total = jnp.zeros((8, columns), jnp.float32)
        for slot in range(grads.shape[0]):
            piece = grads[slot : slot + 1, at * columns : (at + 1) * columns]
            total += jnp.where(row == info[SAMPLE + slot], piece, 0.0)
        total = total.astype(jnp.bfloat16).astype(jnp.float32)
        place = info[ROW_Y] ^ (at // 2)

        @pl.when(info[CORE] == at % 2)
        def _():
            keep[place, :8] = total
            keep[place, 8:] = biases

        @pl.when(info[CORE] != at % 2)
        def _():
            send[place, :8] = total
            send[place, 8:] = biases


def rows_body(info, own, got, weight_t, lifted, part, cond, send, bias, lift, buffer):
    total = own[...] + got[...]
    rows = total[:8].astype(jnp.bfloat16)
    part[...] = rows.astype(jnp.float32)
    cond[...] = dot(rows, weight_t[...])
    columns = part.shape[1]
    edge = -(-columns // LANES) * LANES
    size = lift.shape[1] // 4
    buffer[...] = jnp.zeros_like(buffer)
    buffer[:6, :columns] = part[:6]
    for at in range(2):

        @pl.when(info[ROW_X] == at)
        def _():
            for high in range(4):
                bias[high : high + 1] = total[8 + 2 * high + at : 9 + 2 * high + at]
                row = total[9 + 2 * high - at : 10 + 2 * high - at]
                top = row.astype(jnp.bfloat16).astype(jnp.float32)
                buffer[6 + high : 7 + high, :columns] = top
                buffer[10 + high : 11 + high, :columns] = row - top
                mine, theirs = (2 * high + at) * size, (2 * high + 1 - at) * size
                place = slice(high * size, (high + 1) * size)
                lift[:, place] = lifted[:, mine : mine + size]
                buffer[:8, edge + high * size : edge + (high + 1) * size] = lifted[:, theirs : theirs + size]

    send[...] = buffer[...].astype(send.dtype)


def spread_body(info, part, got, bias, lift, cond, cond_got, both, own_bias, own_lift, cond_sum, *rest):
    sends, total, lifts, buffer = rest[:3], rest[3], rest[4], rest[5]
    cond_sum[...] = cond[...] + cond_got[...]
    columns = part.shape[1]
    edge = -(-columns // LANES) * LANES
    size = lift.shape[1] // 4
    arrived = got[...].astype(jnp.float32)
    total[:4] = bias[...] + arrived[6:10, :columns] + arrived[10:14, :columns]
    lifts[...] = jnp.zeros_like(lifts)
    for high in range(4):
        place = slice(high * size, (high + 1) * size)
        lifts[high, :6] = lift[:6, place]
        lifts[high, 6:12] = arrived[:6, edge + high * size : edge + (high + 1) * size]
    both[...] = jnp.zeros_like(both)
    both[:6] = part[:6]
    both[6:12] = arrived[:6, :columns]
    high = 2 * info[ROW_Z1] + info[ROW_Z0]
    own_bias[...] = total[pl.ds(high, 1)]
    own_lift[...] = lifts[high]
    for far in range(1, 4):
        row = total[pl.ds(high ^ far, 1)]
        top = row.astype(jnp.bfloat16).astype(jnp.float32)
        buffer[...] = jnp.zeros_like(buffer)
        buffer[:12, :columns] = both[:12]
        buffer[12:13, :columns] = top
        buffer[13:14, :columns] = row - top
        buffer[:, edge : edge + size] = lifts[high ^ far]
        sends[far - 1][...] = buffer[...].astype(jnp.bfloat16)


def ada_body(info, both, own_lift, own_bias, got_1, got_2, got_3, weight, bias, sums, rows, lifts):
    columns = both.shape[1]
    size = own_lift.shape[1]
    edge = -(-columns // LANES) * LANES
    row = lax.broadcasted_iota(jnp.int32, (16, 1), 0)
    rows[:16] = both[...].astype(jnp.bfloat16)
    lifts[:16] = own_lift[...].astype(jnp.bfloat16)
    total = own_bias[...]
    for at, got in enumerate((got_1, got_2, got_3)):
        place = pl.ds(16 * (at + 1), 16)
        arrived = got[...].astype(jnp.float32)
        rows[place] = jnp.where(row < 12, arrived[:, :columns], 0.0).astype(jnp.bfloat16)
        lifts[place] = jnp.where(row < 12, arrived[:, edge : edge + size], 0.0).astype(jnp.bfloat16)
        total += arrived[12:13, :columns] + arrived[13:14, :columns]
    sums[...] = total
    weight[...] = dot(lifts[...], rows[...], 0, 0)
    bias[...] = jnp.sum(rows[...].astype(jnp.float32), axis=0, keepdims=True)


def quick_shards(
    tokens,
    condition,
    counts,
    sample_order,
    weight_qkv,
    bias_query,
    bias_value,
    weight_out,
    bias_out,
    weight_up,
    bias_up,
    weight_down,
    bias_down,
    weight_ada,
    bias_ada,
    cotangent,
):
    slots, seq, width = tokens.shape
    count = slots * seq
    ff_width = weight_up.shape[1]
    mod_count, dp_count = lax.axis_size("mod"), lax.axis_size("dp")
    mod_index, dp_index = lax.axis_index("mod"), lax.axis_index("dp")
    f32, bf16 = jnp.float32, jnp.bfloat16
    steps = {"c": ("mod", 1), "y": ("mod", 2), "x": ("dp", 1), "0": ("dp", 2), "1": ("dp", 4)}

    def trade(value, name):
        return swap(value, *steps[name])

    row_total = sample_order.shape[1]
    columns = 6 * width // mod_count
    smem = pl.BlockSpec(memory_space=pltpu.SMEM)
    weight_ada_t = weight_ada.T
    start_ins = [condition, weight_ada_t, bias_ada.astype(f32)[None]]
    start_shapes = [(8, columns), (8, width)]
    info, part_mods, lifted = pl.pallas_call(
        start_body,
        grid_spec=pltpu.PrefetchScalarGridSpec(
            num_scalar_prefetch=2,
            grid=(1,),
            in_specs=[whole(value.shape) for value in start_ins],
            out_specs=[smem] + [whole(shape) for shape in start_shapes],
        ),
        out_shape=[jax.ShapeDtypeStruct((9,), jnp.int32)]
        + [jax.ShapeDtypeStruct(shape, f32) for shape in start_shapes],
        compiler_params=pltpu.CompilerParams(vmem_limit_bytes=63 * 1024 * 1024),
        cost_estimate=cost(3.0),
    )(counts, sample_order, *start_ins)
    parts_got = [swap(part_mods, "mod", far) for far in range(1, mod_count)]
    stats_ins = (tokens, bias_query, bias_value, bias_out, bias_up, bias_down)
    stats_shapes = [(slots, seq, LANES), (1, 3 * width), (1, width), (4, width), (1, width)]
    stats, bias_qkv, bias_out, bias_up, bias_down = run(
        stats_body,
        info,
        (1,),
        [(value, whole(value.shape)) for value in stats_ins],
        [(shape, f32, whole(shape)) for shape in stats_shapes],
        (),
        (part_mods,),
    )

    mods_shape = (slots, 6, width)
    flat = (count, width)
    turned = (width, count)
    row = (1, width)
    left_rows = 7 * width // 2
    block = ff_width // 4
    pair = (2, count, block)
    anywhere = pl.BlockSpec(memory_space=pl.ANY)

    def far_off(*values):
        return [(value, anywhere) for value in values]

    def near(*values):
        return [(value, whole(value.shape)) for value in values]

    def far_outs(*shapes):
        return [(shape, dtype, anywhere) for shape, dtype in shapes]

    def near_outs(*shapes):
        return [(shape, f32, whole(shape)) for shape in shapes]

    lefts, packed, proj, entry_b, grad_down, down_mine, others, mods, logs, bias_down_sum, bias_up_1 = run(
        forward_body,
        info,
        (1,),
        far_off(tokens, cotangent, weight_qkv, weight_out, weight_up, weight_down)
        + near(part_mods, *parts_got, stats, bias_qkv, bias_out, bias_up),
        far_outs(
            ((left_rows, count), bf16),
            ((count, 3 * width), bf16),
            (flat, f32),
            (flat, bf16),
            (flat, bf16),
            ((width // 2, count), bf16),
            ((2, *pair), bf16),
        )
        + near_outs(mods_shape, (slots, HEADS, seq), row, (2, 1, block)),
        [
            hold(slots, seq, width),
            hold(slots, seq, width),
            hold(3, width, width),
            hold(width, width),
            hold(2, width, block),
            hold(2, block, width),
            hold(count, 3 * width),
            hold(left_rows, count),
            pltpu.VMEM(flat, f32),
            hold(*flat),
            hold(*flat),
            hold(width // 2, count),
            hold(2, *pair),
            pltpu.VMEM((width, seq), f32),
            pltpu.VMEM((width, seq), f32),
            pltpu.SemaphoreType.DMA((24,)),
        ],
        time=30.0,
    )
    lefts_got = trade(lefts, "c")
    others_got = trade(others, "c")
    active_mine, grad_up_mine, bias_up_0 = run(
        feed_mine_body,
        info,
        (1,),
        far_off(entry_b, grad_down, weight_up, weight_down) + near(bias_up),
        far_outs((pair, bf16), (pair, bf16)) + near_outs((2, 1, block)),
        [
            hold(*flat),
            hold(*flat),
            hold(2, width, block),
            hold(2, block, width),
            hold(*pair),
            hold(*pair),
            pltpu.SemaphoreType.DMA((12,)),
        ],
        time=9.0,
    )
    active_mine_got = trade(active_mine, "c")

    class Part:
        def __init__(self, kept, send, order):
            self.kept, self.order = kept, order
            self.got = trade(send, order[0])

        def fold(self, after):
            kept, send = fold(info, self.kept, self.got, after)
            return self.go_on(kept, send)

        def go_on(self, kept, send):
            self.kept, self.order = kept, self.order[1:]
            self.got = trade(send, self.order[0])
            return kept

    def join_parts(parts, after, join, place=resident, time=5.0):
        pairs = [(part.kept, part.got) for part in parts]
        ((kept, send),) = fold_all(info, pairs, after, join, place, time)
        return Part(kept, send, parts[0].order[1:]), kept

    def fold_parts(parts, after, step=fold_all):
        folded = step(info, [(part.kept, part.got) for part in parts], after)
        for part, (kept, send) in zip(parts, folded):
            part.go_on(kept, send)
        return folded[-1][0]

    keep, send = column_grad(
        info,
        lefts,
        lefts_got,
        (grad_up_mine.reshape(1, *pair), others_got),
        [("xy10", 0, block)],
        [(2, 0, block, 0)],
        (active_mine,),
    )
    up = Part(keep, send, "xy10")
    token = keep
    keep_a, send_a, keep_b, send_b = down_grad(
        info,
        down_mine,
        lefts_got,
        (others, active_mine, others_got, active_mine_got),
        (token,),
    )
    down_a, down_b = Part(keep_a, send_a, "y01x"), Part(keep_b, send_b, "0y1x")
    token = keep_a

    shared = (1, 2, seq, width)
    packed_shape = (count, 3 * width)
    resid, grad_packed, mine_0, mine_1, send_0, send_1, sums_b, bias_out_sum, bias_qkv_sum = run(
        back_body,
        info,
        (1,),
        far_off(others, grad_up_mine, weight_up, tokens, cotangent, proj, weight_out, packed)
        + near(mods, logs),
        far_outs((flat, f32), (packed_shape, bf16), *[(shared, bf16)] * 4)
        + near_outs((slots, 3, width), row, (1, 3 * width)),
        [
            hold(4, count, block),
            hold(4, width, block),
            hold(slots, seq, width),
            hold(slots, seq, width),
            pltpu.VMEM(flat, f32),
            hold(width, width),
            hold(*packed_shape),
            pltpu.VMEM(flat, f32),
            pltpu.VMEM(flat, f32),
            hold(*flat),
            hold(*flat),
            pltpu.VMEM((width, seq), f32),
            pltpu.VMEM((width, seq), f32),
            pltpu.VMEM((seq, 2 * width), f32),
            hold(*packed_shape),
            hold(slots, *shared[1:]),
            hold(slots, *shared[1:]),
            pltpu.SemaphoreType.DMA((24,)),
        ],
        (token,),
        time=30.0,
    )
    shared_mine = [mine_0, mine_1]
    shared_got = [trade(send_0, "c"), trade(send_1, "c")]
    token = grad_packed
    token = fold_parts((down_a, down_b), (token,), fold_wide)
    seam = 3 * width // 4
    cuts = [0, 4 * LANES, 6 * LANES, width]
    orders = ["xy01", "yx01", "0xy1"]
    halves = column_grad(
        info,
        lefts,
        lefts_got,
        shared_mine + shared_got,
        [(order, low, high - low) for order, low, high in zip(orders, cuts[:-1], cuts[1:])],
        [(0, 0, 7 * LANES, 0), (1, 6 * LANES, width - 6 * LANES, seam)],
        (token,),
    )
    qkv_a, qkv_b, qkv_c = (
        Part(keep, send, order) for keep, send, order in zip(halves[::2], halves[1::2], orders)
    )
    token = up.fold((halves[0],))
    down, token = join_parts((down_a, down_b), (token,), 1, whole)

    grad_tokens, sums_a = run(
        token_grad_body,
        info,
        (1,),
        far_off(grad_packed, weight_qkv, resid, tokens) + near(mods),
        far_outs((tokens.shape, bf16)) + near_outs((slots, 2, width)),
        [
            hold(3, *flat),
            hold(3, width, width),
            pltpu.VMEM(flat, f32),
            hold(slots, seq, width),
            pltpu.VMEM(flat, f32),
            hold(slots, seq, width),
            pltpu.SemaphoreType.DMA((12,)),
        ],
        (token,),
        time=16000.0,
    )
    token = fold_parts((qkv_c,), (sums_a,), fold_wide)
    token = fold_parts((qkv_a, qkv_b), (token,), fold_wide)
    mixed_out, sums_gate = run(
        output_body,
        info,
        (1,),
        far_off(others, active_mine, weight_down, tokens, cotangent, proj) + near(mods, bias_down),
        far_outs((tokens.shape, bf16)) + near_outs((slots, 1, width)),
        [
            hold(4, count, block),
            hold(4, block, width),
            hold(slots, seq, width),
            hold(slots, seq, width),
            pltpu.VMEM(flat, f32),
            pltpu.VMEM(flat, f32),
            hold(slots, seq, width),
            pltpu.SemaphoreType.DMA((16,)),
        ],
        (token,),
        time=20.0,
    )
    token = fold_parts((down,), (sums_gate,))
    token = fold_parts((up,), (token,))
    small_ins = [
        sums_a,
        sums_b,
        sums_gate,
        bias_qkv_sum,
        bias_out_sum,
        bias_up_0,
        bias_up_1,
        bias_down_sum,
    ]
    small_shape = (2, 16, columns)
    small_keep, small_send = run(
        small_body,
        info,
        (1,),
        [(value, resident(value.shape)) for value in small_ins],
        [(small_shape, f32, resident(small_shape))] * 2,
        (),
        (token,),
        vmem=16,
    )
    small = Part(small_keep, small_send, "cy")
    token = fold_parts((small,), (small_keep,))
    qkv, token = join_parts((qkv_a, qkv_b), (token,), 2)
    token = fold_parts((qkv_c,), (token,))
    lift_shape = (8, width // 2)
    edge = -(-columns // LANES) * LANES
    over_x, over_z = (16, edge + width // 2), (16, edge + 2 * LANES)
    rows_outs = [
        ((8, columns), f32),
        ((8, width), f32),
        (over_x, bf16),
        ((4, columns), f32),
        (lift_shape, f32),
    ]
    part_rows, cond_part, send_x, keep_bias, keep_lift = run(
        rows_body,
        info,
        (1,),
        [
            (value, resident(value.shape))
            for value in (small.kept[0], small.got[0], weight_ada_t, lifted)
        ],
        [(shape, dtype, resident(shape)) for shape, dtype in rows_outs],
        [pltpu.VMEM(over_x, f32)],
        (token,),
        vmem=24,
    )
    token = part_rows
    got_x = trade(send_x, "x")
    cond_sum = cond_part + trade(cond_part, "c")
    token = fold_parts((up,), (token,))
    qkv, token = join_parts((qkv, qkv_c), (token,), 2)
    end_shape = (width // mod_count, ff_width // dp_count)
    (grad_down_out,) = run(
        down_last_body,
        info,
        (1,),
        [(value, resident(value.shape)) for value in (down.kept, down.got)],
        [(end_shape, f32, resident(end_shape))],
        (),
        (token,),
        vmem=24,
    )
    token = grad_down_out
    cond_got = trade(cond_sum, "y")
    spread_outs = [((16, columns), f32), ((1, columns), f32), ((16, width // 8), f32), ((8, width), f32)]
    spread_outs += [(over_z, bf16)] * 3
    both, bias_sum, own_lift, cond_sum, *sends = run(
        spread_body,
        info,
        (1,),
        [
            (value, resident(value.shape))
            for value in (part_rows, got_x, keep_bias, keep_lift, cond_sum, cond_got)
        ],
        [(shape, dtype, resident(shape)) for shape, dtype in spread_outs],
        [
            pltpu.VMEM((8, columns), f32),
            pltpu.VMEM((4, 16, width // 8), f32),
            pltpu.VMEM(over_z, f32),
        ],
        (token,),
        vmem=24,
    )
    token = both
    got_z = [swap(sends[far - 1], "dp", 2 * far) for far in range(1, 4)]

    ends = [value for part in (up, qkv) for value in (part.kept, part.got)]
    end_rows = width // dp_count
    end_shapes = [
        (end_rows, ff_width // mod_count),
        (end_rows, 3 * width // mod_count),
        (end_rows, width // mod_count),
    ]
    grad_up_out, grad_qkv_out, grad_out_out = run(
        last_body,
        info,
        (1,),
        [(value, resident(value.shape)) for value in ends],
        [(shape, f32, resident(shape)) for shape in end_shapes],
        (),
        (token,),
        vmem=24,
    )
    token = grad_up_out

    cond_sum = cond_sum[:row_total]
    _, silu_back = jax.vjp(jax.nn.silu, condition)
    grad_condition = silu_back(cond_sum)[0]
    ada_outs = [(width // dp_count, columns), (1, columns), (1, columns)]
    grad_weight_ada, grad_bias_ada, bias_sum = run(
        ada_body,
        info,
        (1,),
        [(value, resident(value.shape)) for value in (both, own_lift, bias_sum, *got_z)],
        [(shape, f32, resident(shape)) for shape in ada_outs],
        [pltpu.VMEM((64, columns), bf16), pltpu.VMEM((64, width // 8), bf16)],
        (token,),
        vmem=24,
    )
    grad_bias_ada, bias_sum = grad_bias_ada[0], bias_sum[0]
    bias_done = []
    for size in (width, width, width, ff_width, width):
        bias_done.append(bias_sum[: size // dp_count])
        bias_sum = bias_sum[size // dp_count :]

    grad_down_out = grad_down_out.T
    return (
        mixed_out,
        grad_tokens,
        grad_condition,
        grad_qkv_out,
        bias_done[0],
        bias_done[1],
        grad_out_out,
        bias_done[2],
        grad_up_out,
        bias_done[3],
        grad_down_out,
        bias_done[4],
        grad_weight_ada,
        grad_bias_ada,
    )


def solution(mesh):
    in_specs = (
        P(("dp", "mod"), None, None),
        P("dp", None),
        P("dp", None),
        P("dp", None),
        P(),
        P(),
        P(),
        P(),
        P(),
        P(),
        P(),
        P(),
        P(),
        P(None, "mod"),
        P("mod"),
        P(("dp", "mod"), None, None),
    )
    out_specs = (
        P(("dp", "mod"), None, None),
        P(("dp", "mod"), None, None),
        P("dp", None),
        P("dp", "mod"),
        P("dp"),
        P("dp"),
        P("dp", "mod"),
        P("dp"),
        P("dp", "mod"),
        P("dp"),
        P("dp", "mod"),
        P("dp"),
        P("dp", "mod"),
        P("mod"),
    )
    quick = mesh.shape["mod"] == 4 and mesh.shape["dp"] == 8
    body = quick_shards if quick else shards
    return jax.shard_map(body, mesh=mesh, in_specs=in_specs, out_specs=out_specs, check_vma=False)
```

```python
import functools

import jax
import jax.numpy as jnp
from jax import lax
from jax.experimental import pallas as pl
from jax.experimental.pallas import tpu as pltpu
from jax.sharding import PartitionSpec as P

HEADS = 16
HEAD = 72
LANES = 128
SCALE = HEAD ** (-0.5)
GELU = (2.0 / 3.141592653589793) ** 0.5
COST = 1.0e6


norm_eps = 1e-06
highest = lax.Precision.HIGHEST


def layer_norm(values_in):
    average = jnp.mean(values_in, axis=-1, keepdims=True)
    centred = values_in - average
    variance = jnp.mean(centred * centred, axis=-1, keepdims=True)
    factor = lax.rsqrt(variance + norm_eps)
    return (centred * factor, factor)


def norm_back(grad_normed, normed, factor):
    first_mean = jnp.mean(grad_normed, axis=-1, keepdims=True)
    second_mean = jnp.mean(grad_normed * normed, axis=-1, keepdims=True)
    return factor * (grad_normed - first_mean - normed * second_mean)


def swap(value, axis, bit):
    pairs = [(index, index ^ bit) for index in range(lax.axis_size(axis))]
    return lax.ppermute(value, axis, pairs)


def own_bit(axis, bit):
    return lax.axis_index(axis) // bit % 2


def pick(value, dim, which):
    return lax.dynamic_index_in_dim(value, which, dim, keepdims=False)


def halve(value, dim, axis, bit):
    mine = own_bit(axis, bit)
    got = swap(pick(value, dim, 1 - mine), axis, bit)
    kept = pick(value, dim, mine)
    return (kept.astype(jnp.float32) + got.astype(jnp.float32)).astype(value.dtype)


def bits_below(count):
    return [1 << power for power in range(count.bit_length() - 1)]


class Scatter:
    def __init__(self, value, names, block):
        self.names = list(names)
        self.value = value.reshape((2,) * len(self.names) + tuple(block))

    def step(self, axis, bit):
        at = self.names.index((axis, bit))
        self.value = halve(self.value, at, axis, bit)
        self.names.pop(at)

    def steps(self, todo):
        for axis, bit in todo:
            self.step(axis, bit)
        return self.value


def weight_grad_kernel(left_own, left_got, right_own, right_got, out_ref):
    total = jnp.dot(left_own[...], right_own[...], preferred_element_type=jnp.float32)
    total += jnp.dot(left_got[...], right_got[...], preferred_element_type=jnp.float32)
    out_ref[...] = total.astype(out_ref.dtype).reshape(out_ref.shape)


def weight_grad(left_own, left_got, right_own, right_got, tile, out_shape, out_block, out_index):
    rows, depth = left_own.shape
    steps = right_own.shape[1] // tile
    left_spec = pl.BlockSpec((rows, depth), lambda step: (0, 0))
    right_spec = pl.BlockSpec((depth, tile), lambda step: (0, step))
    return pl.pallas_call(
        weight_grad_kernel,
        grid=(steps,),
        in_specs=[left_spec, left_spec, right_spec, right_spec],
        out_specs=pl.BlockSpec(out_block, out_index),
        out_shape=jax.ShapeDtypeStruct(out_shape, jnp.bfloat16),
        compiler_params=pltpu.CompilerParams(vmem_limit_bytes=48 * 1024 * 1024),
        cost_estimate=pl.CostEstimate(
            flops=4 * rows * depth * tile * steps,
            bytes_accessed=4 * rows * depth + 4 * depth * tile * steps + 2 * rows * tile * steps,
            transcendentals=0,
        ),
    )(left_own, left_got, right_own, right_got)


def shards(
    tokens,
    condition,
    counts,
    sample_order,
    weight_qkv,
    bias_query,
    bias_value,
    weight_out,
    bias_out,
    weight_up,
    bias_up,
    weight_down,
    bias_down,
    weight_ada,
    bias_ada,
    cotangent,
):
    slot_count, seq_len, model_width = tokens.shape
    mod_count = lax.axis_size("mod")
    mod_index = lax.axis_index("mod")
    dp_count = lax.axis_size("dp")
    half_mod = mod_count // 2
    core = own_bit("mod", 1)
    row_counts = counts[0]
    row_total = sample_order.shape[1]
    starts = jnp.cumsum(row_counts) - row_counts
    device_ids = jnp.arange(mod_count, dtype=jnp.int32)
    own_count = jnp.sum(jnp.where(device_ids == mod_index, row_counts, 0))
    first_slot = jnp.sum(jnp.where(device_ids == mod_index, starts, 0))
    within = jnp.arange(slot_count, dtype=jnp.int32)
    alive_mask = (within < own_count).astype(jnp.float32)
    position = jnp.minimum(first_slot + within, row_total - 1)
    local_rows = jnp.take(sample_order[0], position)
    picker = (local_rows[:, None] == jnp.arange(row_total, dtype=jnp.int32)[None, :]).astype(
        jnp.float32
    )
    lifted = jax.nn.silu(condition).astype(jnp.bfloat16)
    lifted_all = lax.all_gather(lifted, "dp", axis=0, tiled=True)
    part_mods = jnp.dot(lifted, weight_ada, preferred_element_type=jnp.float32) + bias_ada.astype(
        jnp.float32
    )
    modulation = jnp.dot(
        picker, lax.all_gather(part_mods, "mod", axis=1, tiled=True), precision=highest
    )
    pieces = [
        modulation[:, None, column * model_width : (column + 1) * model_width]
        for column in range(6)
    ]
    shift_a, scale_a, gate_a, shift_b, scale_b, gate_b = pieces
    inputs_f = tokens.astype(jnp.float32)
    normed_a, factor_a = layer_norm(inputs_f)
    entry_a = (normed_a * (1.0 + scale_a) + shift_a).astype(jnp.bfloat16)
    bias_qkv = jnp.concatenate([bias_query, jnp.zeros_like(bias_query), bias_value])
    packed = (
        jnp.einsum("bsd,de->bse", entry_a, weight_qkv, preferred_element_type=jnp.float32)
        + bias_qkv
    ).astype(jnp.bfloat16)
    queries = packed[:, :, :model_width].reshape(slot_count, seq_len, HEADS, HEAD)
    keys_all = packed[:, :, model_width : 2 * model_width].reshape(slot_count, seq_len, HEADS, HEAD)
    values_all = packed[:, :, 2 * model_width :].reshape(slot_count, seq_len, HEADS, HEAD)
    score_scale = HEAD ** (-0.5)
    scores = (
        jnp.einsum("bqhd,bkhd->bhqk", queries, keys_all, preferred_element_type=jnp.float32)
        * score_scale
    )
    log_total = jax.nn.logsumexp(scores, axis=-1, keepdims=True)
    softmax_w = jnp.exp(scores - log_total).astype(jnp.bfloat16)
    attended = jnp.einsum(
        "bhqk,bkhd->bqhd", softmax_w, values_all, preferred_element_type=jnp.float32
    )
    attended = attended.reshape(slot_count, seq_len, model_width).astype(jnp.bfloat16)
    projected = (
        jnp.einsum("bsd,de->bse", attended, weight_out, preferred_element_type=jnp.float32)
        + bias_out
    )
    residual = inputs_f + gate_a * projected
    normed_b, factor_b = layer_norm(residual)
    entry_b = (normed_b * (1.0 + scale_b) + shift_b).astype(jnp.bfloat16)
    upward = (
        jnp.einsum("bsd,df->bsf", entry_b, weight_up, preferred_element_type=jnp.float32) + bias_up
    )
    active_low = jax.nn.gelu(upward, approximate=True).astype(jnp.bfloat16)
    downward = (
        jnp.einsum("bsf,fd->bsd", active_low, weight_down, preferred_element_type=jnp.float32)
        + bias_down
    )
    mixed_out = (alive_mask[:, None, None] * (residual + gate_b * downward)).astype(jnp.bfloat16)
    grad_out = cotangent.astype(jnp.float32) * alive_mask[:, None, None]
    grad_gate_b = jnp.sum(grad_out * downward, axis=1)
    grad_down = (grad_out * gate_b).astype(jnp.bfloat16)
    grad_bias_down = jnp.sum(grad_down.astype(jnp.float32), axis=(0, 1))
    grad_active = jnp.einsum(
        "bsd,fd->bsf", grad_down, weight_down, preferred_element_type=jnp.float32
    )
    _, gelu_back = jax.vjp(lambda inside: jax.nn.gelu(inside, approximate=True), upward)
    grad_upward = gelu_back(grad_active)[0].astype(jnp.bfloat16)
    grad_bias_up = jnp.sum(grad_upward.astype(jnp.float32), axis=(0, 1))
    grad_entry_b = jnp.einsum(
        "bsf,df->bsd", grad_upward, weight_up, preferred_element_type=jnp.float32
    )
    grad_shift_b = jnp.sum(grad_entry_b, axis=1)
    grad_scale_b = jnp.sum(grad_entry_b * normed_b, axis=1)
    grad_resid = grad_out + norm_back(grad_entry_b * (1.0 + scale_b), normed_b, factor_b)
    grad_gate_a = jnp.sum(grad_resid * projected, axis=1)
    grad_proj = (grad_resid * gate_a).astype(jnp.bfloat16)
    grad_bias_out = jnp.sum(grad_proj.astype(jnp.float32), axis=(0, 1))
    grad_attended = jnp.einsum(
        "bse,de->bsd", grad_proj, weight_out, preferred_element_type=jnp.float32
    )
    grad_attended = grad_attended.astype(jnp.bfloat16).reshape(slot_count, seq_len, HEADS, HEAD)
    again_scores = (
        jnp.einsum("bqhd,bkhd->bhqk", queries, keys_all, preferred_element_type=jnp.float32)
        * score_scale
    )
    again_probs = jnp.exp(again_scores - log_total)
    again_low = again_probs.astype(jnp.bfloat16)
    grad_values = jnp.einsum(
        "bhqk,bqhd->bkhd", again_low, grad_attended, preferred_element_type=jnp.float32
    )
    grad_probs = jnp.einsum(
        "bqhd,bkhd->bhqk", grad_attended, values_all, preferred_element_type=jnp.float32
    )
    row_dots = jnp.sum(grad_probs * again_probs, axis=-1, keepdims=True)
    grad_scores = (again_probs * (grad_probs - row_dots)).astype(jnp.bfloat16)
    grad_queries = (
        jnp.einsum("bhqk,bkhd->bqhd", grad_scores, keys_all, preferred_element_type=jnp.float32)
        * score_scale
    )
    grad_keys = (
        jnp.einsum("bhqk,bqhd->bkhd", grad_scores, queries, preferred_element_type=jnp.float32)
        * score_scale
    )
    grad_packed = jnp.concatenate(
        [
            grad_queries.reshape(slot_count, seq_len, model_width),
            grad_keys.reshape(slot_count, seq_len, model_width),
            grad_values.reshape(slot_count, seq_len, model_width),
        ],
        axis=-1,
    ).astype(jnp.bfloat16)
    grad_bias_all = jnp.sum(grad_packed.astype(jnp.float32), axis=(0, 1))
    grad_bias_query = grad_bias_all[:model_width]
    grad_bias_value = grad_bias_all[2 * model_width :]
    grad_entry_a = jnp.einsum(
        "bse,de->bsd", grad_packed, weight_qkv, preferred_element_type=jnp.float32
    )
    grad_shift_a = jnp.sum(grad_entry_a, axis=1)
    grad_scale_a = jnp.sum(grad_entry_a * normed_a, axis=1)
    grad_tokens = (
        grad_resid + norm_back(grad_entry_a * (1.0 + scale_a), normed_a, factor_a)
    ).astype(jnp.bfloat16)
    grad_modulation = jnp.concatenate(
        [grad_shift_a, grad_scale_a, grad_gate_a, grad_shift_b, grad_scale_b, grad_gate_b], axis=1
    )
    tokens_here = slot_count * seq_len
    ff_width = weight_up.shape[1]
    dp_bits = bits_below(dp_count)
    cut = max(dp_count // 4, 2)
    x_steps = [("dp", bit) for bit in dp_bits if bit < cut]
    z_steps = [("dp", bit) for bit in dp_bits if bit >= cut]
    y_steps = [("mod", bit) for bit in bits_below(mod_count) if bit > 1]
    dp_names = [("dp", bit) for bit in reversed(dp_bits)]
    y_names = list(reversed(y_steps))
    row_width = model_width // dp_count

    def columns_of(value, block, pad_to):
        parts = value.reshape(tokens_here, half_mod, 2, block)
        halves = []
        for which in (core, 1 - core):
            part = pick(parts, 2, which)
            part = jnp.pad(part, ((0, 0), (0, 0), (0, pad_to - block)))
            halves.append(part.reshape(tokens_here, half_mod * pad_to))
        return halves

    def weight_by_columns(left, right):
        block = right.shape[-1] // mod_count
        pad_to = -(-block // 128) * 128
        left_t = left.reshape(tokens_here, model_width).T
        mine, others = columns_of(right, block, pad_to)
        result = weight_grad(
            left_t,
            swap(left_t, "mod", 1),
            mine,
            swap(others, "mod", 1),
            pad_to,
            (half_mod, model_width, pad_to),
            (1, model_width, pad_to),
            lambda step: (step, 0, 0),
        )
        return Scatter(result, y_names + dp_names, (row_width, pad_to)), block

    down_t = grad_down.reshape(tokens_here, model_width).T.reshape(
        half_mod, 2, model_width // mod_count, tokens_here
    )
    down_mine = pick(down_t, 1, core).reshape(model_width // 2, tokens_here)
    down_others = pick(down_t, 1, 1 - core).reshape(model_width // 2, tokens_here)
    active_flat = active_low.reshape(tokens_here, ff_width)
    down_block = ff_width // dp_count
    piece = cut * down_block
    pieces_count = dp_count // cut
    down_result = weight_grad(
        down_mine,
        swap(down_others, "mod", 1),
        active_flat,
        swap(active_flat, "mod", 1),
        piece,
        (pieces_count, model_width // 2, piece),
        (1, model_width // 2, piece),
        lambda step: (step, 0, 0),
    )
    down_rows = model_width // mod_count
    z_names = list(reversed(z_steps))
    x_names = list(reversed(x_steps))
    down_done = Scatter(down_result, z_names + y_names, (down_rows, piece)).steps(y_steps + z_steps)
    down_done = down_done.reshape(down_rows, cut, down_block).transpose(1, 0, 2)
    down_done = Scatter(down_done, x_names, (down_rows, down_block)).steps(x_steps)
    grad_weight_down = down_done.astype(jnp.float32).T

    up_scatter, up_block = weight_by_columns(entry_b, grad_upward)
    grad_weight_up = up_scatter.steps(x_steps + z_steps + y_steps)[:, :up_block]
    grad_weight_up = grad_weight_up.astype(jnp.float32)
    out_scatter, out_block = weight_by_columns(attended, grad_proj)
    grad_weight_out = out_scatter.steps(x_steps + y_steps + z_steps)[:, :out_block]
    grad_weight_out = grad_weight_out.astype(jnp.float32)
    qkv_scatter, qkv_block = weight_by_columns(entry_a, grad_packed)
    grad_weight_qkv = qkv_scatter.steps(y_steps + x_steps + z_steps)[:, :qkv_block]
    grad_weight_qkv = grad_weight_qkv.astype(jnp.float32)

    bias_parts = [grad_bias_query, grad_bias_value, grad_bias_out, grad_bias_up, grad_bias_down]
    bias_rows = jnp.concatenate([part.reshape(dp_count, -1) for part in bias_parts], axis=1)
    bias_sum = Scatter(bias_rows, dp_names, bias_rows.shape[1:]).steps(x_steps + z_steps)
    for axis, bit in y_steps + [("mod", 1)]:
        bias_sum = bias_sum + swap(bias_sum, axis, bit)
    bias_done = []
    for part in bias_parts:
        width = part.shape[0] // dp_count
        bias_done.append(bias_sum[:width])
        bias_sum = bias_sum[width:]
    row_grads = jnp.dot(picker.T, grad_modulation, precision=highest)
    row_blocks = row_grads.astype(jnp.bfloat16).reshape(row_total, mod_count, -1).transpose(1, 0, 2)
    part_grads = Scatter(
        row_blocks, y_names + [("mod", 1)], row_blocks.shape[1:]
    ).steps([("mod", 1)] + y_steps)
    rows_all = lax.all_gather(part_grads, "dp", axis=0, tiled=True)
    lifted_own = lax.dynamic_slice_in_dim(
        lifted_all, lax.axis_index("dp") * row_width, row_width, axis=1
    )
    grad_weight_ada = jnp.einsum(
        "rd,rc->dc", lifted_own, rows_all, preferred_element_type=jnp.float32
    )
    grad_bias_ada = jnp.sum(rows_all.astype(jnp.float32), axis=0)
    cond_part = jnp.einsum("rc,dc->rd", part_grads, weight_ada, preferred_element_type=jnp.float32)
    cond_sum = cond_part
    for axis, bit in [("mod", 1)] + y_steps:
        cond_sum = cond_sum + swap(cond_sum, axis, bit)
    _, silu_back = jax.vjp(jax.nn.silu, condition)
    grad_condition = silu_back(cond_sum)[0]
    return (
        mixed_out,
        grad_tokens,
        grad_condition,
        grad_weight_qkv,
        bias_done[0],
        bias_done[1],
        grad_weight_out,
        bias_done[2],
        grad_weight_up,
        bias_done[3],
        grad_weight_down,
        bias_done[4],
        grad_weight_ada,
        grad_bias_ada,
    )


def head_window(head):
    low = HEAD * head
    start = low // LANES * LANES
    stop = -(-(low + HEAD) // LANES) * LANES
    lanes = lax.broadcasted_iota(jnp.int32, (1, stop - start), 1) + start
    return start, stop, (lanes >= low) & (lanes < low + HEAD)


def dot(left, right, left_dim=1, right_dim=0):
    return lax.dot_general(
        left, right, (((left_dim,), (right_dim,)), ((), ())), preferred_element_type=jnp.float32
    )


def whole(shape):
    return pl.BlockSpec(shape, lambda *_: (0,) * len(shape))


def cost(time):
    return pl.CostEstimate(flops=int(time * COST), bytes_accessed=1, transcendentals=0)


def resident(shape):
    return pl.BlockSpec(memory_space=pltpu.VMEM)


def run(body, info, grid, ins, outs, scratch=(), after=(), time=5.0, vmem=63):
    count_in, count_after = len(ins), len(after)

    def kernel(info_ref, *refs):
        body(info_ref, *refs[:count_in], *refs[count_in + count_after :])

    return pl.pallas_call(
        kernel,
        grid_spec=pltpu.PrefetchScalarGridSpec(
            num_scalar_prefetch=1,
            grid=grid,
            in_specs=[spec for _, spec in ins] + [pl.BlockSpec(memory_space=pl.ANY)] * count_after,
            out_specs=[spec for _, _, spec in outs],
            scratch_shapes=list(scratch),
        ),
        out_shape=[jax.ShapeDtypeStruct(shape, dtype) for shape, dtype, _ in outs],
        compiler_params=pltpu.CompilerParams(vmem_limit_bytes=vmem * 1024 * 1024),
        cost_estimate=cost(time),
    )(info, *[value for value, _ in ins], *after)


GROUP = 4
POWER = SCALE * 1.4426950408889634
CORE, ROW_Y, ROW_X, ROW_Z0, ROW_Z1, LIVE, SAMPLE = 0, 1, 2, 3, 4, 5, 7


def start_body(counts, order, condition, weight_t, bias_ada, info, part, lifted):
    mod_index, dp_index = lax.axis_index("mod"), lax.axis_index("dp")
    own_count, first_slot = 0, 0
    for at in range(counts.shape[1]):
        own_count += jnp.where(mod_index == at, counts[0, at], 0)
        first_slot += jnp.where(at < mod_index, counts[0, at], 0)
    info[CORE], info[ROW_Y] = mod_index % 2, mod_index // 2
    info[ROW_X], info[ROW_Z0], info[ROW_Z1] = dp_index % 2, dp_index // 2 % 2, dp_index // 4
    for slot in range(2):
        info[LIVE + slot] = jnp.where(slot < own_count, 1, 0)
        info[SAMPLE + slot] = order[0, jnp.minimum(first_slot + slot, order.shape[1] - 1)]
    rows = condition.shape[0]
    values = condition[...]
    values = (values / (1.0 + jnp.exp(-values))).astype(jnp.bfloat16)
    lifted[...] = jnp.zeros_like(lifted)
    lifted[:rows] = values.astype(jnp.float32)
    part[...] = jnp.zeros_like(part)
    part[:rows] = dot(values, weight_t[...], 1, 1) + bias_ada[...]


def stats_body(info, tokens, query, value, out, up, down, stats, bias_qkv, bias_out, bias_up, bias_down):
    for slot in range(tokens.shape[0]):
        values = tokens[slot].astype(jnp.float32)
        average = jnp.mean(values, axis=-1, keepdims=True)
        centred = values - average
        factor = lax.rsqrt(jnp.mean(centred * centred, axis=-1, keepdims=True) + norm_eps)
        lane = lax.broadcasted_iota(jnp.int32, (1, LANES), 1)
        stats[slot] = jnp.where(lane == 0, average, factor)
    width = query.shape[0]
    bias_qkv[...] = jnp.zeros_like(bias_qkv)
    bias_qkv[0, :width] = query[...]
    bias_qkv[0, 2 * width :] = value[...]
    bias_out[0] = out[...]
    for at in range(4):
        bias_up[at] = up[at * width : (at + 1) * width]
    bias_down[0] = down[...]


def feed(entry, down, up, bias, weight_down):
    inner = dot(entry, up) + bias
    back = dot(down, weight_down, 1, 1)
    square = inner * inner
    bend = jnp.tanh(GELU * (inner + 0.044715 * (square * inner)))
    half = 0.5 * (1.0 + bend)
    slope = half + 0.5 * inner * (1.0 - bend * bend) * (GELU + 3.0 * 0.044715 * GELU * square)
    grad = (back * slope).astype(jnp.bfloat16)
    active = (inner * half).astype(jnp.bfloat16)
    return active, grad, jnp.sum(grad.astype(jnp.float32), axis=0, keepdims=True)


class Copies:
    def __init__(self, semaphores):
        self.semaphores, self.count, self.going = semaphores, 0, []

    def start(self, source, target):
        copy = pltpu.make_async_copy(source, target, self.semaphores.at[self.count])
        self.count += 1
        copy.start()
        return copy

    def leave(self, source, target):
        self.going.append(self.start(source, target))

    def end(self):
        for copy in self.going:
            copy.wait()


def columns_at(ref, block, width):
    return ref.at[:, pl.ds(pl.multiple_of(block * width, LANES), width)]


def rows_at(ref, block, width):
    return ref.at[pl.ds(pl.multiple_of(block * width, LANES), width)]


def hold(*shape):
    return pltpu.VMEM(shape, jnp.bfloat16)


def forward_body(info, *refs):
    tokens, cot, weight_qkv, weight_out, weight_up, weight_down = refs[:6]
    parts, stats, bias_qkv, bias_out, bias_up = refs[6:10], refs[10], *refs[11:14]
    lefts, packed, proj, entry_b, down, mine, others = refs[14:21]
    mods, logs, bias_down, bias_grad = refs[21:25]
    x, g, wq, wo, wu, wd, packed_v, lefts_v, proj_v, entry_v, down_v, mine_v, others_v = refs[25:38]
    value_t, out_t, semaphores = refs[38:]
    slots, seq, width = x.shape
    block = wu.shape[-1]
    copies = Copies(semaphores)
    got_x = [copies.start(tokens.at[slot], x.at[slot]) for slot in range(slots)]
    thirds = [slice(at * width, (at + 1) * width) for at in range(3)]
    got_q = [copies.start(weight_qkv.at[:, third], wq.at[at]) for at, third in enumerate(thirds)]
    got_g = copies.start(cot, g)
    got_o = copies.start(weight_out, wo)
    ahead = []
    for at in range(2):
        spot = 2 * at + 1 - info[CORE]
        ahead.append(copies.start(columns_at(weight_up, spot, block), wu.at[at]))
        ahead.append(copies.start(rows_at(weight_down, spot, block), wd.at[at]))

    own = 2 * info[ROW_Y] + info[CORE]
    columns = parts[0].shape[1]
    for slot in range(slots):
        for far, part in enumerate(parts):
            row = part[pl.ds(info[SAMPLE + slot], 1)]
            for spot in range(4):

                @pl.when(own ^ far == spot)
                def _():
                    low, high = spot * columns, (spot + 1) * columns
                    for piece in range(low // width, -(-high // width)):
                        start, stop = max(low, piece * width), min(high, (piece + 1) * width)
                        mods[slot, piece : piece + 1, start - piece * width : stop - piece * width] = (
                            row[:, start - low : stop - low]
                        )

    for slot in range(slots):
        rows = slice(slot * seq, (slot + 1) * seq)
        got_x[slot].wait()
        normed = (x[slot].astype(jnp.float32) - stats[slot, :, :1]) * stats[slot, :, 1:2]
        value = (normed * (1.0 + mods[slot, 1:2]) + mods[slot, 0:1]).astype(jnp.bfloat16)
        entry_v[rows] = value
        lefts_v[:width, rows] = value.T
    for at, third in enumerate(thirds):
        got_q[at].wait()
        part = dot(entry_v[...], wq[at]) + bias_qkv[:, third]
        packed_v[:, third] = part.astype(jnp.bfloat16)
    copies.leave(packed_v, packed)

    got_g.wait()
    sums = jnp.zeros((1, width), jnp.float32)
    for slot in range(slots):
        rows = slice(slot * seq, (slot + 1) * seq)
        live = info[LIVE + slot].astype(jnp.float32)
        grad = (g[slot].astype(jnp.float32) * live * mods[slot, 5:6]).astype(jnp.bfloat16)
        down_v[rows] = grad
        sums += jnp.sum(grad.astype(jnp.float32), axis=0, keepdims=True)
        turned = grad.T
        part = width // 4
        for at in range(4):
            piece = turned[at * part : (at + 1) * part]
            place = at // 2 * part

            @pl.when(info[CORE] == at % 2)
            def _():
                mine_v[place : place + part, rows] = piece

            @pl.when(info[CORE] != at % 2)
            def _():
                lefts_v[3 * width + place : 3 * width + place + part, rows] = piece

    bias_down[...] = sums
    copies.leave(down_v, down)
    copies.leave(mine_v, mine)

    for slot in range(slots):
        rows = slice(slot * seq, (slot + 1) * seq)
        value_t[...] = packed_v[rows, 2 * width :].T.astype(jnp.float32)
        for first in range(0, HEADS, GROUP):
            heads = range(first, first + GROUP)
            scores = []
            for head in heads:
                start, stop, inside = head_window(head)
                query = jnp.where(inside, packed_v[rows, start:stop], 0)
                scores.append(dot(packed_v[rows, width + start : width + stop], query, 1, 1) * POWER)
            tops = [jnp.max(score, axis=0, keepdims=True) for score in scores]
            powers = [jnp.exp2(score - top) for score, top in zip(scores, tops)]
            totals = [jnp.sum(power, axis=0, keepdims=True) for power in powers]
            for head, top, power, total in zip(heads, tops, powers, totals):
                logs[slot, head : head + 1] = top + jnp.log2(total)
                mine_rows = slice(head * HEAD, (head + 1) * HEAD)
                result = dot(value_t[mine_rows].astype(jnp.bfloat16), power.astype(jnp.bfloat16))
                out_t[mine_rows] = result * (1.0 / total)
        lefts_v[width : 2 * width, rows] = out_t[...].astype(jnp.bfloat16)

    got_o.wait()
    proj_v[...] = dot(lefts_v[width : 2 * width], wo[...], 0, 0) + bias_out[...]
    copies.leave(proj_v, proj)
    for slot in range(slots):
        rows = slice(slot * seq, (slot + 1) * seq)
        residual = x[slot].astype(jnp.float32) + mods[slot, 2:3] * proj_v[rows]
        normed, _ = layer_norm(residual)
        value = (normed * (1.0 + mods[slot, 4:5]) + mods[slot, 3:4]).astype(jnp.bfloat16)
        entry_v[rows] = value
        lefts_v[2 * width : 3 * width, rows] = value.T
    copies.leave(lefts_v, lefts)
    copies.leave(entry_v, entry_b)

    for at in range(2):
        ahead[2 * at].wait()
        ahead[2 * at + 1].wait()
        bias = bias_up[pl.ds(2 * at + 1 - info[CORE], 1)]
        others_v[0, at], others_v[1, at], bias_grad[at] = feed(
            entry_v[...], down_v[...], wu[at], bias, wd[at]
        )
        for kind in range(2):
            copies.leave(others_v.at[kind, at], others.at[kind, at])
    copies.end()


def feed_mine_body(info, *refs):
    entry_b, down, weight_up, weight_down, bias_up, active, grad, bias_grad = refs[:8]
    entry_v, down_v, wu, wd, active_v, grad_v, semaphores = refs[8:]
    block = wu.shape[-1]
    copies = Copies(semaphores)
    ahead = [copies.start(entry_b, entry_v)]
    for at in range(2):
        spot = 2 * at + info[CORE]
        ahead.append(copies.start(columns_at(weight_up, spot, block), wu.at[at]))
        if at == 0:
            ahead.append(copies.start(down, down_v))
        ahead.append(copies.start(rows_at(weight_down, spot, block), wd.at[at]))
    for at in range(2):
        for copy in ahead[:4] if at == 0 else ahead[4:]:
            copy.wait()
        bias = bias_up[pl.ds(2 * at + info[CORE], 1)]
        active_v[at], grad_v[at], bias_grad[at] = feed(
            entry_v[...], down_v[...], wu[at], bias, wd[at]
        )
        copies.leave(active_v.at[at], active.at[at])
        copies.leave(grad_v.at[at], grad.at[at])
    copies.end()


def down_grad_body(info, *refs):
    mine, lefts_got, others, active_mine, others_got, mine_got = refs[:6]
    keep_a, send_a, keep_b, send_b = refs[6:10]
    left, right, keep_a_v, send_a_v, keep_b_v, send_b_v, semaphores = refs[10:]
    depth = mine.shape[1]
    rows = mine.shape[0] // 2
    half = rows // 2
    wide = right.shape[-1] // 2
    base = lefts_got.shape[0] - 2 * rows
    copies = Copies(semaphores)
    ahead = []
    for part in range(2):
        for bit in range(2):
            place = slice((2 * part + bit) * half, (2 * part + bit + 1) * half)
            spot = (info[ROW_Y] ^ bit) * rows + part * half
            for source, start, tokens in ((mine, 0, slice(0, depth)), (lefts_got, base, slice(depth, 2 * depth))):
                own = source.at[pl.ds(pl.multiple_of(start + spot, 16), half)]
                ahead.append(copies.start(own, left.at[place, tokens]))
    blocks = [[], []]
    for chunk in range(2):
        same = (info[ROW_Z0] ^ (1 - chunk)) == info[CORE]
        for bit in range(2):
            at = info[ROW_Z1] ^ bit
            columns = slice(bit * wide, (bit + 1) * wide)
            for kind, (one, two) in enumerate(((active_mine, others), (others_got, mine_got))):
                target = right.at[chunk, kind * depth : (kind + 1) * depth, columns]
                one = one.at[at] if kind == 0 else one.at[0, at]
                two = two.at[0, at] if kind == 0 else two.at[at]
                copy = pltpu.make_async_copy(one, target, semaphores.at[copies.count])
                also = pltpu.make_async_copy(two, target, semaphores.at[copies.count])
                copies.count += 1
                pl.when(same)(copy.start)
                pl.when(jnp.logical_not(same))(also.start)
                blocks[chunk].append(copy)
    for copy in ahead:
        copy.wait()
    for chunk in range(2):
        for copy in blocks[chunk]:
            copy.wait()
        total = dot(left[...], right[chunk]).astype(jnp.bfloat16)
        for bit in range(2):
            columns = slice(bit * wide, (bit + 1) * wide)
            place = 2 * (1 - chunk) + bit
            keep_a_v[place] = total[:half, columns]
            send_a_v[place] = total[half : 2 * half, columns]
            for low in range(2):
                own = slice((2 + low) * half, (3 + low) * half)
                (keep_b_v if chunk else send_b_v)[2 * low + bit] = total[own, columns]
        for source, target in ((keep_a_v, keep_a), (send_a_v, send_a)):
            place = pl.ds(2 * (1 - chunk), 2)
            copies.leave(source.at[place], target.at[place])
        copies.leave(*((keep_b_v, keep_b) if chunk else (send_b_v, send_b)))
    copies.end()


def down_grad(info, mine, lefts_got, actives, after):
    depth, wide = actives[0].shape[-2:]
    half = mine.shape[0] // 4
    shape = (4, half, wide)
    ins = (mine, lefts_got, *actives)
    anywhere = pl.BlockSpec(memory_space=pl.ANY)
    return run(
        down_grad_body,
        info,
        (1,),
        [(value, anywhere) for value in ins],
        [(shape, jnp.bfloat16, anywhere)] * 4,
        [hold(4 * half, 2 * depth), hold(2, 2 * depth, 2 * wide)]
        + [hold(*shape)] * 4
        + [pltpu.SemaphoreType.DMA((24,))],
        after,
    )


def column_grad(info, own, got, rights, parts, groups, after):
    depth = own.shape[-1]
    rows = own.shape[0] // 28
    width = 8 * rows
    count = len(parts)

    def body(info, own, got, *rest):
        rights, rest = rest[: len(rights_in)], rest[len(rights_in) :]
        outs, rest = rest[: 2 * count], rest[2 * count :]
        holds, rest = rest[: 2 * count], rest[2 * count :]
        lefts, wides, semaphores = rest[: len(groups)], rest[len(groups) : -1], rest[-1]
        copies = Copies(semaphores)
        ahead = []
        for at, (spot, start, columns, _) in enumerate(groups):
            copies_of = []
            for block in range(8):
                bit_x, bit_0, bit_1 = 1 - block // 4, block // 2 % 2, block % 2
                owner = (
                    4 * (info[ROW_Z1] ^ bit_1) + 2 * (info[ROW_Z0] ^ bit_0) + (info[ROW_X] ^ bit_x)
                )
                place = pl.ds(pl.multiple_of(spot * width + owner * rows, 16), rows)
                there = slice(block * rows, (block + 1) * rows)
                for kind, source in enumerate((own, got)):
                    target = lefts[at].at[there, kind * depth : (kind + 1) * depth]
                    copies_of.append(copies.start(source.at[place], target))
            for bit in range(2):
                row = 0
                for ref in rights:
                    source = ref.at[ref.shape[0] - 1, info[ROW_Y] ^ bit, :, start : start + columns]
                    tokens = ref.shape[2]
                    target = wides[at].at[row : row + tokens, bit * columns : (bit + 1) * columns]
                    copies_of.append(copies.start(source, target))
                    row += tokens
            ahead.append(copies_of)
        for chunk in range(2):
            totals = []
            for at in range(len(groups)):
                if chunk == 0:
                    for copy in ahead[at]:
                        copy.wait()
                totals.append(dot(lefts[at][chunk * 4 * rows : (chunk + 1) * 4 * rows], wides[at][...]))
            for at, (order, start, columns) in enumerate(parts):
                keep, send = holds[2 * at], holds[2 * at + 1]
                for block in range(4):
                    for bit_y in range(2):
                        piece = gather(totals, block, bit_y, start, columns)
                        bit = {"x": 1 - chunk, "0": block // 2, "1": block % 2, "y": bit_y}
                        spot = tuple(bit[name] for name in order[1:])
                        target = send if bit[order[0]] else keep
                        target[4 * spot[0] + 2 * spot[1] + spot[2]] = piece.astype(jnp.bfloat16)
                if order[0] == "x":
                    copies.leave(*((keep, outs[2 * at]) if chunk else (send, outs[2 * at + 1])))
                elif chunk:
                    copies.leave(keep, outs[2 * at])
                    copies.leave(send, outs[2 * at + 1])
        copies.end()

    def gather(totals, block, bit_y, start, columns):
        own = slice(block * rows, (block + 1) * rows)
        pieces = []
        for at, (_, first, wide, middle) in enumerate(groups):
            after_this = groups[at + 1] if at + 1 < len(groups) else None
            low = max(start, middle // LANES * LANES if at else 0)
            high = min(start + columns, after_this[3] // LANES * LANES if after_this else first + wide)
            base = bit_y * wide - first
            if at and middle % LANES and low == middle // LANES * LANES and low < high:
                before = groups[at - 1]
                lane = lax.broadcasted_iota(jnp.int32, (1, LANES), 1) + low
                old = totals[at - 1][own, bit_y * before[2] - before[1] + low :][:, :LANES]
                new = totals[at][own, base + low : base + low + LANES]
                pieces.append(jnp.where(lane < middle, old, new))
                low += LANES
            if low < high:
                pieces.append(totals[at][own, base + low : base + high])
        return pieces[0] if len(pieces) == 1 else jnp.concatenate(pieces, axis=1)

    rights_in = rights
    anywhere = pl.BlockSpec(memory_space=pl.ANY)
    shapes = [(8, rows, columns) for _, _, columns in parts for _ in range(2)]
    return run(
        body,
        info,
        (1,),
        [(value, anywhere) for value in (own, got, *rights)],
        [(shape, jnp.bfloat16, anywhere) for shape in shapes],
        [hold(*shape) for shape in shapes]
        + [hold(width, 2 * depth)] * len(groups)
        + [hold(2 * depth, 2 * columns) for _, _, columns, _ in groups]
        + [pltpu.SemaphoreType.DMA((64,))],
        after,
        time=8.0,
    )


def fold_body(info, kept_0, kept_1, got_0, got_1, keep, send):
    for kept, got, out in ((kept_0, got_0, keep), (kept_1, got_1, send)):
        out[...] = (kept[...].astype(jnp.float32) + got[...].astype(jnp.float32)).astype(out.dtype)


def fold(info, kept, got, after):
    count, rows, columns = kept.shape
    half = count // 2
    low = pl.BlockSpec((half // 2, rows, columns), lambda step, bits: (step, 0, 0))
    high = pl.BlockSpec((half // 2, rows, columns), lambda step, bits: (step + 2, 0, 0))
    return run(
        fold_body,
        info,
        (2,),
        [(kept, low), (kept, high), (got, low), (got, high)],
        [((half, rows, columns), kept.dtype, low)] * 2,
        (),
        after,
        time=3.0,
    )


def fold_wide_body(info, *refs):
    count = len(refs) // 6
    for at in range(count):
        fold_body(info, *refs[4 * at : 4 * at + 4], *refs[4 * count + 2 * at : 4 * count + 2 * at + 2])


def fold_wide(info, pairs, after):
    ins, outs = [], []
    for kept, got in pairs:
        count, rows, columns = kept.shape
        half = count // 2
        low = pl.BlockSpec((half // 2, rows, columns), lambda step, bits: (step, 0, 0))
        high = pl.BlockSpec((half // 2, rows, columns), lambda step, bits: (step + 2, 0, 0))
        ins += [(value, spec) for value in (kept, got) for spec in (low, high)]
        outs += [((half, rows, columns), kept.dtype, low)] * 2
    results = run(fold_wide_body, info, (2,), ins, outs, (), after)
    return list(zip(results[::2], results[1::2]))


def fold_all_body(info, *refs, join):
    ins = len(refs) - 2 if join is not None else len(refs) // 2
    outs = refs[ins:]
    place = 0
    for at in range(ins // 2):
        kept, got = refs[2 * at], refs[2 * at + 1]
        keep, send = outs if join is not None else outs[2 * at : 2 * at + 2]
        own = [slice(None)] * 3
        if join is not None:
            own[join] = slice(place, place + kept.shape[join])
            place += kept.shape[join]
        half = kept.shape[0] // 2
        if half:
            for out, rows in ((keep, slice(0, half)), (send, slice(half, 2 * half))):
                total = kept[rows].astype(jnp.float32) + got[rows].astype(jnp.float32)
                out[tuple(own)] = total.astype(out.dtype)
            continue
        total = (kept[0].astype(jnp.float32) + got[0].astype(jnp.float32)).astype(keep.dtype)
        half = total.shape[-1] // 2
        for side in range(2):

            @pl.when(info[ROW_X] == side)
            def _():
                keep[0] = total[:, side * half : (side + 1) * half]
                send[0] = total[:, (1 - side) * half : (2 - side) * half]


def fold_all(info, pairs, after, join=None, place=resident, time=5.0):
    shapes = []
    for kept, _ in pairs:
        count, rows, columns = kept.shape
        shapes.append((count // 2, rows, columns) if count > 1 else (1, rows, columns // 2))
    if join is not None:
        shape = list(shapes[0])
        shape[join] = sum(one[join] for one in shapes)
        shapes = [tuple(shape)]
    outs = [(shape, pairs[0][0].dtype, place(shape)) for shape in shapes for _ in range(2)]
    ins = [(value, place(value.shape)) for pair in pairs for value in pair]
    body = functools.partial(fold_all_body, join=join)
    vmem = 24 if place is resident else 63
    results = run(body, info, (1,), ins, outs, (), after, time=time, vmem=vmem)
    return list(zip(results[::2], results[1::2]))


def last_body(info, *refs):
    up, qkv, out = refs[-3:]

    def total(kept, got):
        return kept[0].astype(jnp.float32) + got[0].astype(jnp.float32)

    up[...] = total(*refs[:2])
    both = total(*refs[2:4])
    edge = qkv.shape[1]
    qkv[...] = both[:, :edge]
    out[...] = both[:, edge:]


def down_last_body(info, kept, got, out):
    out[...] = kept[0].astype(jnp.float32) + got[0].astype(jnp.float32)


def back_body(info, *refs):
    others, grad_mine, weight_up, tokens, cot, proj, weight_out, packed, mods, logs = refs[:10]
    resid, grad_packed, shared_0, shared_1, send_0, send_1 = refs[10:16]
    sums, bias_out, bias_qkv = refs[16:19]
    grads, wu, x, g, proj_v, wo, packed_v, acc, resid_v, grad_v, att_v = refs[19:30]
    key_t, query_t, rest_v, result_v, mine_v, send_v, semaphores = refs[30:]
    slots, seq, width = x.shape
    block = wu.shape[-1]
    copies = Copies(semaphores)
    ahead = []
    for at in range(2):
        for kind, source in enumerate((others.at[1, at], grad_mine.at[at])):
            spot = 2 * at + (info[CORE] if kind else 1 - info[CORE])
            place = 2 * at + kind
            ahead.append(copies.start(source, grads.at[place]))
            ahead.append(copies.start(columns_at(weight_up, spot, block), wu.at[place]))
    late = [copies.start(tokens, x), copies.start(cot, g), copies.start(proj, proj_v)]
    got_o = copies.start(weight_out, wo)
    got_p = copies.start(packed, packed_v)
    for place in range(4):
        ahead[2 * place].wait()
        ahead[2 * place + 1].wait()
        part = dot(grads[place], wu[place], 1, 1)
        if place == 0:
            acc[...] = part
        else:
            acc[...] += part
    for copy in late:
        copy.wait()
    bias = jnp.zeros((1, width), jnp.float32)
    for slot in range(slots):
        rows = slice(slot * seq, (slot + 1) * seq)
        grad = acc[rows]
        projected = proj_v[rows]
        normed, factor = layer_norm(x[slot].astype(jnp.float32) + mods[slot, 2:3] * projected)
        live = info[LIVE + slot].astype(jnp.float32)
        sums[slot, 0:1] = jnp.sum(grad, axis=0, keepdims=True)
        sums[slot, 1:2] = jnp.sum(grad * normed, axis=0, keepdims=True)
        back = g[slot].astype(jnp.float32) * live + norm_back(
            grad * (1.0 + mods[slot, 4:5]), normed, factor
        )
        resid_v[rows] = back
        sums[slot, 2:3] = jnp.sum(back * projected, axis=0, keepdims=True)
        result = (back * mods[slot, 2:3]).astype(jnp.bfloat16)
        grad_v[rows] = result
        bias += jnp.sum(result.astype(jnp.float32), axis=0, keepdims=True)
    bias_out[...] = bias
    copies.leave(resid_v, resid)

    got_o.wait()
    att_v[...] = dot(grad_v[...], wo[...], 1, 1).astype(jnp.bfloat16)
    got_p.wait()
    total = jnp.zeros((1, 3 * width), jnp.float32)
    for slot in range(slots):
        rows = slice(slot * seq, (slot + 1) * seq)
        key_t[...] = packed_v[rows, width : 2 * width].T.astype(jnp.float32)
        rest_v[...] = jnp.zeros_like(rest_v)
        for first in range(0, HEADS, GROUP):
            heads = range(first, first + GROUP)
            queries, grads_att, probs, grad_probs = [], [], [], []
            for head in heads:
                start, stop, inside = head_window(head)
                queries.append(jnp.where(inside, packed_v[rows, start:stop], 0))
                grads_att.append(jnp.where(inside, att_v[rows, start:stop], 0))
                key = packed_v[rows, width + start : width + stop]
                value = packed_v[rows, 2 * width + start : 2 * width + stop]
                probs.append(dot(key, queries[-1], 1, 1))
                grad_probs.append(dot(value, grads_att[-1], 1, 1))
            probs = [
                jnp.exp2(score * POWER - logs[slot, head : head + 1])
                for head, score in zip(heads, probs)
            ]
            inner = [
                jnp.sum(prob * grad, axis=0, keepdims=True) for prob, grad in zip(probs, grad_probs)
            ]
            grad_scores = [
                (prob * (grad - mean)).astype(jnp.bfloat16)
                for prob, grad, mean in zip(probs, grad_probs, inner)
            ]
            for at, head in enumerate(heads):
                start, stop, _ = head_window(head)
                own = slice(head * HEAD, (head + 1) * HEAD)
                query_t[own] = dot(key_t[own].astype(jnp.bfloat16), grad_scores[at]) * SCALE
                rest_v[:, start:stop] += dot(grad_scores[at], queries[at]) * SCALE
                rest_v[:, width + start : width + stop] += dot(
                    probs[at].astype(jnp.bfloat16), grads_att[at]
                )
        parts = [query_t[...].T, rest_v[...]]
        result = jnp.concatenate(parts, axis=1)
        low = result.astype(jnp.bfloat16)
        result_v[rows] = low
        total += jnp.sum(low.astype(jnp.float32), axis=0, keepdims=True)
        block, out_block = 3 * width // 4, width // 4
        rounded = grad_v[rows].astype(jnp.float32)
        for at in range(4):
            piece = jnp.concatenate(
                [
                    result[:, at * block : (at + 1) * block],
                    rounded[:, at * out_block : (at + 1) * out_block],
                ],
                axis=1,
            ).astype(jnp.bfloat16)

            @pl.when(info[CORE] == at % 2)
            def _():
                mine_v[slot, at // 2] = piece

            @pl.when(info[CORE] != at % 2)
            def _():
                send_v[slot, at // 2] = piece

        copies.leave(send_v.at[slot], (send_0, send_1)[slot].at[0])
        copies.leave(mine_v.at[slot], (shared_0, shared_1)[slot].at[0])
        copies.leave(result_v.at[rows], grad_packed.at[rows])
    bias_qkv[...] = total
    copies.end()


def token_grad_body(info, *refs):
    grad_packed, weight_qkv, resid, tokens, mods, grad_tokens, sums = refs[:7]
    grads, wq, resid_v, x, acc, tokens_v, semaphores = refs[7:]
    slots, seq, width = x.shape
    copies = Copies(semaphores)
    ahead = []
    for at in range(3):
        third = slice(at * width, (at + 1) * width)
        ahead.append(copies.start(grad_packed.at[:, third], grads.at[at]))
        ahead.append(copies.start(weight_qkv.at[:, third], wq.at[at]))
    late = [copies.start(tokens, x), copies.start(resid, resid_v)]
    for at in range(3):
        ahead[2 * at].wait()
        ahead[2 * at + 1].wait()
        part = dot(grads[at], wq[at], 1, 1)
        if at == 0:
            acc[...] = part
        else:
            acc[...] += part
    for copy in late:
        copy.wait()
    for slot in range(slots):
        rows = slice(slot * seq, (slot + 1) * seq)
        back = acc[rows]
        normed, factor = layer_norm(x[slot].astype(jnp.float32))
        sums[slot, 0:1] = jnp.sum(back, axis=0, keepdims=True)
        sums[slot, 1:2] = jnp.sum(back * normed, axis=0, keepdims=True)
        result = resid_v[rows] + norm_back(back * (1.0 + mods[slot, 1:2]), normed, factor)
        tokens_v[slot] = result.astype(jnp.bfloat16)
        copies.leave(tokens_v.at[slot], grad_tokens.at[slot])
    copies.end()


def output_body(info, *refs):
    others, active_mine, weight_down, tokens, cot, proj, mods, bias, mixed, sums = refs[:10]
    active, wd, x, g, proj_v, acc, mixed_v, semaphores = refs[10:]
    slots, seq, width = x.shape
    block = wd.shape[1]
    copies = Copies(semaphores)
    ahead = []
    for at in range(2):
        for kind, source in enumerate((others.at[0, at], active_mine.at[at])):
            spot = 2 * at + (info[CORE] if kind else 1 - info[CORE])
            place = 2 * at + kind
            ahead.append(copies.start(source, active.at[place]))
            ahead.append(copies.start(rows_at(weight_down, spot, block), wd.at[place]))
    late = [copies.start(tokens, x), copies.start(cot, g), copies.start(proj, proj_v)]
    for place in range(4):
        ahead[2 * place].wait()
        ahead[2 * place + 1].wait()
        part = dot(active[place], wd[place])
        if place == 0:
            acc[...] = part
        else:
            acc[...] += part
    for copy in late:
        copy.wait()
    for slot in range(slots):
        rows = slice(slot * seq, (slot + 1) * seq)
        downward = acc[rows] + bias[...]
        live = info[LIVE + slot].astype(jnp.float32)
        residual = x[slot].astype(jnp.float32) + mods[slot, 2:3] * proj_v[rows]
        mixed_v[slot] = (live * (residual + mods[slot, 5:6] * downward)).astype(jnp.bfloat16)
        copies.leave(mixed_v.at[slot], mixed.at[slot])
        sums[slot] = jnp.sum(g[slot].astype(jnp.float32) * live * downward, axis=0, keepdims=True)
    copies.end()


def small_body(info, sums_a, sums_b, sums_gate, in_qkv, in_out, in_up_0, in_up_1, in_down, *rest):
    keep, send = rest
    width = in_out.shape[-1]
    part = width // 8
    grads = jnp.concatenate(
        [
            jnp.concatenate(
                [
                    sums_a[slot, 0:1],
                    sums_a[slot, 1:2],
                    sums_b[slot, 2:3],
                    sums_b[slot, 0:1],
                    sums_b[slot, 1:2],
                    sums_gate[slot],
                ],
                axis=1,
            )
            for slot in range(sums_a.shape[0])
        ],
        axis=0,
    )
    query, value = in_qkv[:, :width], in_qkv[:, 2 * width :]
    even = info[CORE] == 0
    ups = []
    for at in range(2):
        ups.append(jnp.where(even, in_up_0[at], in_up_1[at]))
        ups.append(jnp.where(even, in_up_1[at], in_up_0[at]))
    up = jnp.concatenate(ups, axis=1)
    wide = up.shape[1] // 8
    columns = grads.shape[1] // 4
    row = lax.broadcasted_iota(jnp.int32, (8, 1), 0)
    biases = []
    for at in range(8):
        own = slice(at * part, (at + 1) * part)
        biases.append(
            jnp.concatenate(
                [
                    query[:, own],
                    value[:, own],
                    in_out[:, own],
                    up[:, at * wide : (at + 1) * wide],
                    in_down[:, own],
                    jnp.zeros((1, columns - 4 * part - wide), jnp.float32),
                ],
                axis=1,
            )
        )
    biases = jnp.concatenate(biases, axis=0)
    for at in range(4):
        total = jnp.zeros((8, columns), jnp.float32)
        for slot in range(grads.shape[0]):
            piece = grads[slot : slot + 1, at * columns : (at + 1) * columns]
            total += jnp.where(row == info[SAMPLE + slot], piece, 0.0)
        total = total.astype(jnp.bfloat16).astype(jnp.float32)
        place = info[ROW_Y] ^ (at // 2)

        @pl.when(info[CORE] == at % 2)
        def _():
            keep[place, :8] = total
            keep[place, 8:] = biases

        @pl.when(info[CORE] != at % 2)
        def _():
            send[place, :8] = total
            send[place, 8:] = biases


def rows_body(info, own, got, weight_t, lifted, part, cond, send, bias, lift, buffer):
    total = own[...] + got[...]
    rows = total[:8].astype(jnp.bfloat16)
    part[...] = rows.astype(jnp.float32)
    cond[...] = dot(rows, weight_t[...])
    columns = part.shape[1]
    edge = -(-columns // LANES) * LANES
    size = lift.shape[1] // 4
    buffer[...] = jnp.zeros_like(buffer)
    buffer[:6, :columns] = part[:6]
    for at in range(2):

        @pl.when(info[ROW_X] == at)
        def _():
            for high in range(4):
                bias[high : high + 1] = total[8 + 2 * high + at : 9 + 2 * high + at]
                row = total[9 + 2 * high - at : 10 + 2 * high - at]
                top = row.astype(jnp.bfloat16).astype(jnp.float32)
                buffer[6 + high : 7 + high, :columns] = top
                buffer[10 + high : 11 + high, :columns] = row - top
                mine, theirs = (2 * high + at) * size, (2 * high + 1 - at) * size
                place = slice(high * size, (high + 1) * size)
                lift[:, place] = lifted[:, mine : mine + size]
                buffer[:8, edge + high * size : edge + (high + 1) * size] = lifted[:, theirs : theirs + size]

    send[...] = buffer[...].astype(send.dtype)


def spread_body(info, part, got, bias, lift, cond, cond_got, both, own_bias, own_lift, cond_sum, *rest):
    sends, total, lifts, buffer = rest[:3], rest[3], rest[4], rest[5]
    cond_sum[...] = cond[...] + cond_got[...]
    columns = part.shape[1]
    edge = -(-columns // LANES) * LANES
    size = lift.shape[1] // 4
    arrived = got[...].astype(jnp.float32)
    total[:4] = bias[...] + arrived[6:10, :columns] + arrived[10:14, :columns]
    lifts[...] = jnp.zeros_like(lifts)
    for high in range(4):
        place = slice(high * size, (high + 1) * size)
        lifts[high, :6] = lift[:6, place]
        lifts[high, 6:12] = arrived[:6, edge + high * size : edge + (high + 1) * size]
    both[...] = jnp.zeros_like(both)
    both[:6] = part[:6]
    both[6:12] = arrived[:6, :columns]
    high = 2 * info[ROW_Z1] + info[ROW_Z0]
    own_bias[...] = total[pl.ds(high, 1)]
    own_lift[...] = lifts[high]
    for far in range(1, 4):
        row = total[pl.ds(high ^ far, 1)]
        top = row.astype(jnp.bfloat16).astype(jnp.float32)
        buffer[...] = jnp.zeros_like(buffer)
        buffer[:12, :columns] = both[:12]
        buffer[12:13, :columns] = top
        buffer[13:14, :columns] = row - top
        buffer[:, edge : edge + size] = lifts[high ^ far]
        sends[far - 1][...] = buffer[...].astype(jnp.bfloat16)


def ada_body(info, both, own_lift, own_bias, got_1, got_2, got_3, weight, bias, sums, rows, lifts):
    columns = both.shape[1]
    size = own_lift.shape[1]
    edge = -(-columns // LANES) * LANES
    row = lax.broadcasted_iota(jnp.int32, (16, 1), 0)
    rows[:16] = both[...].astype(jnp.bfloat16)
    lifts[:16] = own_lift[...].astype(jnp.bfloat16)
    total = own_bias[...]
    for at, got in enumerate((got_1, got_2, got_3)):
        place = pl.ds(16 * (at + 1), 16)
        arrived = got[...].astype(jnp.float32)
        rows[place] = jnp.where(row < 12, arrived[:, :columns], 0.0).astype(jnp.bfloat16)
        lifts[place] = jnp.where(row < 12, arrived[:, edge : edge + size], 0.0).astype(jnp.bfloat16)
        total += arrived[12:13, :columns] + arrived[13:14, :columns]
    sums[...] = total
    weight[...] = dot(lifts[...], rows[...], 0, 0)
    bias[...] = jnp.sum(rows[...].astype(jnp.float32), axis=0, keepdims=True)


def quick_shards(
    tokens,
    condition,
    counts,
    sample_order,
    weight_qkv,
    bias_query,
    bias_value,
    weight_out,
    bias_out,
    weight_up,
    bias_up,
    weight_down,
    bias_down,
    weight_ada,
    bias_ada,
    cotangent,
):
    slots, seq, width = tokens.shape
    count = slots * seq
    ff_width = weight_up.shape[1]
    mod_count, dp_count = lax.axis_size("mod"), lax.axis_size("dp")
    mod_index, dp_index = lax.axis_index("mod"), lax.axis_index("dp")
    f32, bf16 = jnp.float32, jnp.bfloat16
    steps = {"c": ("mod", 1), "y": ("mod", 2), "x": ("dp", 1), "0": ("dp", 2), "1": ("dp", 4)}

    def trade(value, name):
        return swap(value, *steps[name])

    row_total = sample_order.shape[1]
    columns = 6 * width // mod_count
    smem = pl.BlockSpec(memory_space=pltpu.SMEM)
    weight_ada_t = weight_ada.T
    start_ins = [condition, weight_ada_t, bias_ada.astype(f32)[None]]
    start_shapes = [(8, columns), (8, width)]
    info, part_mods, lifted = pl.pallas_call(
        start_body,
        grid_spec=pltpu.PrefetchScalarGridSpec(
            num_scalar_prefetch=2,
            grid=(1,),
            in_specs=[whole(value.shape) for value in start_ins],
            out_specs=[smem] + [whole(shape) for shape in start_shapes],
        ),
        out_shape=[jax.ShapeDtypeStruct((9,), jnp.int32)]
        + [jax.ShapeDtypeStruct(shape, f32) for shape in start_shapes],
        compiler_params=pltpu.CompilerParams(vmem_limit_bytes=63 * 1024 * 1024),
        cost_estimate=cost(3.0),
    )(counts, sample_order, *start_ins)
    parts_got = [swap(part_mods, "mod", far) for far in range(1, mod_count)]
    stats_ins = (tokens, bias_query, bias_value, bias_out, bias_up, bias_down)
    stats_shapes = [(slots, seq, LANES), (1, 3 * width), (1, width), (4, width), (1, width)]
    stats, bias_qkv, bias_out, bias_up, bias_down = run(
        stats_body,
        info,
        (1,),
        [(value, whole(value.shape)) for value in stats_ins],
        [(shape, f32, whole(shape)) for shape in stats_shapes],
        (),
        (part_mods,),
    )

    mods_shape = (slots, 6, width)
    flat = (count, width)
    turned = (width, count)
    row = (1, width)
    left_rows = 7 * width // 2
    block = ff_width // 4
    pair = (2, count, block)
    anywhere = pl.BlockSpec(memory_space=pl.ANY)

    def far_off(*values):
        return [(value, anywhere) for value in values]

    def near(*values):
        return [(value, whole(value.shape)) for value in values]

    def far_outs(*shapes):
        return [(shape, dtype, anywhere) for shape, dtype in shapes]

    def near_outs(*shapes):
        return [(shape, f32, whole(shape)) for shape in shapes]

    lefts, packed, proj, entry_b, grad_down, down_mine, others, mods, logs, bias_down_sum, bias_up_1 = run(
        forward_body,
        info,
        (1,),
        far_off(tokens, cotangent, weight_qkv, weight_out, weight_up, weight_down)
        + near(part_mods, *parts_got, stats, bias_qkv, bias_out, bias_up),
        far_outs(
            ((left_rows, count), bf16),
            ((count, 3 * width), bf16),
            (flat, f32),
            (flat, bf16),
            (flat, bf16),
            ((width // 2, count), bf16),
            ((2, *pair), bf16),
        )
        + near_outs(mods_shape, (slots, HEADS, seq), row, (2, 1, block)),
        [
            hold(slots, seq, width),
            hold(slots, seq, width),
            hold(3, width, width),
            hold(width, width),
            hold(2, width, block),
            hold(2, block, width),
            hold(count, 3 * width),
            hold(left_rows, count),
            pltpu.VMEM(flat, f32),
            hold(*flat),
            hold(*flat),
            hold(width // 2, count),
            hold(2, *pair),
            pltpu.VMEM((width, seq), f32),
            pltpu.VMEM((width, seq), f32),
            pltpu.SemaphoreType.DMA((24,)),
        ],
        time=30.0,
    )
    lefts_got = trade(lefts, "c")
    others_got = trade(others, "c")
    active_mine, grad_up_mine, bias_up_0 = run(
        feed_mine_body,
        info,
        (1,),
        far_off(entry_b, grad_down, weight_up, weight_down) + near(bias_up),
        far_outs((pair, bf16), (pair, bf16)) + near_outs((2, 1, block)),
        [
            hold(*flat),
            hold(*flat),
            hold(2, width, block),
            hold(2, block, width),
            hold(*pair),
            hold(*pair),
            pltpu.SemaphoreType.DMA((12,)),
        ],
        time=9.0,
    )
    active_mine_got = trade(active_mine, "c")

    class Part:
        def __init__(self, kept, send, order):
            self.kept, self.order = kept, order
            self.got = trade(send, order[0])

        def fold(self, after):
            kept, send = fold(info, self.kept, self.got, after)
            return self.go_on(kept, send)

        def go_on(self, kept, send):
            self.kept, self.order = kept, self.order[1:]
            self.got = trade(send, self.order[0])
            return kept

    def join_parts(parts, after, join, place=resident, time=5.0):
        pairs = [(part.kept, part.got) for part in parts]
        ((kept, send),) = fold_all(info, pairs, after, join, place, time)
        return Part(kept, send, parts[0].order[1:]), kept

    def fold_parts(parts, after, step=fold_all):
        folded = step(info, [(part.kept, part.got) for part in parts], after)
        for part, (kept, send) in zip(parts, folded):
            part.go_on(kept, send)
        return folded[-1][0]

    keep, send = column_grad(
        info,
        lefts,
        lefts_got,
        (grad_up_mine.reshape(1, *pair), others_got),
        [("xy10", 0, block)],
        [(2, 0, block, 0)],
        (active_mine,),
    )
    up = Part(keep, send, "xy10")
    token = keep
    keep_a, send_a, keep_b, send_b = down_grad(
        info,
        down_mine,
        lefts_got,
        (others, active_mine, others_got, active_mine_got),
        (token,),
    )
    down_a, down_b = Part(keep_a, send_a, "y01x"), Part(keep_b, send_b, "0y1x")
    token = keep_a

    shared = (1, 2, seq, width)
    packed_shape = (count, 3 * width)
    resid, grad_packed, mine_0, mine_1, send_0, send_1, sums_b, bias_out_sum, bias_qkv_sum = run(
        back_body,
        info,
        (1,),
        far_off(others, grad_up_mine, weight_up, tokens, cotangent, proj, weight_out, packed)
        + near(mods, logs),
        far_outs((flat, f32), (packed_shape, bf16), *[(shared, bf16)] * 4)
        + near_outs((slots, 3, width), row, (1, 3 * width)),
        [
            hold(4, count, block),
            hold(4, width, block),
            hold(slots, seq, width),
            hold(slots, seq, width),
            pltpu.VMEM(flat, f32),
            hold(width, width),
            hold(*packed_shape),
            pltpu.VMEM(flat, f32),
            pltpu.VMEM(flat, f32),
            hold(*flat),
            hold(*flat),
            pltpu.VMEM((width, seq), f32),
            pltpu.VMEM((width, seq), f32),
            pltpu.VMEM((seq, 2 * width), f32),
            hold(*packed_shape),
            hold(slots, *shared[1:]),
            hold(slots, *shared[1:]),
            pltpu.SemaphoreType.DMA((24,)),
        ],
        (token,),
        time=30.0,
    )
    shared_mine = [mine_0, mine_1]
    shared_got = [trade(send_0, "c"), trade(send_1, "c")]
    token = grad_packed
    token = fold_parts((down_a, down_b), (token,), fold_wide)
    seam = 3 * width // 4
    cuts = [0, 4 * LANES, 6 * LANES, width]
    orders = ["xy01", "yx01", "0xy1"]
    halves = column_grad(
        info,
        lefts,
        lefts_got,
        shared_mine + shared_got,
        [(order, low, high - low) for order, low, high in zip(orders, cuts[:-1], cuts[1:])],
        [(0, 0, 7 * LANES, 0), (1, 6 * LANES, width - 6 * LANES, seam)],
        (token,),
    )
    qkv_a, qkv_b, qkv_c = (
        Part(keep, send, order) for keep, send, order in zip(halves[::2], halves[1::2], orders)
    )
    token = up.fold((halves[0],))
    down, token = join_parts((down_a, down_b), (token,), 1, whole)

    grad_tokens, sums_a = run(
        token_grad_body,
        info,
        (1,),
        far_off(grad_packed, weight_qkv, resid, tokens) + near(mods),
        far_outs((tokens.shape, bf16)) + near_outs((slots, 2, width)),
        [
            hold(3, *flat),
            hold(3, width, width),
            pltpu.VMEM(flat, f32),
            hold(slots, seq, width),
            pltpu.VMEM(flat, f32),
            hold(slots, seq, width),
            pltpu.SemaphoreType.DMA((12,)),
        ],
        (token,),
        time=16000.0,
    )
    token = fold_parts((qkv_c,), (sums_a,), fold_wide)
    token = fold_parts((qkv_a, qkv_b), (token,), fold_wide)
    mixed_out, sums_gate = run(
        output_body,
        info,
        (1,),
        far_off(others, active_mine, weight_down, tokens, cotangent, proj) + near(mods, bias_down),
        far_outs((tokens.shape, bf16)) + near_outs((slots, 1, width)),
        [
            hold(4, count, block),
            hold(4, block, width),
            hold(slots, seq, width),
            hold(slots, seq, width),
            pltpu.VMEM(flat, f32),
            pltpu.VMEM(flat, f32),
            hold(slots, seq, width),
            pltpu.SemaphoreType.DMA((16,)),
        ],
        (token,),
        time=20.0,
    )
    token = fold_parts((down,), (sums_gate,))
    token = fold_parts((up,), (token,))
    token = fold_parts((qkv_c,), (token,))
    small_ins = [
        sums_a,
        sums_b,
        sums_gate,
        bias_qkv_sum,
        bias_out_sum,
        bias_up_0,
        bias_up_1,
        bias_down_sum,
    ]
    small_shape = (2, 16, columns)
    small_keep, small_send = run(
        small_body,
        info,
        (1,),
        [(value, resident(value.shape)) for value in small_ins],
        [(small_shape, f32, resident(small_shape))] * 2,
        (),
        (token,),
        vmem=16,
    )
    small = Part(small_keep, small_send, "cy")
    qkv, token = join_parts((qkv_a, qkv_b), (small_keep,), 2)
    token = fold_parts((small,), (token,))
    lift_shape = (8, width // 2)
    edge = -(-columns // LANES) * LANES
    over_x, over_z = (16, edge + width // 2), (16, edge + 2 * LANES)
    rows_outs = [
        ((8, columns), f32),
        ((8, width), f32),
        (over_x, bf16),
        ((4, columns), f32),
        (lift_shape, f32),
    ]
    part_rows, cond_part, send_x, keep_bias, keep_lift = run(
        rows_body,
        info,
        (1,),
        [
            (value, resident(value.shape))
            for value in (small.kept[0], small.got[0], weight_ada_t, lifted)
        ],
        [(shape, dtype, resident(shape)) for shape, dtype in rows_outs],
        [pltpu.VMEM(over_x, f32)],
        (token,),
        vmem=24,
    )
    token = part_rows
    got_x = trade(send_x, "x")
    cond_sum = cond_part + trade(cond_part, "c")
    end_shape = (width // mod_count, ff_width // dp_count)
    (grad_down_out,) = run(
        down_last_body,
        info,
        (1,),
        [(value, resident(value.shape)) for value in (down.kept, down.got)],
        [(end_shape, f32, resident(end_shape))],
        (),
        (token,),
        vmem=24,
    )
    token = grad_down_out
    cond_got = trade(cond_sum, "y")
    spread_outs = [((16, columns), f32), ((1, columns), f32), ((16, width // 8), f32), ((8, width), f32)]
    spread_outs += [(over_z, bf16)] * 3
    both, bias_sum, own_lift, cond_sum, *sends = run(
        spread_body,
        info,
        (1,),
        [
            (value, resident(value.shape))
            for value in (part_rows, got_x, keep_bias, keep_lift, cond_sum, cond_got)
        ],
        [(shape, dtype, resident(shape)) for shape, dtype in spread_outs],
        [
            pltpu.VMEM((8, columns), f32),
            pltpu.VMEM((4, 16, width // 8), f32),
            pltpu.VMEM(over_z, f32),
        ],
        (token,),
        vmem=24,
    )
    token = both
    got_z = [swap(sends[far - 1], "dp", 2 * far) for far in range(1, 4)]
    token = fold_parts((up,), (token,))
    qkv, token = join_parts((qkv, qkv_c), (token,), 2)

    ends = [value for part in (up, qkv) for value in (part.kept, part.got)]
    end_rows = width // dp_count
    end_shapes = [
        (end_rows, ff_width // mod_count),
        (end_rows, 3 * width // mod_count),
        (end_rows, width // mod_count),
    ]
    grad_up_out, grad_qkv_out, grad_out_out = run(
        last_body,
        info,
        (1,),
        [(value, resident(value.shape)) for value in ends],
        [(shape, f32, resident(shape)) for shape in end_shapes],
        (),
        (token,),
        vmem=24,
    )
    token = grad_up_out

    cond_sum = cond_sum[:row_total]
    _, silu_back = jax.vjp(jax.nn.silu, condition)
    grad_condition = silu_back(cond_sum)[0]
    ada_outs = [(width // dp_count, columns), (1, columns), (1, columns)]
    grad_weight_ada, grad_bias_ada, bias_sum = run(
        ada_body,
        info,
        (1,),
        [(value, resident(value.shape)) for value in (both, own_lift, bias_sum, *got_z)],
        [(shape, f32, resident(shape)) for shape in ada_outs],
        [pltpu.VMEM((64, columns), bf16), pltpu.VMEM((64, width // 8), bf16)],
        (token,),
        vmem=24,
    )
    grad_bias_ada, bias_sum = grad_bias_ada[0], bias_sum[0]
    bias_done = []
    for size in (width, width, width, ff_width, width):
        bias_done.append(bias_sum[: size // dp_count])
        bias_sum = bias_sum[size // dp_count :]

    grad_down_out = grad_down_out.T
    return (
        mixed_out,
        grad_tokens,
        grad_condition,
        grad_qkv_out,
        bias_done[0],
        bias_done[1],
        grad_out_out,
        bias_done[2],
        grad_up_out,
        bias_done[3],
        grad_down_out,
        bias_done[4],
        grad_weight_ada,
        grad_bias_ada,
    )


def solution(mesh):
    in_specs = (
        P(("dp", "mod"), None, None),
        P("dp", None),
        P("dp", None),
        P("dp", None),
        P(),
        P(),
        P(),
        P(),
        P(),
        P(),
        P(),
        P(),
        P(),
        P(None, "mod"),
        P("mod"),
        P(("dp", "mod"), None, None),
    )
    out_specs = (
        P(("dp", "mod"), None, None),
        P(("dp", "mod"), None, None),
        P("dp", None),
        P("dp", "mod"),
        P("dp"),
        P("dp"),
        P("dp", "mod"),
        P("dp"),
        P("dp", "mod"),
        P("dp"),
        P("dp", "mod"),
        P("dp"),
        P("dp", "mod"),
        P("mod"),
    )
    quick = mesh.shape["mod"] == 4 and mesh.shape["dp"] == 8
    body = quick_shards if quick else shards
    return jax.shard_map(body, mesh=mesh, in_specs=in_specs, out_specs=out_specs, check_vma=False)
```

```python
import functools

import jax
import jax.numpy as jnp
from jax import lax
from jax.experimental import pallas as pl
from jax.experimental.pallas import tpu as pltpu
from jax.sharding import PartitionSpec as P

HEADS = 16
HEAD = 72
LANES = 128
SCALE = HEAD ** (-0.5)
GELU = (2.0 / 3.141592653589793) ** 0.5
COST = 1.0e6


norm_eps = 1e-06
highest = lax.Precision.HIGHEST


def layer_norm(values_in):
    average = jnp.mean(values_in, axis=-1, keepdims=True)
    centred = values_in - average
    variance = jnp.mean(centred * centred, axis=-1, keepdims=True)
    factor = lax.rsqrt(variance + norm_eps)
    return (centred * factor, factor)


def norm_back(grad_normed, normed, factor):
    first_mean = jnp.mean(grad_normed, axis=-1, keepdims=True)
    second_mean = jnp.mean(grad_normed * normed, axis=-1, keepdims=True)
    return factor * (grad_normed - first_mean - normed * second_mean)


def swap(value, axis, bit):
    pairs = [(index, index ^ bit) for index in range(lax.axis_size(axis))]
    return lax.ppermute(value, axis, pairs)


def own_bit(axis, bit):
    return lax.axis_index(axis) // bit % 2


def pick(value, dim, which):
    return lax.dynamic_index_in_dim(value, which, dim, keepdims=False)


def halve(value, dim, axis, bit):
    mine = own_bit(axis, bit)
    got = swap(pick(value, dim, 1 - mine), axis, bit)
    kept = pick(value, dim, mine)
    return (kept.astype(jnp.float32) + got.astype(jnp.float32)).astype(value.dtype)


def bits_below(count):
    return [1 << power for power in range(count.bit_length() - 1)]


class Scatter:
    def __init__(self, value, names, block):
        self.names = list(names)
        self.value = value.reshape((2,) * len(self.names) + tuple(block))

    def step(self, axis, bit):
        at = self.names.index((axis, bit))
        self.value = halve(self.value, at, axis, bit)
        self.names.pop(at)

    def steps(self, todo):
        for axis, bit in todo:
            self.step(axis, bit)
        return self.value


def weight_grad_kernel(left_own, left_got, right_own, right_got, out_ref):
    total = jnp.dot(left_own[...], right_own[...], preferred_element_type=jnp.float32)
    total += jnp.dot(left_got[...], right_got[...], preferred_element_type=jnp.float32)
    out_ref[...] = total.astype(out_ref.dtype).reshape(out_ref.shape)


def weight_grad(left_own, left_got, right_own, right_got, tile, out_shape, out_block, out_index):
    rows, depth = left_own.shape
    steps = right_own.shape[1] // tile
    left_spec = pl.BlockSpec((rows, depth), lambda step: (0, 0))
    right_spec = pl.BlockSpec((depth, tile), lambda step: (0, step))
    return pl.pallas_call(
        weight_grad_kernel,
        grid=(steps,),
        in_specs=[left_spec, left_spec, right_spec, right_spec],
        out_specs=pl.BlockSpec(out_block, out_index),
        out_shape=jax.ShapeDtypeStruct(out_shape, jnp.bfloat16),
        compiler_params=pltpu.CompilerParams(vmem_limit_bytes=48 * 1024 * 1024),
        cost_estimate=pl.CostEstimate(
            flops=4 * rows * depth * tile * steps,
            bytes_accessed=4 * rows * depth + 4 * depth * tile * steps + 2 * rows * tile * steps,
            transcendentals=0,
        ),
    )(left_own, left_got, right_own, right_got)


def shards(
    tokens,
    condition,
    counts,
    sample_order,
    weight_qkv,
    bias_query,
    bias_value,
    weight_out,
    bias_out,
    weight_up,
    bias_up,
    weight_down,
    bias_down,
    weight_ada,
    bias_ada,
    cotangent,
):
    slot_count, seq_len, model_width = tokens.shape
    mod_count = lax.axis_size("mod")
    mod_index = lax.axis_index("mod")
    dp_count = lax.axis_size("dp")
    half_mod = mod_count // 2
    core = own_bit("mod", 1)
    row_counts = counts[0]
    row_total = sample_order.shape[1]
    starts = jnp.cumsum(row_counts) - row_counts
    device_ids = jnp.arange(mod_count, dtype=jnp.int32)
    own_count = jnp.sum(jnp.where(device_ids == mod_index, row_counts, 0))
    first_slot = jnp.sum(jnp.where(device_ids == mod_index, starts, 0))
    within = jnp.arange(slot_count, dtype=jnp.int32)
    alive_mask = (within < own_count).astype(jnp.float32)
    position = jnp.minimum(first_slot + within, row_total - 1)
    local_rows = jnp.take(sample_order[0], position)
    picker = (local_rows[:, None] == jnp.arange(row_total, dtype=jnp.int32)[None, :]).astype(
        jnp.float32
    )
    lifted = jax.nn.silu(condition).astype(jnp.bfloat16)
    lifted_all = lax.all_gather(lifted, "dp", axis=0, tiled=True)
    part_mods = jnp.dot(lifted, weight_ada, preferred_element_type=jnp.float32) + bias_ada.astype(
        jnp.float32
    )
    modulation = jnp.dot(
        picker, lax.all_gather(part_mods, "mod", axis=1, tiled=True), precision=highest
    )
    pieces = [
        modulation[:, None, column * model_width : (column + 1) * model_width]
        for column in range(6)
    ]
    shift_a, scale_a, gate_a, shift_b, scale_b, gate_b = pieces
    inputs_f = tokens.astype(jnp.float32)
    normed_a, factor_a = layer_norm(inputs_f)
    entry_a = (normed_a * (1.0 + scale_a) + shift_a).astype(jnp.bfloat16)
    bias_qkv = jnp.concatenate([bias_query, jnp.zeros_like(bias_query), bias_value])
    packed = (
        jnp.einsum("bsd,de->bse", entry_a, weight_qkv, preferred_element_type=jnp.float32)
        + bias_qkv
    ).astype(jnp.bfloat16)
    queries = packed[:, :, :model_width].reshape(slot_count, seq_len, HEADS, HEAD)
    keys_all = packed[:, :, model_width : 2 * model_width].reshape(slot_count, seq_len, HEADS, HEAD)
    values_all = packed[:, :, 2 * model_width :].reshape(slot_count, seq_len, HEADS, HEAD)
    score_scale = HEAD ** (-0.5)
    scores = (
        jnp.einsum("bqhd,bkhd->bhqk", queries, keys_all, preferred_element_type=jnp.float32)
        * score_scale
    )
    log_total = jax.nn.logsumexp(scores, axis=-1, keepdims=True)
    softmax_w = jnp.exp(scores - log_total).astype(jnp.bfloat16)
    attended = jnp.einsum(
        "bhqk,bkhd->bqhd", softmax_w, values_all, preferred_element_type=jnp.float32
    )
    attended = attended.reshape(slot_count, seq_len, model_width).astype(jnp.bfloat16)
    projected = (
        jnp.einsum("bsd,de->bse", attended, weight_out, preferred_element_type=jnp.float32)
        + bias_out
    )
    residual = inputs_f + gate_a * projected
    normed_b, factor_b = layer_norm(residual)
    entry_b = (normed_b * (1.0 + scale_b) + shift_b).astype(jnp.bfloat16)
    upward = (
        jnp.einsum("bsd,df->bsf", entry_b, weight_up, preferred_element_type=jnp.float32) + bias_up
    )
    active_low = jax.nn.gelu(upward, approximate=True).astype(jnp.bfloat16)
    downward = (
        jnp.einsum("bsf,fd->bsd", active_low, weight_down, preferred_element_type=jnp.float32)
        + bias_down
    )
    mixed_out = (alive_mask[:, None, None] * (residual + gate_b * downward)).astype(jnp.bfloat16)
    grad_out = cotangent.astype(jnp.float32) * alive_mask[:, None, None]
    grad_gate_b = jnp.sum(grad_out * downward, axis=1)
    grad_down = (grad_out * gate_b).astype(jnp.bfloat16)
    grad_bias_down = jnp.sum(grad_down.astype(jnp.float32), axis=(0, 1))
    grad_active = jnp.einsum(
        "bsd,fd->bsf", grad_down, weight_down, preferred_element_type=jnp.float32
    )
    _, gelu_back = jax.vjp(lambda inside: jax.nn.gelu(inside, approximate=True), upward)
    grad_upward = gelu_back(grad_active)[0].astype(jnp.bfloat16)
    grad_bias_up = jnp.sum(grad_upward.astype(jnp.float32), axis=(0, 1))
    grad_entry_b = jnp.einsum(
        "bsf,df->bsd", grad_upward, weight_up, preferred_element_type=jnp.float32
    )
    grad_shift_b = jnp.sum(grad_entry_b, axis=1)
    grad_scale_b = jnp.sum(grad_entry_b * normed_b, axis=1)
    grad_resid = grad_out + norm_back(grad_entry_b * (1.0 + scale_b), normed_b, factor_b)
    grad_gate_a = jnp.sum(grad_resid * projected, axis=1)
    grad_proj = (grad_resid * gate_a).astype(jnp.bfloat16)
    grad_bias_out = jnp.sum(grad_proj.astype(jnp.float32), axis=(0, 1))
    grad_attended = jnp.einsum(
        "bse,de->bsd", grad_proj, weight_out, preferred_element_type=jnp.float32
    )
    grad_attended = grad_attended.astype(jnp.bfloat16).reshape(slot_count, seq_len, HEADS, HEAD)
    again_scores = (
        jnp.einsum("bqhd,bkhd->bhqk", queries, keys_all, preferred_element_type=jnp.float32)
        * score_scale
    )
    again_probs = jnp.exp(again_scores - log_total)
    again_low = again_probs.astype(jnp.bfloat16)
    grad_values = jnp.einsum(
        "bhqk,bqhd->bkhd", again_low, grad_attended, preferred_element_type=jnp.float32
    )
    grad_probs = jnp.einsum(
        "bqhd,bkhd->bhqk", grad_attended, values_all, preferred_element_type=jnp.float32
    )
    row_dots = jnp.sum(grad_probs * again_probs, axis=-1, keepdims=True)
    grad_scores = (again_probs * (grad_probs - row_dots)).astype(jnp.bfloat16)
    grad_queries = (
        jnp.einsum("bhqk,bkhd->bqhd", grad_scores, keys_all, preferred_element_type=jnp.float32)
        * score_scale
    )
    grad_keys = (
        jnp.einsum("bhqk,bqhd->bkhd", grad_scores, queries, preferred_element_type=jnp.float32)
        * score_scale
    )
    grad_packed = jnp.concatenate(
        [
            grad_queries.reshape(slot_count, seq_len, model_width),
            grad_keys.reshape(slot_count, seq_len, model_width),
            grad_values.reshape(slot_count, seq_len, model_width),
        ],
        axis=-1,
    ).astype(jnp.bfloat16)
    grad_bias_all = jnp.sum(grad_packed.astype(jnp.float32), axis=(0, 1))
    grad_bias_query = grad_bias_all[:model_width]
    grad_bias_value = grad_bias_all[2 * model_width :]
    grad_entry_a = jnp.einsum(
        "bse,de->bsd", grad_packed, weight_qkv, preferred_element_type=jnp.float32
    )
    grad_shift_a = jnp.sum(grad_entry_a, axis=1)
    grad_scale_a = jnp.sum(grad_entry_a * normed_a, axis=1)
    grad_tokens = (
        grad_resid + norm_back(grad_entry_a * (1.0 + scale_a), normed_a, factor_a)
    ).astype(jnp.bfloat16)
    grad_modulation = jnp.concatenate(
        [grad_shift_a, grad_scale_a, grad_gate_a, grad_shift_b, grad_scale_b, grad_gate_b], axis=1
    )
    tokens_here = slot_count * seq_len
    ff_width = weight_up.shape[1]
    dp_bits = bits_below(dp_count)
    cut = max(dp_count // 4, 2)
    x_steps = [("dp", bit) for bit in dp_bits if bit < cut]
    z_steps = [("dp", bit) for bit in dp_bits if bit >= cut]
    y_steps = [("mod", bit) for bit in bits_below(mod_count) if bit > 1]
    dp_names = [("dp", bit) for bit in reversed(dp_bits)]
    y_names = list(reversed(y_steps))
    row_width = model_width // dp_count

    def columns_of(value, block, pad_to):
        parts = value.reshape(tokens_here, half_mod, 2, block)
        halves = []
        for which in (core, 1 - core):
            part = pick(parts, 2, which)
            part = jnp.pad(part, ((0, 0), (0, 0), (0, pad_to - block)))
            halves.append(part.reshape(tokens_here, half_mod * pad_to))
        return halves

    def weight_by_columns(left, right):
        block = right.shape[-1] // mod_count
        pad_to = -(-block // 128) * 128
        left_t = left.reshape(tokens_here, model_width).T
        mine, others = columns_of(right, block, pad_to)
        result = weight_grad(
            left_t,
            swap(left_t, "mod", 1),
            mine,
            swap(others, "mod", 1),
            pad_to,
            (half_mod, model_width, pad_to),
            (1, model_width, pad_to),
            lambda step: (step, 0, 0),
        )
        return Scatter(result, y_names + dp_names, (row_width, pad_to)), block

    down_t = grad_down.reshape(tokens_here, model_width).T.reshape(
        half_mod, 2, model_width // mod_count, tokens_here
    )
    down_mine = pick(down_t, 1, core).reshape(model_width // 2, tokens_here)
    down_others = pick(down_t, 1, 1 - core).reshape(model_width // 2, tokens_here)
    active_flat = active_low.reshape(tokens_here, ff_width)
    down_block = ff_width // dp_count
    piece = cut * down_block
    pieces_count = dp_count // cut
    down_result = weight_grad(
        down_mine,
        swap(down_others, "mod", 1),
        active_flat,
        swap(active_flat, "mod", 1),
        piece,
        (pieces_count, model_width // 2, piece),
        (1, model_width // 2, piece),
        lambda step: (step, 0, 0),
    )
    down_rows = model_width // mod_count
    z_names = list(reversed(z_steps))
    x_names = list(reversed(x_steps))
    down_done = Scatter(down_result, z_names + y_names, (down_rows, piece)).steps(y_steps + z_steps)
    down_done = down_done.reshape(down_rows, cut, down_block).transpose(1, 0, 2)
    down_done = Scatter(down_done, x_names, (down_rows, down_block)).steps(x_steps)
    grad_weight_down = down_done.astype(jnp.float32).T

    up_scatter, up_block = weight_by_columns(entry_b, grad_upward)
    grad_weight_up = up_scatter.steps(x_steps + z_steps + y_steps)[:, :up_block]
    grad_weight_up = grad_weight_up.astype(jnp.float32)
    out_scatter, out_block = weight_by_columns(attended, grad_proj)
    grad_weight_out = out_scatter.steps(x_steps + y_steps + z_steps)[:, :out_block]
    grad_weight_out = grad_weight_out.astype(jnp.float32)
    qkv_scatter, qkv_block = weight_by_columns(entry_a, grad_packed)
    grad_weight_qkv = qkv_scatter.steps(y_steps + x_steps + z_steps)[:, :qkv_block]
    grad_weight_qkv = grad_weight_qkv.astype(jnp.float32)

    bias_parts = [grad_bias_query, grad_bias_value, grad_bias_out, grad_bias_up, grad_bias_down]
    bias_rows = jnp.concatenate([part.reshape(dp_count, -1) for part in bias_parts], axis=1)
    bias_sum = Scatter(bias_rows, dp_names, bias_rows.shape[1:]).steps(x_steps + z_steps)
    for axis, bit in y_steps + [("mod", 1)]:
        bias_sum = bias_sum + swap(bias_sum, axis, bit)
    bias_done = []
    for part in bias_parts:
        width = part.shape[0] // dp_count
        bias_done.append(bias_sum[:width])
        bias_sum = bias_sum[width:]
    row_grads = jnp.dot(picker.T, grad_modulation, precision=highest)
    row_blocks = row_grads.astype(jnp.bfloat16).reshape(row_total, mod_count, -1).transpose(1, 0, 2)
    part_grads = Scatter(
        row_blocks, y_names + [("mod", 1)], row_blocks.shape[1:]
    ).steps([("mod", 1)] + y_steps)
    rows_all = lax.all_gather(part_grads, "dp", axis=0, tiled=True)
    lifted_own = lax.dynamic_slice_in_dim(
        lifted_all, lax.axis_index("dp") * row_width, row_width, axis=1
    )
    grad_weight_ada = jnp.einsum(
        "rd,rc->dc", lifted_own, rows_all, preferred_element_type=jnp.float32
    )
    grad_bias_ada = jnp.sum(rows_all.astype(jnp.float32), axis=0)
    cond_part = jnp.einsum("rc,dc->rd", part_grads, weight_ada, preferred_element_type=jnp.float32)
    cond_sum = cond_part
    for axis, bit in [("mod", 1)] + y_steps:
        cond_sum = cond_sum + swap(cond_sum, axis, bit)
    _, silu_back = jax.vjp(jax.nn.silu, condition)
    grad_condition = silu_back(cond_sum)[0]
    return (
        mixed_out,
        grad_tokens,
        grad_condition,
        grad_weight_qkv,
        bias_done[0],
        bias_done[1],
        grad_weight_out,
        bias_done[2],
        grad_weight_up,
        bias_done[3],
        grad_weight_down,
        bias_done[4],
        grad_weight_ada,
        grad_bias_ada,
    )


def head_window(head):
    low = HEAD * head
    start = low // LANES * LANES
    stop = -(-(low + HEAD) // LANES) * LANES
    lanes = lax.broadcasted_iota(jnp.int32, (1, stop - start), 1) + start
    return start, stop, (lanes >= low) & (lanes < low + HEAD)


def dot(left, right, left_dim=1, right_dim=0):
    return lax.dot_general(
        left, right, (((left_dim,), (right_dim,)), ((), ())), preferred_element_type=jnp.float32
    )


def whole(shape):
    return pl.BlockSpec(shape, lambda *_: (0,) * len(shape))


def cost(time):
    return pl.CostEstimate(flops=int(time * COST), bytes_accessed=1, transcendentals=0)


def resident(shape):
    return pl.BlockSpec(memory_space=pltpu.VMEM)


def run(body, info, grid, ins, outs, scratch=(), after=(), time=5.0, vmem=63):
    count_in, count_after = len(ins), len(after)

    def kernel(info_ref, *refs):
        body(info_ref, *refs[:count_in], *refs[count_in + count_after :])

    return pl.pallas_call(
        kernel,
        grid_spec=pltpu.PrefetchScalarGridSpec(
            num_scalar_prefetch=1,
            grid=grid,
            in_specs=[spec for _, spec in ins] + [pl.BlockSpec(memory_space=pl.ANY)] * count_after,
            out_specs=[spec for _, _, spec in outs],
            scratch_shapes=list(scratch),
        ),
        out_shape=[jax.ShapeDtypeStruct(shape, dtype) for shape, dtype, _ in outs],
        compiler_params=pltpu.CompilerParams(vmem_limit_bytes=vmem * 1024 * 1024),
        cost_estimate=cost(time),
    )(info, *[value for value, _ in ins], *after)


GROUP = 4
POWER = SCALE * 1.4426950408889634
CORE, ROW_Y, ROW_X, ROW_Z0, ROW_Z1, LIVE, SAMPLE = 0, 1, 2, 3, 4, 5, 7


def start_body(counts, order, condition, weight_t, bias_ada, info, part, lifted):
    mod_index, dp_index = lax.axis_index("mod"), lax.axis_index("dp")
    own_count, first_slot = 0, 0
    for at in range(counts.shape[1]):
        own_count += jnp.where(mod_index == at, counts[0, at], 0)
        first_slot += jnp.where(at < mod_index, counts[0, at], 0)
    info[CORE], info[ROW_Y] = mod_index % 2, mod_index // 2
    info[ROW_X], info[ROW_Z0], info[ROW_Z1] = dp_index % 2, dp_index // 2 % 2, dp_index // 4
    for slot in range(2):
        info[LIVE + slot] = jnp.where(slot < own_count, 1, 0)
        info[SAMPLE + slot] = order[0, jnp.minimum(first_slot + slot, order.shape[1] - 1)]
    rows = condition.shape[0]
    values = condition[...]
    values = (values / (1.0 + jnp.exp(-values))).astype(jnp.bfloat16)
    lifted[...] = jnp.zeros_like(lifted)
    lifted[:rows] = values.astype(jnp.float32)
    part[...] = jnp.zeros_like(part)
    part[:rows] = dot(values, weight_t[...], 1, 1) + bias_ada[...]


def stats_body(info, tokens, query, value, out, up, down, stats, bias_qkv, bias_out, bias_up, bias_down):
    for slot in range(tokens.shape[0]):
        values = tokens[slot].astype(jnp.float32)
        average = jnp.mean(values, axis=-1, keepdims=True)
        centred = values - average
        factor = lax.rsqrt(jnp.mean(centred * centred, axis=-1, keepdims=True) + norm_eps)
        lane = lax.broadcasted_iota(jnp.int32, (1, LANES), 1)
        stats[slot] = jnp.where(lane == 0, average, factor)
    width = query.shape[0]
    bias_qkv[...] = jnp.zeros_like(bias_qkv)
    bias_qkv[0, :width] = query[...]
    bias_qkv[0, 2 * width :] = value[...]
    bias_out[0] = out[...]
    for at in range(4):
        bias_up[at] = up[at * width : (at + 1) * width]
    bias_down[0] = down[...]


def feed(entry, down, up, bias, weight_down):
    inner = dot(entry, up) + bias
    back = dot(down, weight_down, 1, 1)
    square = inner * inner
    bend = jnp.tanh(GELU * (inner + 0.044715 * (square * inner)))
    half = 0.5 * (1.0 + bend)
    slope = half + 0.5 * inner * (1.0 - bend * bend) * (GELU + 3.0 * 0.044715 * GELU * square)
    grad = (back * slope).astype(jnp.bfloat16)
    active = (inner * half).astype(jnp.bfloat16)
    return active, grad, jnp.sum(grad.astype(jnp.float32), axis=0, keepdims=True)


class Copies:
    def __init__(self, semaphores):
        self.semaphores, self.count, self.going = semaphores, 0, []

    def start(self, source, target):
        copy = pltpu.make_async_copy(source, target, self.semaphores.at[self.count])
        self.count += 1
        copy.start()
        return copy

    def leave(self, source, target):
        self.going.append(self.start(source, target))

    def end(self):
        for copy in self.going:
            copy.wait()


def columns_at(ref, block, width):
    return ref.at[:, pl.ds(pl.multiple_of(block * width, LANES), width)]


def rows_at(ref, block, width):
    return ref.at[pl.ds(pl.multiple_of(block * width, LANES), width)]


def hold(*shape):
    return pltpu.VMEM(shape, jnp.bfloat16)


def forward_body(info, *refs):
    tokens, cot, weight_qkv, weight_out, weight_up, weight_down = refs[:6]
    parts, stats, bias_qkv, bias_out, bias_up = refs[6:10], refs[10], *refs[11:14]
    lefts, packed, proj, entry_b, down, mine, others = refs[14:21]
    mods, logs, bias_down, bias_grad = refs[21:25]
    x, g, wq, wo, wu, wd, packed_v, lefts_v, proj_v, entry_v, down_v, mine_v, others_v = refs[25:38]
    value_t, out_t, semaphores = refs[38:]
    slots, seq, width = x.shape
    block = wu.shape[-1]
    copies = Copies(semaphores)
    got_x = [copies.start(tokens.at[slot], x.at[slot]) for slot in range(slots)]
    thirds = [slice(at * width, (at + 1) * width) for at in range(3)]
    got_q = [copies.start(weight_qkv.at[:, third], wq.at[at]) for at, third in enumerate(thirds)]
    got_g = copies.start(cot, g)
    got_o = copies.start(weight_out, wo)
    ahead = []
    for at in range(2):
        spot = 2 * at + 1 - info[CORE]
        ahead.append(copies.start(columns_at(weight_up, spot, block), wu.at[at]))
        ahead.append(copies.start(rows_at(weight_down, spot, block), wd.at[at]))

    own = 2 * info[ROW_Y] + info[CORE]
    columns = parts[0].shape[1]
    for slot in range(slots):
        for far, part in enumerate(parts):
            row = part[pl.ds(info[SAMPLE + slot], 1)]
            for spot in range(4):

                @pl.when(own ^ far == spot)
                def _():
                    low, high = spot * columns, (spot + 1) * columns
                    for piece in range(low // width, -(-high // width)):
                        start, stop = max(low, piece * width), min(high, (piece + 1) * width)
                        mods[slot, piece : piece + 1, start - piece * width : stop - piece * width] = (
                            row[:, start - low : stop - low]
                        )

    for slot in range(slots):
        rows = slice(slot * seq, (slot + 1) * seq)
        got_x[slot].wait()
        normed = (x[slot].astype(jnp.float32) - stats[slot, :, :1]) * stats[slot, :, 1:2]
        value = (normed * (1.0 + mods[slot, 1:2]) + mods[slot, 0:1]).astype(jnp.bfloat16)
        entry_v[rows] = value
        lefts_v[:width, rows] = value.T
    for at, third in enumerate(thirds):
        got_q[at].wait()
        part = dot(entry_v[...], wq[at]) + bias_qkv[:, third]
        packed_v[:, third] = part.astype(jnp.bfloat16)
    copies.leave(packed_v, packed)

    got_g.wait()
    sums = jnp.zeros((1, width), jnp.float32)
    for slot in range(slots):
        rows = slice(slot * seq, (slot + 1) * seq)
        live = info[LIVE + slot].astype(jnp.float32)
        grad = (g[slot].astype(jnp.float32) * live * mods[slot, 5:6]).astype(jnp.bfloat16)
        down_v[rows] = grad
        sums += jnp.sum(grad.astype(jnp.float32), axis=0, keepdims=True)
        turned = grad.T
        part = width // 4
        for at in range(4):
            piece = turned[at * part : (at + 1) * part]
            place = at // 2 * part

            @pl.when(info[CORE] == at % 2)
            def _():
                mine_v[place : place + part, rows] = piece

            @pl.when(info[CORE] != at % 2)
            def _():
                lefts_v[3 * width + place : 3 * width + place + part, rows] = piece

    bias_down[...] = sums
    copies.leave(down_v, down)
    copies.leave(mine_v, mine)

    for slot in range(slots):
        rows = slice(slot * seq, (slot + 1) * seq)
        value_t[...] = packed_v[rows, 2 * width :].T.astype(jnp.float32)
        for first in range(0, HEADS, GROUP):
            heads = range(first, first + GROUP)
            scores = []
            for head in heads:
                start, stop, inside = head_window(head)
                query = jnp.where(inside, packed_v[rows, start:stop], 0)
                scores.append(dot(packed_v[rows, width + start : width + stop], query, 1, 1) * POWER)
            tops = [jnp.max(score, axis=0, keepdims=True) for score in scores]
            powers = [jnp.exp2(score - top) for score, top in zip(scores, tops)]
            totals = [jnp.sum(power, axis=0, keepdims=True) for power in powers]
            for head, top, power, total in zip(heads, tops, powers, totals):
                logs[slot, head : head + 1] = top + jnp.log2(total)
                mine_rows = slice(head * HEAD, (head + 1) * HEAD)
                result = dot(value_t[mine_rows].astype(jnp.bfloat16), power.astype(jnp.bfloat16))
                out_t[mine_rows] = result * (1.0 / total)
        lefts_v[width : 2 * width, rows] = out_t[...].astype(jnp.bfloat16)

    got_o.wait()
    proj_v[...] = dot(lefts_v[width : 2 * width], wo[...], 0, 0) + bias_out[...]
    copies.leave(proj_v, proj)
    for slot in range(slots):
        rows = slice(slot * seq, (slot + 1) * seq)
        residual = x[slot].astype(jnp.float32) + mods[slot, 2:3] * proj_v[rows]
        normed, _ = layer_norm(residual)
        value = (normed * (1.0 + mods[slot, 4:5]) + mods[slot, 3:4]).astype(jnp.bfloat16)
        entry_v[rows] = value
        lefts_v[2 * width : 3 * width, rows] = value.T
    copies.leave(lefts_v, lefts)
    copies.leave(entry_v, entry_b)

    for at in range(2):
        ahead[2 * at].wait()
        ahead[2 * at + 1].wait()
        bias = bias_up[pl.ds(2 * at + 1 - info[CORE], 1)]
        others_v[0, at], others_v[1, at], bias_grad[at] = feed(
            entry_v[...], down_v[...], wu[at], bias, wd[at]
        )
        for kind in range(2):
            copies.leave(others_v.at[kind, at], others.at[kind, at])
    copies.end()


def feed_mine_body(info, *refs):
    entry_b, down, weight_up, weight_down, bias_up, active, grad, bias_grad = refs[:8]
    entry_v, down_v, wu, wd, active_v, grad_v, semaphores = refs[8:]
    block = wu.shape[-1]
    copies = Copies(semaphores)
    ahead = [copies.start(entry_b, entry_v)]
    for at in range(2):
        spot = 2 * at + info[CORE]
        ahead.append(copies.start(columns_at(weight_up, spot, block), wu.at[at]))
        if at == 0:
            ahead.append(copies.start(down, down_v))
        ahead.append(copies.start(rows_at(weight_down, spot, block), wd.at[at]))
    for at in range(2):
        for copy in ahead[:4] if at == 0 else ahead[4:]:
            copy.wait()
        bias = bias_up[pl.ds(2 * at + info[CORE], 1)]
        active_v[at], grad_v[at], bias_grad[at] = feed(
            entry_v[...], down_v[...], wu[at], bias, wd[at]
        )
        copies.leave(active_v.at[at], active.at[at])
        copies.leave(grad_v.at[at], grad.at[at])
    copies.end()


def down_grad_body(info, *refs):
    mine, lefts_got, others, active_mine, others_got, mine_got = refs[:6]
    keep_a, send_a, keep_b, send_b = refs[6:10]
    left, right, keep_a_v, send_a_v, keep_b_v, send_b_v, semaphores = refs[10:]
    depth = mine.shape[1]
    rows = mine.shape[0] // 2
    half = rows // 2
    wide = right.shape[-1] // 2
    base = lefts_got.shape[0] - 2 * rows
    copies = Copies(semaphores)
    ahead = []
    for part in range(2):
        for bit in range(2):
            place = slice((2 * part + bit) * half, (2 * part + bit + 1) * half)
            spot = (info[ROW_Y] ^ bit) * rows + part * half
            for source, start, tokens in ((mine, 0, slice(0, depth)), (lefts_got, base, slice(depth, 2 * depth))):
                own = source.at[pl.ds(pl.multiple_of(start + spot, 16), half)]
                ahead.append(copies.start(own, left.at[place, tokens]))
    blocks = [[], []]
    for chunk in range(2):
        same = (info[ROW_Z0] ^ (1 - chunk)) == info[CORE]
        for bit in range(2):
            at = info[ROW_Z1] ^ bit
            columns = slice(bit * wide, (bit + 1) * wide)
            for kind, (one, two) in enumerate(((active_mine, others), (others_got, mine_got))):
                target = right.at[chunk, kind * depth : (kind + 1) * depth, columns]
                one = one.at[at] if kind == 0 else one.at[0, at]
                two = two.at[0, at] if kind == 0 else two.at[at]
                copy = pltpu.make_async_copy(one, target, semaphores.at[copies.count])
                also = pltpu.make_async_copy(two, target, semaphores.at[copies.count])
                copies.count += 1
                pl.when(same)(copy.start)
                pl.when(jnp.logical_not(same))(also.start)
                blocks[chunk].append(copy)
    for copy in ahead:
        copy.wait()
    for chunk in range(2):
        for copy in blocks[chunk]:
            copy.wait()
        total = dot(left[...], right[chunk]).astype(jnp.bfloat16)
        for bit in range(2):
            columns = slice(bit * wide, (bit + 1) * wide)
            place = 2 * (1 - chunk) + bit
            keep_a_v[place] = total[:half, columns]
            send_a_v[place] = total[half : 2 * half, columns]
            for low in range(2):
                own = slice((2 + low) * half, (3 + low) * half)
                (keep_b_v if chunk else send_b_v)[2 * low + bit] = total[own, columns]
        for source, target in ((keep_a_v, keep_a), (send_a_v, send_a)):
            place = pl.ds(2 * (1 - chunk), 2)
            copies.leave(source.at[place], target.at[place])
        copies.leave(*((keep_b_v, keep_b) if chunk else (send_b_v, send_b)))
    copies.end()


def down_grad(info, mine, lefts_got, actives, after):
    depth, wide = actives[0].shape[-2:]
    half = mine.shape[0] // 4
    shape = (4, half, wide)
    ins = (mine, lefts_got, *actives)
    anywhere = pl.BlockSpec(memory_space=pl.ANY)
    return run(
        down_grad_body,
        info,
        (1,),
        [(value, anywhere) for value in ins],
        [(shape, jnp.bfloat16, anywhere)] * 4,
        [hold(4 * half, 2 * depth), hold(2, 2 * depth, 2 * wide)]
        + [hold(*shape)] * 4
        + [pltpu.SemaphoreType.DMA((24,))],
        after,
    )


def column_grad(info, own, got, rights, parts, groups, after):
    depth = own.shape[-1]
    rows = own.shape[0] // 28
    width = 8 * rows
    count = len(parts)

    def body(info, own, got, *rest):
        rights, rest = rest[: len(rights_in)], rest[len(rights_in) :]
        outs, rest = rest[: 2 * count], rest[2 * count :]
        holds, rest = rest[: 2 * count], rest[2 * count :]
        lefts, wides, semaphores = rest[: len(groups)], rest[len(groups) : -1], rest[-1]
        copies = Copies(semaphores)
        ahead = []
        for at, (spot, start, columns, _) in enumerate(groups):
            copies_of = []
            for block in range(8):
                bit_x, bit_0, bit_1 = 1 - block // 4, block // 2 % 2, block % 2
                owner = (
                    4 * (info[ROW_Z1] ^ bit_1) + 2 * (info[ROW_Z0] ^ bit_0) + (info[ROW_X] ^ bit_x)
                )
                place = pl.ds(pl.multiple_of(spot * width + owner * rows, 16), rows)
                there = slice(block * rows, (block + 1) * rows)
                for kind, source in enumerate((own, got)):
                    target = lefts[at].at[there, kind * depth : (kind + 1) * depth]
                    copies_of.append(copies.start(source.at[place], target))
            for bit in range(2):
                row = 0
                for ref in rights:
                    source = ref.at[ref.shape[0] - 1, info[ROW_Y] ^ bit, :, start : start + columns]
                    tokens = ref.shape[2]
                    target = wides[at].at[row : row + tokens, bit * columns : (bit + 1) * columns]
                    copies_of.append(copies.start(source, target))
                    row += tokens
            ahead.append(copies_of)
        for chunk in range(2):
            totals = []
            for at in range(len(groups)):
                if chunk == 0:
                    for copy in ahead[at]:
                        copy.wait()
                totals.append(dot(lefts[at][chunk * 4 * rows : (chunk + 1) * 4 * rows], wides[at][...]))
            for at, (order, start, columns) in enumerate(parts):
                keep, send = holds[2 * at], holds[2 * at + 1]
                for block in range(4):
                    for bit_y in range(2):
                        piece = gather(totals, block, bit_y, start, columns)
                        bit = {"x": 1 - chunk, "0": block // 2, "1": block % 2, "y": bit_y}
                        spot = tuple(bit[name] for name in order[1:])
                        target = send if bit[order[0]] else keep
                        target[4 * spot[0] + 2 * spot[1] + spot[2]] = piece.astype(jnp.bfloat16)
                if order[0] == "x":
                    copies.leave(*((keep, outs[2 * at]) if chunk else (send, outs[2 * at + 1])))
                elif chunk:
                    copies.leave(keep, outs[2 * at])
                    copies.leave(send, outs[2 * at + 1])
        copies.end()

    def gather(totals, block, bit_y, start, columns):
        own = slice(block * rows, (block + 1) * rows)
        pieces = []
        for at, (_, first, wide, middle) in enumerate(groups):
            after_this = groups[at + 1] if at + 1 < len(groups) else None
            low = max(start, middle // LANES * LANES if at else 0)
            high = min(start + columns, after_this[3] // LANES * LANES if after_this else first + wide)
            base = bit_y * wide - first
            if at and middle % LANES and low == middle // LANES * LANES and low < high:
                before = groups[at - 1]
                lane = lax.broadcasted_iota(jnp.int32, (1, LANES), 1) + low
                old = totals[at - 1][own, bit_y * before[2] - before[1] + low :][:, :LANES]
                new = totals[at][own, base + low : base + low + LANES]
                pieces.append(jnp.where(lane < middle, old, new))
                low += LANES
            if low < high:
                pieces.append(totals[at][own, base + low : base + high])
        return pieces[0] if len(pieces) == 1 else jnp.concatenate(pieces, axis=1)

    rights_in = rights
    anywhere = pl.BlockSpec(memory_space=pl.ANY)
    shapes = [(8, rows, columns) for _, _, columns in parts for _ in range(2)]
    return run(
        body,
        info,
        (1,),
        [(value, anywhere) for value in (own, got, *rights)],
        [(shape, jnp.bfloat16, anywhere) for shape in shapes],
        [hold(*shape) for shape in shapes]
        + [hold(width, 2 * depth)] * len(groups)
        + [hold(2 * depth, 2 * columns) for _, _, columns, _ in groups]
        + [pltpu.SemaphoreType.DMA((64,))],
        after,
        time=8.0,
    )


def fold_body(info, kept_0, kept_1, got_0, got_1, keep, send):
    for kept, got, out in ((kept_0, got_0, keep), (kept_1, got_1, send)):
        out[...] = (kept[...].astype(jnp.float32) + got[...].astype(jnp.float32)).astype(out.dtype)


def fold(info, kept, got, after):
    count, rows, columns = kept.shape
    half = count // 2
    low = pl.BlockSpec((half // 2, rows, columns), lambda step, bits: (step, 0, 0))
    high = pl.BlockSpec((half // 2, rows, columns), lambda step, bits: (step + 2, 0, 0))
    return run(
        fold_body,
        info,
        (2,),
        [(kept, low), (kept, high), (got, low), (got, high)],
        [((half, rows, columns), kept.dtype, low)] * 2,
        (),
        after,
        time=3.0,
    )


def fold_wide_body(info, *refs):
    count = len(refs) // 6
    for at in range(count):
        fold_body(info, *refs[4 * at : 4 * at + 4], *refs[4 * count + 2 * at : 4 * count + 2 * at + 2])


def fold_wide(info, pairs, after):
    ins, outs = [], []
    for kept, got in pairs:
        count, rows, columns = kept.shape
        half = count // 2
        low = pl.BlockSpec((half // 2, rows, columns), lambda step, bits: (step, 0, 0))
        high = pl.BlockSpec((half // 2, rows, columns), lambda step, bits: (step + 2, 0, 0))
        ins += [(value, spec) for value in (kept, got) for spec in (low, high)]
        outs += [((half, rows, columns), kept.dtype, low)] * 2
    results = run(fold_wide_body, info, (2,), ins, outs, (), after)
    return list(zip(results[::2], results[1::2]))


def fold_all_body(info, *refs, join):
    ins = len(refs) - 2 if join is not None else len(refs) // 2
    outs = refs[ins:]
    place = 0
    for at in range(ins // 2):
        kept, got = refs[2 * at], refs[2 * at + 1]
        keep, send = outs if join is not None else outs[2 * at : 2 * at + 2]
        own = [slice(None)] * 3
        if join is not None:
            own[join] = slice(place, place + kept.shape[join])
            place += kept.shape[join]
        half = kept.shape[0] // 2
        if half:
            for out, rows in ((keep, slice(0, half)), (send, slice(half, 2 * half))):
                total = kept[rows].astype(jnp.float32) + got[rows].astype(jnp.float32)
                out[tuple(own)] = total.astype(out.dtype)
            continue
        total = (kept[0].astype(jnp.float32) + got[0].astype(jnp.float32)).astype(keep.dtype)
        half = total.shape[-1] // 2
        for side in range(2):

            @pl.when(info[ROW_X] == side)
            def _():
                keep[0] = total[:, side * half : (side + 1) * half]
                send[0] = total[:, (1 - side) * half : (2 - side) * half]


def fold_all(info, pairs, after, join=None, place=resident, time=5.0):
    shapes = []
    for kept, _ in pairs:
        count, rows, columns = kept.shape
        shapes.append((count // 2, rows, columns) if count > 1 else (1, rows, columns // 2))
    if join is not None:
        shape = list(shapes[0])
        shape[join] = sum(one[join] for one in shapes)
        shapes = [tuple(shape)]
    outs = [(shape, pairs[0][0].dtype, place(shape)) for shape in shapes for _ in range(2)]
    ins = [(value, place(value.shape)) for pair in pairs for value in pair]
    body = functools.partial(fold_all_body, join=join)
    vmem = 24 if place is resident else 63
    results = run(body, info, (1,), ins, outs, (), after, time=time, vmem=vmem)
    return list(zip(results[::2], results[1::2]))


def last_body(info, *refs):
    up, qkv, out = refs[-3:]

    def total(kept, got):
        return kept[0].astype(jnp.float32) + got[0].astype(jnp.float32)

    up[...] = total(*refs[:2])
    both = total(*refs[2:4])
    edge = qkv.shape[1]
    qkv[...] = both[:, :edge]
    out[...] = both[:, edge:]


def down_last_body(info, kept, got, out):
    out[...] = kept[0].astype(jnp.float32) + got[0].astype(jnp.float32)


def back_body(info, *refs):
    others, grad_mine, weight_up, tokens, cot, proj, weight_out, packed, mods, logs = refs[:10]
    resid, grad_packed, shared_0, shared_1, send_0, send_1 = refs[10:16]
    sums, bias_out, bias_qkv = refs[16:19]
    grads, wu, x, g, proj_v, wo, packed_v, acc, resid_v, grad_v, att_v = refs[19:30]
    key_t, query_t, rest_v, result_v, mine_v, send_v, semaphores = refs[30:]
    slots, seq, width = x.shape
    block = wu.shape[-1]
    copies = Copies(semaphores)
    ahead = []
    for at in range(2):
        for kind, source in enumerate((others.at[1, at], grad_mine.at[at])):
            spot = 2 * at + (info[CORE] if kind else 1 - info[CORE])
            place = 2 * at + kind
            ahead.append(copies.start(source, grads.at[place]))
            ahead.append(copies.start(columns_at(weight_up, spot, block), wu.at[place]))
    late = [copies.start(tokens, x), copies.start(cot, g), copies.start(proj, proj_v)]
    got_o = copies.start(weight_out, wo)
    got_p = copies.start(packed, packed_v)
    for place in range(4):
        ahead[2 * place].wait()
        ahead[2 * place + 1].wait()
        part = dot(grads[place], wu[place], 1, 1)
        if place == 0:
            acc[...] = part
        else:
            acc[...] += part
    for copy in late:
        copy.wait()
    bias = jnp.zeros((1, width), jnp.float32)
    for slot in range(slots):
        rows = slice(slot * seq, (slot + 1) * seq)
        grad = acc[rows]
        projected = proj_v[rows]
        normed, factor = layer_norm(x[slot].astype(jnp.float32) + mods[slot, 2:3] * projected)
        live = info[LIVE + slot].astype(jnp.float32)
        sums[slot, 0:1] = jnp.sum(grad, axis=0, keepdims=True)
        sums[slot, 1:2] = jnp.sum(grad * normed, axis=0, keepdims=True)
        back = g[slot].astype(jnp.float32) * live + norm_back(
            grad * (1.0 + mods[slot, 4:5]), normed, factor
        )
        resid_v[rows] = back
        sums[slot, 2:3] = jnp.sum(back * projected, axis=0, keepdims=True)
        result = (back * mods[slot, 2:3]).astype(jnp.bfloat16)
        grad_v[rows] = result
        bias += jnp.sum(result.astype(jnp.float32), axis=0, keepdims=True)
    bias_out[...] = bias
    copies.leave(resid_v, resid)

    got_o.wait()
    att_v[...] = dot(grad_v[...], wo[...], 1, 1).astype(jnp.bfloat16)
    got_p.wait()
    total = jnp.zeros((1, 3 * width), jnp.float32)
    for slot in range(slots):
        rows = slice(slot * seq, (slot + 1) * seq)
        key_t[...] = packed_v[rows, width : 2 * width].T.astype(jnp.float32)
        rest_v[...] = jnp.zeros_like(rest_v)
        for first in range(0, HEADS, GROUP):
            heads = range(first, first + GROUP)
            queries, grads_att, probs, grad_probs = [], [], [], []
            for head in heads:
                start, stop, inside = head_window(head)
                queries.append(jnp.where(inside, packed_v[rows, start:stop], 0))
                grads_att.append(jnp.where(inside, att_v[rows, start:stop], 0))
                key = packed_v[rows, width + start : width + stop]
                value = packed_v[rows, 2 * width + start : 2 * width + stop]
                probs.append(dot(key, queries[-1], 1, 1))
                grad_probs.append(dot(value, grads_att[-1], 1, 1))
            probs = [
                jnp.exp2(score * POWER - logs[slot, head : head + 1])
                for head, score in zip(heads, probs)
            ]
            inner = [
                jnp.sum(prob * grad, axis=0, keepdims=True) for prob, grad in zip(probs, grad_probs)
            ]
            grad_scores = [
                (prob * (grad - mean)).astype(jnp.bfloat16)
                for prob, grad, mean in zip(probs, grad_probs, inner)
            ]
            for at, head in enumerate(heads):
                start, stop, _ = head_window(head)
                own = slice(head * HEAD, (head + 1) * HEAD)
                query_t[own] = dot(key_t[own].astype(jnp.bfloat16), grad_scores[at]) * SCALE
                rest_v[:, start:stop] += dot(grad_scores[at], queries[at]) * SCALE
                rest_v[:, width + start : width + stop] += dot(
                    probs[at].astype(jnp.bfloat16), grads_att[at]
                )
        parts = [query_t[...].T, rest_v[...]]
        result = jnp.concatenate(parts, axis=1)
        low = result.astype(jnp.bfloat16)
        result_v[rows] = low
        total += jnp.sum(low.astype(jnp.float32), axis=0, keepdims=True)
        block, out_block = 3 * width // 4, width // 4
        rounded = grad_v[rows].astype(jnp.float32)
        for at in range(4):
            piece = jnp.concatenate(
                [
                    result[:, at * block : (at + 1) * block],
                    rounded[:, at * out_block : (at + 1) * out_block],
                ],
                axis=1,
            ).astype(jnp.bfloat16)

            @pl.when(info[CORE] == at % 2)
            def _():
                mine_v[slot, at // 2] = piece

            @pl.when(info[CORE] != at % 2)
            def _():
                send_v[slot, at // 2] = piece

        copies.leave(send_v.at[slot], (send_0, send_1)[slot].at[0])
        copies.leave(mine_v.at[slot], (shared_0, shared_1)[slot].at[0])
        copies.leave(result_v.at[rows], grad_packed.at[rows])
    bias_qkv[...] = total
    copies.end()


def token_grad_body(info, *refs):
    grad_packed, weight_qkv, resid, tokens, mods, grad_tokens, sums = refs[:7]
    grads, wq, resid_v, x, acc, tokens_v, semaphores = refs[7:]
    slots, seq, width = x.shape
    copies = Copies(semaphores)
    ahead = []
    for at in range(3):
        third = slice(at * width, (at + 1) * width)
        ahead.append(copies.start(grad_packed.at[:, third], grads.at[at]))
        ahead.append(copies.start(weight_qkv.at[:, third], wq.at[at]))
    late = [copies.start(tokens, x), copies.start(resid, resid_v)]
    for at in range(3):
        ahead[2 * at].wait()
        ahead[2 * at + 1].wait()
        part = dot(grads[at], wq[at], 1, 1)
        if at == 0:
            acc[...] = part
        else:
            acc[...] += part
    for copy in late:
        copy.wait()
    for slot in range(slots):
        rows = slice(slot * seq, (slot + 1) * seq)
        back = acc[rows]
        normed, factor = layer_norm(x[slot].astype(jnp.float32))
        sums[slot, 0:1] = jnp.sum(back, axis=0, keepdims=True)
        sums[slot, 1:2] = jnp.sum(back * normed, axis=0, keepdims=True)
        result = resid_v[rows] + norm_back(back * (1.0 + mods[slot, 1:2]), normed, factor)
        tokens_v[slot] = result.astype(jnp.bfloat16)
        copies.leave(tokens_v.at[slot], grad_tokens.at[slot])
    copies.end()


def output_body(info, *refs):
    others, active_mine, weight_down, tokens, cot, proj, mods, bias, mixed, sums = refs[:10]
    active, wd, x, g, proj_v, acc, mixed_v, semaphores = refs[10:]
    slots, seq, width = x.shape
    block = wd.shape[1]
    copies = Copies(semaphores)
    ahead = []
    for at in range(2):
        for kind, source in enumerate((others.at[0, at], active_mine.at[at])):
            spot = 2 * at + (info[CORE] if kind else 1 - info[CORE])
            place = 2 * at + kind
            ahead.append(copies.start(source, active.at[place]))
            ahead.append(copies.start(rows_at(weight_down, spot, block), wd.at[place]))
    late = [copies.start(tokens, x), copies.start(cot, g), copies.start(proj, proj_v)]
    for place in range(4):
        ahead[2 * place].wait()
        ahead[2 * place + 1].wait()
        part = dot(active[place], wd[place])
        if place == 0:
            acc[...] = part
        else:
            acc[...] += part
    for copy in late:
        copy.wait()
    for slot in range(slots):
        rows = slice(slot * seq, (slot + 1) * seq)
        downward = acc[rows] + bias[...]
        live = info[LIVE + slot].astype(jnp.float32)
        residual = x[slot].astype(jnp.float32) + mods[slot, 2:3] * proj_v[rows]
        mixed_v[slot] = (live * (residual + mods[slot, 5:6] * downward)).astype(jnp.bfloat16)
        copies.leave(mixed_v.at[slot], mixed.at[slot])
        sums[slot] = jnp.sum(g[slot].astype(jnp.float32) * live * downward, axis=0, keepdims=True)
    copies.end()


def small_body(info, sums_a, sums_b, sums_gate, in_qkv, in_out, in_up_0, in_up_1, in_down, *rest):
    keep, send = rest
    width = in_out.shape[-1]
    part = width // 8
    grads = jnp.concatenate(
        [
            jnp.concatenate(
                [
                    sums_a[slot, 0:1],
                    sums_a[slot, 1:2],
                    sums_b[slot, 2:3],
                    sums_b[slot, 0:1],
                    sums_b[slot, 1:2],
                    sums_gate[slot],
                ],
                axis=1,
            )
            for slot in range(sums_a.shape[0])
        ],
        axis=0,
    )
    query, value = in_qkv[:, :width], in_qkv[:, 2 * width :]
    even = info[CORE] == 0
    ups = []
    for at in range(2):
        ups.append(jnp.where(even, in_up_0[at], in_up_1[at]))
        ups.append(jnp.where(even, in_up_1[at], in_up_0[at]))
    up = jnp.concatenate(ups, axis=1)
    wide = up.shape[1] // 8
    columns = grads.shape[1] // 4
    row = lax.broadcasted_iota(jnp.int32, (8, 1), 0)
    biases = []
    for at in range(8):
        own = slice(at * part, (at + 1) * part)
        biases.append(
            jnp.concatenate(
                [
                    query[:, own],
                    value[:, own],
                    in_out[:, own],
                    up[:, at * wide : (at + 1) * wide],
                    in_down[:, own],
                    jnp.zeros((1, columns - 4 * part - wide), jnp.float32),
                ],
                axis=1,
            )
        )
    biases = jnp.concatenate(biases, axis=0)
    for at in range(4):
        total = jnp.zeros((8, columns), jnp.float32)
        for slot in range(grads.shape[0]):
            piece = grads[slot : slot + 1, at * columns : (at + 1) * columns]
            total += jnp.where(row == info[SAMPLE + slot], piece, 0.0)
        total = total.astype(jnp.bfloat16).astype(jnp.float32)
        place = info[ROW_Y] ^ (at // 2)

        @pl.when(info[CORE] == at % 2)
        def _():
            keep[place, :8] = total
            keep[place, 8:] = biases

        @pl.when(info[CORE] != at % 2)
        def _():
            send[place, :8] = total
            send[place, 8:] = biases


def rows_body(info, own, got, weight_t, lifted, part, cond, send, bias, lift, buffer):
    total = own[...] + got[...]
    rows = total[:8].astype(jnp.bfloat16)
    part[...] = rows.astype(jnp.float32)
    cond[...] = dot(rows, weight_t[...])
    columns = part.shape[1]
    edge = -(-columns // LANES) * LANES
    size = lift.shape[1] // 4
    buffer[...] = jnp.zeros_like(buffer)
    buffer[:6, :columns] = part[:6]
    for at in range(2):

        @pl.when(info[ROW_X] == at)
        def _():
            for high in range(4):
                bias[high : high + 1] = total[8 + 2 * high + at : 9 + 2 * high + at]
                row = total[9 + 2 * high - at : 10 + 2 * high - at]
                top = row.astype(jnp.bfloat16).astype(jnp.float32)
                buffer[6 + high : 7 + high, :columns] = top
                buffer[10 + high : 11 + high, :columns] = row - top
                mine, theirs = (2 * high + at) * size, (2 * high + 1 - at) * size
                place = slice(high * size, (high + 1) * size)
                lift[:, place] = lifted[:, mine : mine + size]
                buffer[:8, edge + high * size : edge + (high + 1) * size] = lifted[:, theirs : theirs + size]

    send[...] = buffer[...].astype(send.dtype)


def spread_body(info, part, got, bias, lift, cond, cond_got, both, own_bias, own_lift, cond_sum, *rest):
    sends, total, lifts, buffer = rest[:3], rest[3], rest[4], rest[5]
    cond_sum[...] = cond[...] + cond_got[...]
    columns = part.shape[1]
    edge = -(-columns // LANES) * LANES
    size = lift.shape[1] // 4
    arrived = got[...].astype(jnp.float32)
    total[:4] = bias[...] + arrived[6:10, :columns] + arrived[10:14, :columns]
    lifts[...] = jnp.zeros_like(lifts)
    for high in range(4):
        place = slice(high * size, (high + 1) * size)
        lifts[high, :6] = lift[:6, place]
        lifts[high, 6:12] = arrived[:6, edge + high * size : edge + (high + 1) * size]
    both[...] = jnp.zeros_like(both)
    both[:6] = part[:6]
    both[6:12] = arrived[:6, :columns]
    high = 2 * info[ROW_Z1] + info[ROW_Z0]
    own_bias[...] = total[pl.ds(high, 1)]
    own_lift[...] = lifts[high]
    for far in range(1, 4):
        row = total[pl.ds(high ^ far, 1)]
        top = row.astype(jnp.bfloat16).astype(jnp.float32)
        buffer[...] = jnp.zeros_like(buffer)
        buffer[:12, :columns] = both[:12]
        buffer[12:13, :columns] = top
        buffer[13:14, :columns] = row - top
        buffer[:, edge : edge + size] = lifts[high ^ far]
        sends[far - 1][...] = buffer[...].astype(jnp.bfloat16)


def ada_body(info, both, own_lift, own_bias, got_1, got_2, got_3, weight, bias, sums, rows, lifts):
    columns = both.shape[1]
    size = own_lift.shape[1]
    edge = -(-columns // LANES) * LANES
    row = lax.broadcasted_iota(jnp.int32, (16, 1), 0)
    rows[:16] = both[...].astype(jnp.bfloat16)
    lifts[:16] = own_lift[...].astype(jnp.bfloat16)
    total = own_bias[...]
    for at, got in enumerate((got_1, got_2, got_3)):
        place = pl.ds(16 * (at + 1), 16)
        arrived = got[...].astype(jnp.float32)
        rows[place] = jnp.where(row < 12, arrived[:, :columns], 0.0).astype(jnp.bfloat16)
        lifts[place] = jnp.where(row < 12, arrived[:, edge : edge + size], 0.0).astype(jnp.bfloat16)
        total += arrived[12:13, :columns] + arrived[13:14, :columns]
    sums[...] = total
    weight[...] = dot(lifts[...], rows[...], 0, 0)
    bias[...] = jnp.sum(rows[...].astype(jnp.float32), axis=0, keepdims=True)


def quick_shards(
    tokens,
    condition,
    counts,
    sample_order,
    weight_qkv,
    bias_query,
    bias_value,
    weight_out,
    bias_out,
    weight_up,
    bias_up,
    weight_down,
    bias_down,
    weight_ada,
    bias_ada,
    cotangent,
):
    slots, seq, width = tokens.shape
    count = slots * seq
    ff_width = weight_up.shape[1]
    mod_count, dp_count = lax.axis_size("mod"), lax.axis_size("dp")
    mod_index, dp_index = lax.axis_index("mod"), lax.axis_index("dp")
    f32, bf16 = jnp.float32, jnp.bfloat16
    steps = {"c": ("mod", 1), "y": ("mod", 2), "x": ("dp", 1), "0": ("dp", 2), "1": ("dp", 4)}

    def trade(value, name):
        return swap(value, *steps[name])

    row_total = sample_order.shape[1]
    columns = 6 * width // mod_count
    smem = pl.BlockSpec(memory_space=pltpu.SMEM)
    weight_ada_t = weight_ada.T
    start_ins = [condition, weight_ada_t, bias_ada.astype(f32)[None]]
    start_shapes = [(8, columns), (8, width)]
    info, part_mods, lifted = pl.pallas_call(
        start_body,
        grid_spec=pltpu.PrefetchScalarGridSpec(
            num_scalar_prefetch=2,
            grid=(1,),
            in_specs=[whole(value.shape) for value in start_ins],
            out_specs=[smem] + [whole(shape) for shape in start_shapes],
        ),
        out_shape=[jax.ShapeDtypeStruct((9,), jnp.int32)]
        + [jax.ShapeDtypeStruct(shape, f32) for shape in start_shapes],
        compiler_params=pltpu.CompilerParams(vmem_limit_bytes=63 * 1024 * 1024),
        cost_estimate=cost(3.0),
    )(counts, sample_order, *start_ins)
    parts_got = [swap(part_mods, "mod", far) for far in range(1, mod_count)]
    stats_ins = (tokens, bias_query, bias_value, bias_out, bias_up, bias_down)
    stats_shapes = [(slots, seq, LANES), (1, 3 * width), (1, width), (4, width), (1, width)]
    stats, bias_qkv, bias_out, bias_up, bias_down = run(
        stats_body,
        info,
        (1,),
        [(value, whole(value.shape)) for value in stats_ins],
        [(shape, f32, whole(shape)) for shape in stats_shapes],
        (),
        (part_mods,),
    )

    mods_shape = (slots, 6, width)
    flat = (count, width)
    turned = (width, count)
    row = (1, width)
    left_rows = 7 * width // 2
    block = ff_width // 4
    pair = (2, count, block)
    anywhere = pl.BlockSpec(memory_space=pl.ANY)

    def far_off(*values):
        return [(value, anywhere) for value in values]

    def near(*values):
        return [(value, whole(value.shape)) for value in values]

    def far_outs(*shapes):
        return [(shape, dtype, anywhere) for shape, dtype in shapes]

    def near_outs(*shapes):
        return [(shape, f32, whole(shape)) for shape in shapes]

    lefts, packed, proj, entry_b, grad_down, down_mine, others, mods, logs, bias_down_sum, bias_up_1 = run(
        forward_body,
        info,
        (1,),
        far_off(tokens, cotangent, weight_qkv, weight_out, weight_up, weight_down)
        + near(part_mods, *parts_got, stats, bias_qkv, bias_out, bias_up),
        far_outs(
            ((left_rows, count), bf16),
            ((count, 3 * width), bf16),
            (flat, f32),
            (flat, bf16),
            (flat, bf16),
            ((width // 2, count), bf16),
            ((2, *pair), bf16),
        )
        + near_outs(mods_shape, (slots, HEADS, seq), row, (2, 1, block)),
        [
            hold(slots, seq, width),
            hold(slots, seq, width),
            hold(3, width, width),
            hold(width, width),
            hold(2, width, block),
            hold(2, block, width),
            hold(count, 3 * width),
            hold(left_rows, count),
            pltpu.VMEM(flat, f32),
            hold(*flat),
            hold(*flat),
            hold(width // 2, count),
            hold(2, *pair),
            pltpu.VMEM((width, seq), f32),
            pltpu.VMEM((width, seq), f32),
            pltpu.SemaphoreType.DMA((24,)),
        ],
        time=30.0,
    )
    lefts_got = trade(lefts, "c")
    others_got = trade(others, "c")
    active_mine, grad_up_mine, bias_up_0 = run(
        feed_mine_body,
        info,
        (1,),
        far_off(entry_b, grad_down, weight_up, weight_down) + near(bias_up),
        far_outs((pair, bf16), (pair, bf16)) + near_outs((2, 1, block)),
        [
            hold(*flat),
            hold(*flat),
            hold(2, width, block),
            hold(2, block, width),
            hold(*pair),
            hold(*pair),
            pltpu.SemaphoreType.DMA((12,)),
        ],
        time=9.0,
    )
    active_mine_got = trade(active_mine, "c")

    class Part:
        def __init__(self, kept, send, order):
            self.kept, self.order = kept, order
            self.got = trade(send, order[0])

        def fold(self, after):
            kept, send = fold(info, self.kept, self.got, after)
            return self.go_on(kept, send)

        def go_on(self, kept, send):
            self.kept, self.order = kept, self.order[1:]
            self.got = trade(send, self.order[0])
            return kept

    def join_parts(parts, after, join, place=resident, time=5.0):
        pairs = [(part.kept, part.got) for part in parts]
        ((kept, send),) = fold_all(info, pairs, after, join, place, time)
        return Part(kept, send, parts[0].order[1:]), kept

    def fold_parts(parts, after, step=fold_all):
        folded = step(info, [(part.kept, part.got) for part in parts], after)
        for part, (kept, send) in zip(parts, folded):
            part.go_on(kept, send)
        return folded[-1][0]

    keep, send = column_grad(
        info,
        lefts,
        lefts_got,
        (grad_up_mine.reshape(1, *pair), others_got),
        [("xy10", 0, block)],
        [(2, 0, block, 0)],
        (active_mine,),
    )
    up = Part(keep, send, "xy10")
    token = keep
    keep_a, send_a, keep_b, send_b = down_grad(
        info,
        down_mine,
        lefts_got,
        (others, active_mine, others_got, active_mine_got),
        (token,),
    )
    down_a, down_b = Part(keep_a, send_a, "y01x"), Part(keep_b, send_b, "0y1x")
    token = keep_a

    shared = (1, 2, seq, width)
    packed_shape = (count, 3 * width)
    resid, grad_packed, mine_0, mine_1, send_0, send_1, sums_b, bias_out_sum, bias_qkv_sum = run(
        back_body,
        info,
        (1,),
        far_off(others, grad_up_mine, weight_up, tokens, cotangent, proj, weight_out, packed)
        + near(mods, logs),
        far_outs((flat, f32), (packed_shape, bf16), *[(shared, bf16)] * 4)
        + near_outs((slots, 3, width), row, (1, 3 * width)),
        [
            hold(4, count, block),
            hold(4, width, block),
            hold(slots, seq, width),
            hold(slots, seq, width),
            pltpu.VMEM(flat, f32),
            hold(width, width),
            hold(*packed_shape),
            pltpu.VMEM(flat, f32),
            pltpu.VMEM(flat, f32),
            hold(*flat),
            hold(*flat),
            pltpu.VMEM((width, seq), f32),
            pltpu.VMEM((width, seq), f32),
            pltpu.VMEM((seq, 2 * width), f32),
            hold(*packed_shape),
            hold(slots, *shared[1:]),
            hold(slots, *shared[1:]),
            pltpu.SemaphoreType.DMA((24,)),
        ],
        (token,),
        time=30.0,
    )
    shared_mine = [mine_0, mine_1]
    shared_got = [trade(send_0, "c"), trade(send_1, "c")]
    token = grad_packed
    token = fold_parts((down_a, down_b), (token,), fold_wide)
    seam = 3 * width // 4
    cuts = [0, 4 * LANES, 6 * LANES, width]
    orders = ["xy01", "yx01", "0xy1"]
    halves = column_grad(
        info,
        lefts,
        lefts_got,
        shared_mine + shared_got,
        [(order, low, high - low) for order, low, high in zip(orders, cuts[:-1], cuts[1:])],
        [(0, 0, 7 * LANES, 0), (1, 6 * LANES, width - 6 * LANES, seam)],
        (token,),
    )
    qkv_a, qkv_b, qkv_c = (
        Part(keep, send, order) for keep, send, order in zip(halves[::2], halves[1::2], orders)
    )
    token = up.fold((halves[0],))
    down, token = join_parts((down_a, down_b), (token,), 1, whole)

    grad_tokens, sums_a = run(
        token_grad_body,
        info,
        (1,),
        far_off(grad_packed, weight_qkv, resid, tokens) + near(mods),
        far_outs((tokens.shape, bf16)) + near_outs((slots, 2, width)),
        [
            hold(3, *flat),
            hold(3, width, width),
            pltpu.VMEM(flat, f32),
            hold(slots, seq, width),
            pltpu.VMEM(flat, f32),
            hold(slots, seq, width),
            pltpu.SemaphoreType.DMA((12,)),
        ],
        (token,),
        time=16000.0,
    )
    token = fold_parts((qkv_c,), (sums_a,), fold_wide)
    token = fold_parts((qkv_a, qkv_b), (token,), fold_wide)
    token = fold_parts((up,), (token,), fold_wide)
    mixed_out, sums_gate = run(
        output_body,
        info,
        (1,),
        far_off(others, active_mine, weight_down, tokens, cotangent, proj) + near(mods, bias_down),
        far_outs((tokens.shape, bf16)) + near_outs((slots, 1, width)),
        [
            hold(4, count, block),
            hold(4, block, width),
            hold(slots, seq, width),
            hold(slots, seq, width),
            pltpu.VMEM(flat, f32),
            pltpu.VMEM(flat, f32),
            hold(slots, seq, width),
            pltpu.SemaphoreType.DMA((16,)),
        ],
        (token,),
        time=20.0,
    )
    token = sums_gate
    small_ins = [
        sums_a,
        sums_b,
        sums_gate,
        bias_qkv_sum,
        bias_out_sum,
        bias_up_0,
        bias_up_1,
        bias_down_sum,
    ]
    small_shape = (2, 16, columns)
    small_keep, small_send = run(
        small_body,
        info,
        (1,),
        [(value, resident(value.shape)) for value in small_ins],
        [(small_shape, f32, resident(small_shape))] * 2,
        (),
        (token,),
        vmem=16,
    )
    small = Part(small_keep, small_send, "cy")
    qkv, token = join_parts((qkv_a, qkv_b), (small_keep,), 2)
    token = fold_parts((small,), (token,))
    token = fold_parts((qkv_c,), (token,))
    token = fold_parts((down,), (token,))
    lift_shape = (8, width // 2)
    edge = -(-columns // LANES) * LANES
    over_x, over_z = (16, edge + width // 2), (16, edge + 2 * LANES)
    rows_outs = [
        ((8, columns), f32),
        ((8, width), f32),
        (over_x, bf16),
        ((4, columns), f32),
        (lift_shape, f32),
    ]
    part_rows, cond_part, send_x, keep_bias, keep_lift = run(
        rows_body,
        info,
        (1,),
        [
            (value, resident(value.shape))
            for value in (small.kept[0], small.got[0], weight_ada_t, lifted)
        ],
        [(shape, dtype, resident(shape)) for shape, dtype in rows_outs],
        [pltpu.VMEM(over_x, f32)],
        (token,),
        vmem=24,
    )
    token = part_rows
    got_x = trade(send_x, "x")
    cond_sum = cond_part + trade(cond_part, "c")
    end_shape = (width // mod_count, ff_width // dp_count)
    (grad_down_out,) = run(
        down_last_body,
        info,
        (1,),
        [(value, resident(value.shape)) for value in (down.kept, down.got)],
        [(end_shape, f32, resident(end_shape))],
        (),
        (token,),
        vmem=24,
    )
    token = grad_down_out
    cond_got = trade(cond_sum, "y")
    spread_outs = [((16, columns), f32), ((1, columns), f32), ((16, width // 8), f32), ((8, width), f32)]
    spread_outs += [(over_z, bf16)] * 3
    both, bias_sum, own_lift, cond_sum, *sends = run(
        spread_body,
        info,
        (1,),
        [
            (value, resident(value.shape))
            for value in (part_rows, got_x, keep_bias, keep_lift, cond_sum, cond_got)
        ],
        [(shape, dtype, resident(shape)) for shape, dtype in spread_outs],
        [
            pltpu.VMEM((8, columns), f32),
            pltpu.VMEM((4, 16, width // 8), f32),
            pltpu.VMEM(over_z, f32),
        ],
        (token,),
        vmem=24,
    )
    token = both
    got_z = [swap(sends[far - 1], "dp", 2 * far) for far in range(1, 4)]
    token = fold_parts((up,), (token,))
    qkv, token = join_parts((qkv, qkv_c), (token,), 2)

    ends = [value for part in (up, qkv) for value in (part.kept, part.got)]
    end_rows = width // dp_count
    end_shapes = [
        (end_rows, ff_width // mod_count),
        (end_rows, 3 * width // mod_count),
        (end_rows, width // mod_count),
    ]
    grad_up_out, grad_qkv_out, grad_out_out = run(
        last_body,
        info,
        (1,),
        [(value, resident(value.shape)) for value in ends],
        [(shape, f32, resident(shape)) for shape in end_shapes],
        (),
        (token,),
        vmem=24,
    )
    token = grad_up_out

    cond_sum = cond_sum[:row_total]
    _, silu_back = jax.vjp(jax.nn.silu, condition)
    grad_condition = silu_back(cond_sum)[0]
    ada_outs = [(width // dp_count, columns), (1, columns), (1, columns)]
    grad_weight_ada, grad_bias_ada, bias_sum = run(
        ada_body,
        info,
        (1,),
        [(value, resident(value.shape)) for value in (both, own_lift, bias_sum, *got_z)],
        [(shape, f32, resident(shape)) for shape in ada_outs],
        [pltpu.VMEM((64, columns), bf16), pltpu.VMEM((64, width // 8), bf16)],
        (token,),
        vmem=24,
    )
    grad_bias_ada, bias_sum = grad_bias_ada[0], bias_sum[0]
    bias_done = []
    for size in (width, width, width, ff_width, width):
        bias_done.append(bias_sum[: size // dp_count])
        bias_sum = bias_sum[size // dp_count :]

    grad_down_out = grad_down_out.T
    return (
        mixed_out,
        grad_tokens,
        grad_condition,
        grad_qkv_out,
        bias_done[0],
        bias_done[1],
        grad_out_out,
        bias_done[2],
        grad_up_out,
        bias_done[3],
        grad_down_out,
        bias_done[4],
        grad_weight_ada,
        grad_bias_ada,
    )


def solution(mesh):
    in_specs = (
        P(("dp", "mod"), None, None),
        P("dp", None),
        P("dp", None),
        P("dp", None),
        P(),
        P(),
        P(),
        P(),
        P(),
        P(),
        P(),
        P(),
        P(),
        P(None, "mod"),
        P("mod"),
        P(("dp", "mod"), None, None),
    )
    out_specs = (
        P(("dp", "mod"), None, None),
        P(("dp", "mod"), None, None),
        P("dp", None),
        P("dp", "mod"),
        P("dp"),
        P("dp"),
        P("dp", "mod"),
        P("dp"),
        P("dp", "mod"),
        P("dp"),
        P("dp", "mod"),
        P("dp"),
        P("dp", "mod"),
        P("mod"),
    )
    quick = mesh.shape["mod"] == 4 and mesh.shape["dp"] == 8
    body = quick_shards if quick else shards
    return jax.shard_map(body, mesh=mesh, in_specs=in_specs, out_specs=out_specs, check_vma=False)
```
